32 devices in a mesh: gx: 4 (over y, x), gy: 8 (over z, core).
Axes of the slice: x: 2, y: 2, z: 4, core: 2. Of those that a mesh axis runs over, the one named last changes fastest.
Arguments:
- right_side: float32 [4, 64, 8192], P('gx', None, 'gy')
- weights: float32 [4, 8192], P('gx', 'gy'), may hold values from 0.25 to 1.75
- signs: int32 [4, 8192], P('gx', 'gy'), may hold values from 0 to 1
- face_map: int32 [4, 8192], P('gx', 'gy'), may hold values from 0 to 1023, as said below
- pattern: int32 [4, 8, 64], P('gx', None, 'gy'), may hold values 0 or 1
- factor: float32 [4, 1024, 8192], P('gx', None, 'gy')
Outputs:
- solution_field: float32 [4, 64, 8192], P('gx', None, 'gy')
- residual: float32 [4, 64, 8192], P('gx', None, 'gy')
The draws below stay inside these ranges and needn't reach their ends.
Inputs may be any that keep to these rules, and one draw needn't show every extreme that they name: `face_map`: each subdomain's block of 1024 entries is a permutation of 0 to 1023.
All inputs are finite; a program needn't handle non-finite values. No bound on the sum of `pattern` on one device may be relied on, other than what follows from the above.
Results may differ from the reference program's by a relative error of at most 0.0003.
Values sent between devices are 32-bit elements; how exact they have to be, the bound alone decides.
No kernel may reach another device: no remote copies, remote signals or barrier semaphores. Data moves between devices by JAX's collectives and lax.ppermute only.
A program may use at most 64 MiB of HBM per device.

```python
import jax
import jax.numpy as jnp
from jax import lax

L = 1024
CASES = 64
BLK = 128
ITERS = 4
NB = 8
FACE = 256
SUB_X = 4
SUB_Y = 8


def draw_right_side(key, part):
    rank = (jnp.arange(SUB_X)[:, None] * SUB_Y + jnp.arange(SUB_Y)[None, :]).astype(jnp.float32)
    device_ramp = 3.0 ** (rank / (SUB_X * SUB_Y - 1))
    base_draw = jax.random.normal(jax.random.fold_in(key, 1), (SUB_X, CASES, SUB_Y, L), jnp.float32)
    result = base_draw * device_ramp[:, None, :, None]
    return result.reshape(SUB_X, CASES, SUB_Y * L)


def draw_face_map(key, part):
    key_list = jax.random.split(jax.random.fold_in(key, 7), SUB_X * SUB_Y)
    perms = jax.vmap(lambda one_key: jax.random.permutation(one_key, L))(key_list)
    return perms.reshape(SUB_X, SUB_Y * L).astype(jnp.int32)


def draw_factor(key, part):
    spread = 0.5
    off_part = jax.random.normal(jax.random.fold_in(key, 3), (SUB_X, L, SUB_Y, L), jnp.float32) * (spread / L ** 0.5)
    diag_vals = 1.0 + jax.random.uniform(jax.random.fold_in(key, 4), (SUB_X, L, SUB_Y, 1), jnp.float32)
    identity = jnp.eye(L, dtype=jnp.float32)[None, :, None, :]
    return (off_part + identity * diag_vals).reshape(SUB_X, L, SUB_Y * L)


def place_ends(array, own_key, low, high):
    longest = array.shape.index(max(array.shape))
    spots = []
    for shift in (0, 1):
        where = [jax.random.randint(jax.random.fold_in(own_key, axis), (), 0, length) for axis, length in enumerate(array.shape)]
        where[longest] = (where[longest] + shift) % array.shape[longest]
        spots.append(tuple(where))
    return array.at[spots[0]].set(low).at[spots[1]].set(high)


def setup_inputs(seed: int = 0) -> dict:
    key_of = jax.random.split(jax.random.key(seed), 7)
    return {
        "right_side": draw_right_side(jax.random.fold_in(key_of[6], 71), 0),
        "weights": jnp.clip(1.0 + 0.15 * jax.random.normal(key_of[1], (SUB_X, SUB_Y * L), jnp.float32), 0.25, 1.75),
        "signs": place_ends(jax.random.randint(key_of[2], (SUB_X, SUB_Y * L), 0, 2), jax.random.fold_in(key_of[2], 1), 0, 1).astype(jnp.int32),
        "face_map": draw_face_map(jax.random.fold_in(key_of[6], 71), 0),
        "pattern": place_ends((jax.random.randint(key_of[4], (SUB_X, NB, SUB_Y * NB), 0, 2) < 1).astype(jnp.int32), jax.random.fold_in(key_of[4], 1), 0, 1),
        "factor": draw_factor(jax.random.fold_in(key_of[6], 71), 0),
    }


HIGH = lax.Precision.HIGHEST

def partner(field, face_order, inverse):
    face_vals = jnp.take_along_axis(field, jnp.broadcast_to(face_order, field.shape), axis=3)
    north_vals = face_vals[..., 0:FACE]
    south_vals = face_vals[..., FACE:2 * FACE]
    west_vals = face_vals[..., 2 * FACE:3 * FACE]
    east_vals = face_vals[..., 3 * FACE:]
    empty_row = jnp.zeros_like(north_vals[:1])
    from_north = jnp.concatenate([empty_row, south_vals[:-1]], axis=0)
    from_south = jnp.concatenate([north_vals[1:], empty_row], axis=0)
    empty_col = jnp.zeros_like(north_vals[:, :, :1])
    from_west = jnp.concatenate([empty_col, east_vals[:, :, :-1]], axis=2)
    from_east = jnp.concatenate([west_vals[:, :, 1:], empty_col], axis=2)
    stacked = jnp.concatenate([from_north, from_south, from_west, from_east], axis=3)
    return jnp.take_along_axis(stacked, jnp.broadcast_to(inverse, field.shape), axis=3)

def inner_prod(left, right):
    return jnp.einsum('xayl,xbyl->ab', left, right, precision=HIGH)

def reference(right_side, weights, signs, face_map, pattern, factor):
    loads = right_side.reshape(SUB_X, CASES, SUB_Y, L)
    weighting = weights.reshape(SUB_X, 1, SUB_Y, L)
    jump_sign = (2 * signs - 1).astype(jnp.float32).reshape(SUB_X, 1, SUB_Y, L)
    face_order = face_map.reshape(SUB_X, 1, SUB_Y, L).astype(jnp.int32)
    inverse = jnp.argsort(face_order, axis=-1).astype(jnp.int32)
    keep_blocks = jnp.maximum(pattern.reshape(SUB_X, NB, SUB_Y, NB), jnp.eye(NB, dtype=jnp.int32)[None, :, None, :])
    keep_full = jnp.repeat(jnp.repeat(keep_blocks.astype(jnp.float32), BLK, axis=1), BLK, axis=3)
    factor_masked = factor.reshape(SUB_X, L, SUB_Y, L) * keep_full

    def operate(field):
        lifted = field + 0.5 * jump_sign * partner(field, face_order, inverse)
        halfway = jnp.einsum('xcyi,xiyj->xcyj', lifted, factor_masked, precision=HIGH)
        local_out = jnp.einsum('xcyj,xiyj->xcyi', halfway, factor_masked, precision=HIGH)
        return local_out + 0.5 * partner(jump_sign * local_out, face_order, inverse)

    def apply_left(matrix, field):
        return jnp.einsum('ab,xayl->xbyl', matrix, field, precision=HIGH)
    solution = jnp.zeros_like(loads)
    resid = loads
    direction = weighting * resid
    for iteration in range(ITERS):
        images = operate(direction)
        gram_matrix = inner_prod(direction, images)
        lower_factor = jnp.linalg.cholesky(gram_matrix)
        step_size = jax.scipy.linalg.cho_solve((lower_factor, True), inner_prod(direction, resid))
        solution = solution + apply_left(step_size, direction)
        resid = resid - apply_left(step_size, images)
        if iteration + 1 < ITERS:
            precond = weighting * resid
            update = -jax.scipy.linalg.cho_solve((lower_factor, True), inner_prod(images, precond))
            direction = precond + apply_left(update, direction)
    return (solution.reshape(SUB_X, CASES, SUB_Y * L), resid.reshape(SUB_X, CASES, SUB_Y * L))
```

```python
import jax
import jax.numpy as jnp
from jax import lax
from jax.sharding import PartitionSpec as P

ITERS = 4


HIGH = lax.Precision.HIGHEST


def from_behind(value, axis, steps):
    count = lax.axis_size(axis)
    leading, last = (max(0, -steps), min(count, count - steps))
    return lax.ppermute(value, axis, [(source, source + steps) for source in range(leading, last)])


def inner_prod(left, right):
    return lax.dot_general(left, right, (((1,), (1,)), ((), ())), precision=HIGH)


def stages(value):
    devices = lax.axis_size("gx") * lax.axis_size("gy")
    return (("gx", "gy"),) if devices * value.size <= 2**20 else ("gy", "gx")


def gather_sum(value):
    for axes in stages(value):
        value = jnp.sum(lax.all_gather(value, axes), axis=0)
    return value


def butterfly_sum(value):
    for axis in ("gy", "gx"):
        count = lax.axis_size(axis)
        step = 1
        while step < count:
            pairs = [(source, source ^ step) for source in range(count)]
            value = value + lax.ppermute(value, axis, pairs)
            step *= 2
    return value


def exchange_sum(value):
    for axes in stages(value):
        copies = jnp.broadcast_to(value, (lax.axis_size(axes),) + value.shape)
        value = jnp.sum(lax.all_to_all(copies, axes, 0, 0), axis=0)
    return value


def direct_sum(value):
    for axis in ("gy", "gx"):
        count = lax.axis_size(axis)
        total = value
        for step in range(1, count):
            pairs = [(source, source ^ step) for source in range(count)]
            total = total + lax.ppermute(value, axis, pairs)
        value = total
    return value


def local(right_side, weights, signs, face_map, pattern, factor):
    loads = right_side[0]
    case_count, unknowns = loads.shape
    blocks = pattern.shape[1]
    block_size = unknowns // blocks
    face_len = unknowns // 4
    keep_blocks = jnp.maximum(pattern[0], jnp.eye(blocks, dtype=jnp.int32)).astype(jnp.float32)
    keep_full = jnp.repeat(jnp.repeat(keep_blocks, block_size, axis=0), block_size, axis=1)
    factor_masked = factor[0] * keep_full
    face_order = face_map[0]
    perm = (jnp.arange(unknowns, dtype=jnp.int32)[:, None] == face_order[None, :]).astype(
        jnp.float32
    )
    jump_sign = (2 * signs[0] - 1).astype(jnp.float32)[None, :]
    weighting = weights[0][None, :]

    def partner(field):
        face_vals = jnp.dot(field, perm, precision=HIGH)
        north_vals = face_vals[:, 0:face_len]
        south_vals = face_vals[:, face_len : 2 * face_len]
        west_vals = face_vals[:, 2 * face_len : 3 * face_len]
        east_vals = face_vals[:, 3 * face_len :]
        from_north = from_behind(south_vals, "gx", 1)
        from_south = from_behind(north_vals, "gx", -1)
        from_west = from_behind(east_vals, "gy", 1)
        from_east = from_behind(west_vals, "gy", -1)
        stacked = jnp.concatenate([from_north, from_south, from_west, from_east], axis=1)
        return lax.dot_general(stacked, perm, (((1,), (1,)), ((), ())), precision=HIGH)

    def apply_left(matrix, field):
        return jnp.dot(matrix.T, field, precision=HIGH)

    solution = jnp.zeros_like(loads)
    resid = loads
    direction = weighting * resid
    for iteration in range(ITERS):
        lifted = direction + 0.5 * jump_sign * partner(direction)
        halfway = jnp.dot(lifted, factor_masked, precision=HIGH)
        local_out = lax.dot_general(
            halfway, factor_masked, (((1,), (1,)), ((), ())), precision=HIGH
        )
        images = local_out + 0.5 * partner(jump_sign * local_out)
        summed = gather_sum(
            jnp.stack([inner_prod(direction, images), inner_prod(direction, resid)])
        )
        gram_matrix, along_resid = summed[0], summed[1]
        lower_factor = jnp.linalg.cholesky(gram_matrix)
        step_size = jax.scipy.linalg.cho_solve((lower_factor, True), along_resid)
        solution = solution + apply_left(step_size, direction)
        resid = resid - apply_left(step_size, images)
        if iteration + 1 < ITERS:
            precond = weighting * resid
            crossed = butterfly_sum(inner_prod(images, precond))
            update = -jax.scipy.linalg.cho_solve((lower_factor, True), crossed)
            direction = precond + apply_left(update, direction)
    return (solution[None], resid[None])


def solution(mesh):
    return jax.shard_map(
        local,
        mesh=mesh,
        in_specs=(
            P("gx", None, "gy"),
            P("gx", "gy"),
            P("gx", "gy"),
            P("gx", "gy"),
            P("gx", None, "gy"),
            P("gx", None, "gy"),
        ),
        out_specs=(P("gx", None, "gy"), P("gx", None, "gy")),
        check_vma=False,
    )
```

```python
import jax
import jax.numpy as jnp
from jax import lax
from jax.sharding import PartitionSpec as P

ITERS = 4


HIGH = lax.Precision.HIGHEST


def from_behind(value, axis, steps):
    count = lax.axis_size(axis)
    leading, last = (max(0, -steps), min(count, count - steps))
    return lax.ppermute(value, axis, [(source, source + steps) for source in range(leading, last)])


def inner_prod(left, right):
    return lax.dot_general(left, right, (((1,), (1,)), ((), ())), precision=HIGH)


def stages(value):
    devices = lax.axis_size("gx") * lax.axis_size("gy")
    return (("gx", "gy"),) if devices * value.size <= 2**20 else ("gy", "gx")


def gather_sum(value):
    for axes in stages(value):
        value = jnp.sum(lax.all_gather(value, axes), axis=0)
    return value


def butterfly_sum(value):
    for axis in ("gy", "gx"):
        count = lax.axis_size(axis)
        step = 1
        while step < count:
            pairs = [(source, source ^ step) for source in range(count)]
            value = value + lax.ppermute(value, axis, pairs)
            step *= 2
    return value


def exchange_sum(value):
    for axes in stages(value):
        copies = jnp.broadcast_to(value, (lax.axis_size(axes),) + value.shape)
        value = jnp.sum(lax.all_to_all(copies, axes, 0, 0), axis=0)
    return value


def direct_sum(value):
    for axis in ("gy", "gx"):
        count = lax.axis_size(axis)
        total = value
        for step in range(1, count):
            pairs = [(source, source ^ step) for source in range(count)]
            total = total + lax.ppermute(value, axis, pairs)
        value = total
    return value


def local(right_side, weights, signs, face_map, pattern, factor):
    loads = right_side[0]
    case_count, unknowns = loads.shape
    blocks = pattern.shape[1]
    block_size = unknowns // blocks
    face_len = unknowns // 4
    keep_blocks = jnp.maximum(pattern[0], jnp.eye(blocks, dtype=jnp.int32)).astype(jnp.float32)
    keep_full = jnp.repeat(jnp.repeat(keep_blocks, block_size, axis=0), block_size, axis=1)
    factor_masked = factor[0] * keep_full
    face_order = face_map[0]
    perm = (jnp.arange(unknowns, dtype=jnp.int32)[:, None] == face_order[None, :]).astype(
        jnp.float32
    )
    jump_sign = (2 * signs[0] - 1).astype(jnp.float32)[None, :]
    weighting = weights[0][None, :]

    def partner(field):
        face_vals = jnp.dot(field, perm, precision=HIGH)
        north_vals = face_vals[:, 0:face_len]
        south_vals = face_vals[:, face_len : 2 * face_len]
        west_vals = face_vals[:, 2 * face_len : 3 * face_len]
        east_vals = face_vals[:, 3 * face_len :]
        from_north = from_behind(south_vals, "gx", 1)
        from_south = from_behind(north_vals, "gx", -1)
        from_west = from_behind(east_vals, "gy", 1)
        from_east = from_behind(west_vals, "gy", -1)
        stacked = jnp.concatenate([from_north, from_south, from_west, from_east], axis=1)
        return lax.dot_general(stacked, perm, (((1,), (1,)), ((), ())), precision=HIGH)

    def apply_left(matrix, field):
        return jnp.dot(matrix.T, field, precision=HIGH)

    solution = jnp.zeros_like(loads)
    resid = loads
    direction = weighting * resid
    for iteration in range(ITERS):
        lifted = direction + 0.5 * jump_sign * partner(direction)
        halfway = jnp.dot(lifted, factor_masked, precision=HIGH)
        local_out = lax.dot_general(
            halfway, factor_masked, (((1,), (1,)), ((), ())), precision=HIGH
        )
        images = local_out + 0.5 * partner(jump_sign * local_out)
        summed = exchange_sum(
            jnp.stack([inner_prod(direction, images), inner_prod(direction, resid)])
        )
        gram_matrix, along_resid = summed[0], summed[1]
        lower_factor = jnp.linalg.cholesky(gram_matrix)
        step_size = jax.scipy.linalg.cho_solve((lower_factor, True), along_resid)
        solution = solution + apply_left(step_size, direction)
        resid = resid - apply_left(step_size, images)
        if iteration + 1 < ITERS:
            precond = weighting * resid
            crossed = direct_sum(inner_prod(images, precond))
            update = -jax.scipy.linalg.cho_solve((lower_factor, True), crossed)
            direction = precond + apply_left(update, direction)
    return (solution[None], resid[None])


def solution(mesh):
    return jax.shard_map(
        local,
        mesh=mesh,
        in_specs=(
            P("gx", None, "gy"),
            P("gx", "gy"),
            P("gx", "gy"),
            P("gx", "gy"),
            P("gx", None, "gy"),
            P("gx", None, "gy"),
        ),
        out_specs=(P("gx", None, "gy"), P("gx", None, "gy")),
        check_vma=False,
    )
```

```python
import jax
import jax.numpy as jnp
from jax import lax
from jax.sharding import PartitionSpec as P

HIGH = lax.Precision.HIGHEST


def rounded(value):
    return lax.reduce_precision(value, exponent_bits=8, mantissa_bits=7)


def halves(value):
    high = rounded(value)
    low = rounded(value - high)
    return high.astype(jnp.bfloat16), low.astype(jnp.bfloat16)


def thirds(value):
    high = rounded(value)
    rest = value - high
    middle = rounded(rest)
    low = rest - middle
    return jnp.concatenate([high, middle, low], axis=0).astype(jnp.bfloat16)


def bf16_dot(left, right, right_dim):
    return lax.dot_general(
        left, right, (((1,), (right_dim,)), ((), ())), preferred_element_type=jnp.float32
    )


def exact_pick(value, pick, dim):
    rows = value.shape[0]
    parts = bf16_dot(thirds(value), pick, dim)
    return parts[:rows] + (parts[rows : 2 * rows] + parts[2 * rows :])


def product(value, high, low, dim):
    rows = value.shape[0]
    value_high, value_low = halves(value)
    both = bf16_dot(jnp.concatenate([value_high, value_low], axis=0), high, dim)
    return both[:rows] + (both[rows:] + bf16_dot(value_high, low, dim))


def inner_prod(left, right):
    return lax.dot_general(left, right, (((1,), (1,)), ((), ())), precision=HIGH)


def apply_left(matrix, field):
    return lax.dot_general(matrix, field, (((0,), (0,)), ((), ())), precision=HIGH)


def pairing(count, parity):
    pairs = []
    for source in range(count):
        target = source + 1 if source % 2 == parity else source - 1
        pairs.append((source, target if 0 <= target < count else source))
    return pairs


def swap_along(axis, lower, upper):
    count = lax.axis_size(axis)
    index = lax.axis_index(axis)
    even = index % 2 == 0
    first = lax.ppermute(jnp.where(even, upper, lower), axis, pairing(count, 0))
    second = lax.ppermute(jnp.where(even, lower, upper), axis, pairing(count, 1))
    from_lower = jnp.where(even, second, first)
    from_upper = jnp.where(even, first, second)
    from_lower = jnp.where(index > 0, from_lower, 0.0)
    from_upper = jnp.where(index + 1 < count, from_upper, 0.0)
    return from_lower, from_upper


def swap_faces(field):
    face_len = field.shape[1] // 4
    north, south, west, east = (
        field[:, face * face_len : (face + 1) * face_len] for face in range(4)
    )
    from_west, from_east = swap_along("gy", west, east)
    from_north, from_south = swap_along("gx", north, south)
    return jnp.concatenate([from_north, from_south, from_west, from_east], axis=1)


def stage_masks():
    stages = []
    for axis in ("gy", "gx"):
        count = lax.axis_size(axis)
        step = 1
        if axis == "gy":
            stages.append((axis, (1,)))
            step = 2
        while step < count:
            if step * 2 < count:
                stages.append((axis, (step, 2 * step, 3 * step)))
            else:
                stages.append((axis, (step,)))
            step *= 4
    return stages


def combine(value, operation):
    for axis, masks in stage_masks():
        count = lax.axis_size(axis)
        others = [
            lax.ppermute(value, axis, [(source, source ^ mask) for source in range(count)])
            for mask in masks
        ]
        value = operation(value, others[0])
        if len(others) == 3:
            value = operation(value, operation(others[1], others[2]))
    return value


def spd_solve(matrix, right):
    return jax.scipy.linalg.cho_solve((jnp.linalg.cholesky(matrix), True), right)


def local(right_side, weights, signs, face_map, pattern, factor):
    case_count, unknowns = right_side.shape[1:]
    blocks = pattern.shape[1]
    block_size = unknowns // blocks
    keep_blocks = jnp.maximum(pattern[0], jnp.eye(blocks, dtype=jnp.int32)).astype(jnp.float32)
    keep_full = jnp.repeat(jnp.repeat(keep_blocks, block_size, axis=0), block_size, axis=1)
    factor_masked = factor[0] * keep_full
    pick = (jnp.arange(unknowns, dtype=jnp.int32)[:, None] == face_map[0][None, :]).astype(
        jnp.bfloat16
    )
    largest = combine(jnp.full((8, 128), jnp.max(jnp.abs(factor_masked))), jnp.maximum)
    inverse_largest = 1.0 / largest[:1, :1]
    scale = inverse_largest * inverse_largest

    sign_row = (2 * signs[0] - 1).astype(jnp.float32)[None, :]
    small = jnp.concatenate(
        [right_side[0], weights[0][None, :], sign_row, jnp.zeros((6, unknowns), jnp.float32)],
        axis=0,
    )
    small = exact_pick(small, pick, 0)
    ghosts = swap_faces(small)
    resid, ghost_resid = small[:case_count], ghosts[:case_count]
    weighting, ghost_weighting = (
        small[case_count : case_count + 1],
        ghosts[case_count : case_count + 1],
    )
    jump, ghost_jump = (
        small[case_count + 1 : case_count + 2],
        ghosts[case_count + 1 : case_count + 2],
    )
    half_jump = 0.5 * jump * jnp.abs(ghost_jump)

    factor_high, factor_low = halves(factor_masked)
    rows_of = lambda part: lax.dot_general(
        pick, part, (((0,), (0,)), ((), ())), preferred_element_type=jnp.float32
    ).astype(jnp.bfloat16)
    factor_high, factor_low = rows_of(factor_high), rows_of(factor_low)

    def halfway(field, ghost):
        return product(field + half_jump * ghost, factor_high, factor_low, 0)

    def lift(half):
        return product(half, factor_high, factor_low, 1)

    def images(out):
        signed_ghost = swap_faces(jump * out)
        return out + 0.5 * signed_ghost, ghost_jump * signed_ghost + half_jump * out

    def basis(resid, ghost_resid):
        first, ghost_first = weighting * resid, ghost_weighting * ghost_resid
        half_first = halfway(first, ghost_first)
        image_first, ghost_image_first = images(lift(half_first))
        second = scale * (weighting * image_first)
        ghost_second = scale * (ghost_weighting * ghost_image_first)
        half_second = halfway(second, ghost_second)
        return (
            (first, second),
            (half_first, half_second),
            (image_first, ghost_image_first),
        )

    def square(a00, a01, a11):
        return jnp.concatenate(
            [jnp.concatenate([a00, a01], axis=1), jnp.concatenate([a01.T, a11], axis=1)], axis=0
        )

    fields, halfs, (image0, ghost_image0) = basis(resid, ghost_resid)
    local_sums = jnp.concatenate(
        [
            jnp.concatenate([inner_prod(halfs[0], halfs[0]), inner_prod(halfs[0], halfs[1])], axis=1),
            jnp.concatenate([inner_prod(halfs[1], halfs[1]), inner_prod(fields[0], resid)], axis=1),
        ],
        axis=0,
    )
    sums = combine(local_sums, jnp.add)
    image1, ghost_image1 = images(lift(halfs[1]))
    c = case_count
    gram = square(sums[:c, :c], sums[:c, c:], sums[c:, :c])
    right = jnp.concatenate([sums[c:, c:], scale * sums[:c, :c]], axis=0)
    gram_factor = jnp.linalg.cholesky(gram)
    steps = jax.scipy.linalg.cho_solve((gram_factor, True), right)
    new_resid = resid - apply_left(steps[:c], image0) - apply_left(steps[c:], image1)
    ghost_resid = (
        ghost_resid - apply_left(steps[:c], ghost_image0) - apply_left(steps[c:], ghost_image1)
    )
    resid = new_resid

    new_fields, new_halfs, (new_image0, _) = basis(resid, ghost_resid)
    both_halfs = jnp.concatenate([halfs[1], new_halfs[0], new_halfs[1]], axis=0)
    cross = inner_prod(both_halfs, jnp.concatenate([new_halfs[0], new_halfs[1]], axis=0))
    local_sums = jnp.concatenate(
        [
            cross[:c],
            cross[c : 2 * c],
            jnp.concatenate([inner_prod(new_fields[0], resid), cross[2 * c :, c:]], axis=1),
        ],
        axis=0,
    )
    sums = combine(local_sums, jnp.add)
    new_image1, _ = images(lift(new_halfs[1]))
    along = jnp.concatenate(
        [
            jnp.concatenate([jnp.zeros((c, c), jnp.float32), sums[:c, :c]], axis=1),
            sums[:c],
        ],
        axis=0,
    )
    conjugating = -jax.scipy.linalg.cho_solve((gram_factor, True), along)
    new_gram = square(sums[c : 2 * c, :c], sums[c : 2 * c, c:], sums[2 * c :, c:])
    new_gram = new_gram + apply_left(along, conjugating)
    right = jnp.concatenate([sums[2 * c :, :c], scale * sums[c : 2 * c, :c]], axis=0)
    new_steps = spd_solve(new_gram, right)
    old_steps = jnp.dot(conjugating, new_steps, precision=HIGH)
    total_steps = steps + old_steps
    solution = (
        apply_left(total_steps[:c], fields[0])
        + apply_left(total_steps[c:], fields[1])
        + apply_left(new_steps[:c], new_fields[0])
        + apply_left(new_steps[c:], new_fields[1])
    )
    resid = (
        resid
        - apply_left(old_steps[:c], image0)
        - apply_left(old_steps[c:], image1)
        - apply_left(new_steps[:c], new_image0)
        - apply_left(new_steps[c:], new_image1)
    )
    outs = exact_pick(jnp.concatenate([solution, resid], axis=0), pick, 1)
    return (outs[None, :c], outs[None, c:])


def solution(mesh):
    return jax.shard_map(
        local,
        mesh=mesh,
        in_specs=(
            P("gx", None, "gy"),
            P("gx", "gy"),
            P("gx", "gy"),
            P("gx", "gy"),
            P("gx", None, "gy"),
            P("gx", None, "gy"),
        ),
        out_specs=(P("gx", None, "gy"), P("gx", None, "gy")),
        check_vma=False,
    )
```

```python
import functools

import jax
import jax.numpy as jnp
from jax import lax
from jax.experimental import pallas as pl
from jax.experimental.pallas import tpu as pltpu
from jax.sharding import PartitionSpec as P

HIGH = lax.Precision.HIGHEST
VMEM = pl.BlockSpec(memory_space=pltpu.VMEM)
SMEM = pl.BlockSpec(memory_space=pltpu.SMEM)
PAD = 8
PIVOT = 4
SUBLANES = 8
LANES = 128


def halves(value):
    high = value.astype(jnp.bfloat16)
    low = (value - high.astype(jnp.float32)).astype(jnp.bfloat16)
    return high, low


def thirds(value):
    high = value.astype(jnp.bfloat16)
    rest = value - high.astype(jnp.float32)
    middle = rest.astype(jnp.bfloat16)
    low = (rest - middle.astype(jnp.float32)).astype(jnp.bfloat16)
    return jnp.concatenate([high, middle, low], axis=0)


def bf16_dot(left, right, right_dim):
    return lax.dot_general(
        left, right, (((1,), (right_dim,)), ((), ())), preferred_element_type=jnp.float32
    )


def exact_pick(value, pick):
    rows = value.shape[0]
    parts = bf16_dot(thirds(value), pick, 0)
    return parts[:rows] + (parts[rows : 2 * rows] + parts[2 * rows :])


def product(value, high, low, dim):
    rows = value.shape[0]
    value_high, value_low = halves(value)
    both = bf16_dot(jnp.concatenate([value_high, value_low], axis=0), high[...], dim)
    return both[:rows] + (both[rows:] + bf16_dot(value_high, low[...], dim))


def inner_prod(left, right):
    return lax.dot_general(
        left, right, (((1,), (1,)), ((), ())), precision=HIGH, preferred_element_type=jnp.float32
    )


def times(left, right):
    return jnp.dot(left, right, precision=HIGH, preferred_element_type=jnp.float32)


def row_to_square(row, size):
    return jnp.broadcast_to(row, (LANES, size)).T


def pick_columns(face_row):
    size = face_row.shape[1]
    unknown = lax.broadcasted_iota(jnp.int32, (size, size), 0)
    return jnp.where(unknown == face_row, 1.0, 0.0).astype(jnp.bfloat16)


def pick_rows(face_row):
    size = face_row.shape[1]
    face = row_to_square(face_row, size)
    lane = lax.broadcasted_iota(jnp.int32, (size, LANES), 1)
    return jnp.concatenate(
        [
            jnp.where(face == lane + start, 1.0, 0.0).astype(jnp.bfloat16)
            for start in range(0, size, LANES)
        ],
        axis=1,
    )


def faces_of(field):
    face_len = field.shape[1] // 4
    return [field[:, face * face_len : (face + 1) * face_len] for face in range(4)]


def write_faces(place, field, outs):
    north, south, west, east = faces_of(field)
    even_x, even_y = place[0] % 2 == 0, place[1] % 2 == 0
    outs[0][...] = jnp.where(even_x, south, north)
    outs[1][...] = jnp.where(even_x, north, south)
    outs[2][...] = jnp.where(even_y, east, west)
    outs[3][...] = jnp.where(even_y, west, east)


def read_faces(place, received):
    x_first, x_second, y_first, y_second = [one[...] for one in received]
    even_x, even_y = place[0] % 2 == 0, place[1] % 2 == 0
    north = jnp.where(place[0] > 0, jnp.where(even_x, x_second, x_first), 0.0)
    south = jnp.where(place[0] + 1 < place[2], jnp.where(even_x, x_first, x_second), 0.0)
    west = jnp.where(place[1] > 0, jnp.where(even_y, y_second, y_first), 0.0)
    east = jnp.where(place[1] + 1 < place[3], jnp.where(even_y, y_first, y_second), 0.0)
    return jnp.concatenate([north, south, west, east], axis=1)


def rows_of(small, cases):
    return small[:cases], small[cases : cases + 1], small[cases + 1 : cases + 2]


def images_of(out, signed_ghost, jump, ghost_jump):
    image = out + 0.5 * signed_ghost
    ghost = ghost_jump * signed_ghost + (0.5 * jump * jnp.abs(ghost_jump)) * out
    return image, ghost


def lane_splat(tile, lane):
    return jnp.broadcast_to(tile[:, lane : lane + 1], (SUBLANES, LANES))


def row_splat(tile, row):
    return jnp.broadcast_to(tile[row : row + 1], (SUBLANES, LANES))


def eliminate(matrix, right, want_inverse):
    size = matrix.shape[0]
    eye = lax.broadcasted_iota(jnp.int32, matrix.shape, 0) == lax.broadcasted_iota(
        jnp.int32, matrix.shape, 1
    )
    diagonal = jnp.where(eye, matrix, 0.0)
    by_row = lax.rsqrt(jnp.sum(diagonal, axis=1, keepdims=True))
    by_column = lax.rsqrt(jnp.sum(diagonal, axis=0, keepdims=True))
    matrix = matrix * by_row * by_column
    right = right * by_row
    count = size // SUBLANES
    tiles = [
        [
            matrix[t * SUBLANES : (t + 1) * SUBLANES],
            right[t * SUBLANES : (t + 1) * SUBLANES],
        ]
        for t in range(count)
    ]
    lane = lax.broadcasted_iota(jnp.int32, (SUBLANES, LANES), 1)
    sublane = lax.broadcasted_iota(jnp.int32, (SUBLANES, LANES), 0)
    for start in range(0, size, PIVOT):
        home, first = start // SUBLANES, start % SUBLANES
        columns = [
            [lane_splat(tiles[t][0], start + k) for k in range(PIVOT)] for t in range(count)
        ]
        p = [[row_splat(columns[home][k], first + i) for k in range(PIVOT)] for i in range(PIVOT)]
        block = (lane >= start) & (lane < start + PIVOT)
        r = []
        for i in range(PIVOT):
            row = [row_splat(one, first + i) for one in tiles[home]]
            if want_inverse:
                row[0] = jnp.where(block, jnp.where(lane == start + i, 1.0, 0.0), row[0])
            r.append(row)
        a, b, d = p[0][0], p[0][1], p[1][1]
        inv = 1.0 / (a * d - b * b)
        a, b, d = a * inv, b * inv, d * inv
        t00 = d * p[0][2] - b * p[1][2]
        t01 = d * p[0][3] - b * p[1][3]
        t10 = a * p[1][2] - b * p[0][2]
        t11 = a * p[1][3] - b * p[0][3]
        s00 = p[2][2] - (p[0][2] * t00 + p[1][2] * t10)
        s01 = p[2][3] - (p[0][2] * t01 + p[1][2] * t11)
        s11 = p[3][3] - (p[0][3] * t01 + p[1][3] * t11)
        inv = 1.0 / (s00 * s11 - s01 * s01)
        s00, s01, s11 = s00 * inv, s01 * inv, s11 * inv
        solved = [[], [], [], []]
        for side in range(2):
            y0 = d * r[0][side] - b * r[1][side]
            y1 = a * r[1][side] - b * r[0][side]
            z2 = r[2][side] - (p[0][2] * y0 + p[1][2] * y1)
            z3 = r[3][side] - (p[0][3] * y0 + p[1][3] * y1)
            n2 = s11 * z2 - s01 * z3
            n3 = s00 * z3 - s01 * z2
            solved[0].append(y0 - (t00 * n2 + t01 * n3))
            solved[1].append(y1 - (t10 * n2 + t11 * n3))
            solved[2].append(n2)
            solved[3].append(n3)
        for t in range(count):
            for side in range(2):
                old = tiles[t][side]
                if want_inverse and side == 0:
                    old = jnp.where(block, 0.0, old)
                c = columns[t]
                new = old - (
                    (c[0] * solved[0][side] + c[1] * solved[1][side])
                    + (c[2] * solved[2][side] + c[3] * solved[3][side])
                )
                if t == home:
                    for i in range(PIVOT):
                        new = jnp.where(sublane == first + i, solved[i][side], new)
                tiles[t][side] = new
    inverse = jnp.concatenate([one[0] for one in tiles], axis=0) * by_row * by_column
    return inverse, jnp.concatenate([one[1] for one in tiles], axis=0) * by_row


def square(a00, a01, a11):
    return jnp.concatenate(
        [jnp.concatenate([a00, a01], axis=1), jnp.concatenate([a01.T, a11], axis=1)], axis=0
    )


def start_kernel(place, loads, weights, signs, face_map, small, *sends):
    cases, size = loads.shape
    jump = (2 * signs[...] - 1).astype(jnp.float32)
    rest = jnp.concatenate(
        [weights[...], jump, jnp.zeros((PAD - 2, size), jnp.float32)], axis=0
    )
    value = jnp.concatenate([loads[...], rest], axis=0)
    value = exact_pick(value, pick_columns(face_map[...]))
    small[...] = value
    write_faces(place, value, sends)


def factor_kernel(blocks, pattern, factor, face_map, high, low, masked_high, masked_low):
    size = factor.shape[0]
    length = size // blocks
    for i in range(blocks):
        for j in range(blocks):
            rows, columns = pl.ds(i * length, length), pl.ds(j * length, length)
            value = factor[rows, columns]
            if i != j:
                value = jnp.where(pattern[i, j] == 1, value, 0.0)
            masked_high[rows, columns], masked_low[rows, columns] = halves(value)
    pick = pick_rows(face_map[...])
    high[...] = bf16_dot(pick, masked_high[...], 0).astype(jnp.bfloat16)
    low[...] = bf16_dot(pick, masked_low[...], 0).astype(jnp.bfloat16)


def first_kernel(place, small, x0, x1, y0, y1, high, low, ghosts, half, out, *sends):
    value, ghost = small[...], read_faces(place, (x0, x1, y0, y1))
    ghosts[...] = ghost
    cases = half.shape[0]
    resid, weighting, jump = rows_of(value, cases)
    ghost_resid, ghost_weighting, _ = rows_of(ghost, cases)
    field = weighting * resid + (0.5 * jump) * (ghost_weighting * ghost_resid)
    halfway = product(field, high, low, 0)
    half[...] = halfway
    lifted = product(halfway, high, low, 1)
    out[...] = lifted
    write_faces(place, jump * lifted, sends)


def gram_kernel(
    place, small, ghosts, half, out, x0, x1, y0, y1, high, low, image, ghost_image, second, sums
):
    cases = half.shape[0]
    resid, weighting, jump = rows_of(small[...], cases)
    _, ghost_weighting, ghost_jump = rows_of(ghosts[...], cases)
    own, ghost = images_of(out[...], read_faces(place, (x0, x1, y0, y1)), jump, ghost_jump)
    image[...] = own
    ghost_image[...] = ghost
    field = weighting * own + (0.5 * jump) * (ghost_weighting * ghost)
    largest = jnp.max(jnp.max(jnp.abs(field), axis=1, keepdims=True), axis=0, keepdims=True)
    scale = 1.0 / jnp.maximum(largest, 1e-30)
    second_half = product(field * scale, high, low, 0)
    second[:cases] = second_half
    second[cases:] = jnp.broadcast_to(scale, (PAD, field.shape[1]))
    first_half = half[...]
    cross = inner_prod(second_half, jnp.concatenate([first_half, second_half], axis=0))
    sums[:cases, :cases] = inner_prod(first_half, first_half)
    sums[:cases, cases:] = inner_prod(weighting * resid, resid)
    sums[cases : 2 * cases, :cases] = cross[:, :cases].T
    sums[cases : 2 * cases, cases:] = cross[:, cases:]
    sums[2 * cases :] = jnp.broadcast_to(scale, (PAD, sums.shape[1]))


def lift_kernel(place, small, second, high, low, out, *sends):
    cases = out.shape[0]
    jump = small[cases + 1 : cases + 2]
    lifted = product(second[:cases], high, low, 1)
    out[...] = lifted
    write_faces(place, jnp.concatenate([jump * lifted, second[cases:]], axis=0), sends)


def step_kernel(
    place, small, ghosts, sums, image0, ghost_image0, second, out1, x0, x1, y0, y1, high, low,
    state, inverse, image1, half, out, *sends
):
    cases = half.shape[0]
    resid, weighting, jump = rows_of(small[...], cases)
    ghost_resid, ghost_weighting, ghost_jump = rows_of(ghosts[...], cases)
    total = sums[...]
    scale = total[2 * cases : 2 * cases + 1, :1]
    gram00 = total[:cases, :cases]
    right = jnp.concatenate([total[:cases, cases:], scale * gram00], axis=0)
    right = jnp.concatenate([right, jnp.zeros_like(right)], axis=1)
    gram = square(
        gram00, total[cases : 2 * cases, :cases], total[cases : 2 * cases, cases:]
    )
    inverted, steps = eliminate(gram, right, True)
    inverse[...] = inverted
    steps = steps.T[:cases]
    received = read_faces(place, (x0, x1, y0, y1))
    own_ratio = scale / second[cases : cases + 1]
    there = received[cases : cases + 1]
    ghost_ratio = jnp.where(there > 0.0, scale / jnp.where(there > 0.0, there, 1.0), 0.0)
    own1, ghost1 = images_of(
        out1[...] * own_ratio, received[:cases] * ghost_ratio, jump, ghost_jump
    )
    image1[...] = own1
    resid = resid - times(steps, jnp.concatenate([image0[...], own1], axis=0))
    ghost_resid = ghost_resid - times(
        steps, jnp.concatenate([ghost_image0[...], ghost1], axis=0)
    )
    state[:cases] = resid
    state[cases : 2 * cases, : 2 * cases] = steps
    field = weighting * resid + (0.5 * jump) * (ghost_weighting * ghost_resid)
    halfway = product(field, high, low, 0)
    half[...] = halfway
    lifted = product(halfway, high, low, 1)
    out[...] = lifted
    write_faces(place, jump * lifted, sends)


def next_gram_kernel(
    place, small, ghosts, sums, second, state, half, out, x0, x1, y0, y1, high, low,
    image, next_half, next_sums
):
    cases = half.shape[0]
    _, weighting, jump = rows_of(small[...], cases)
    _, ghost_weighting, ghost_jump = rows_of(ghosts[...], cases)
    scale = sums[2 * cases : 2 * cases + 1, :1]
    own, ghost = images_of(out[...], read_faces(place, (x0, x1, y0, y1)), jump, ghost_jump)
    image[...] = own
    field = scale * (weighting * own + (0.5 * jump) * (ghost_weighting * ghost))
    halfway = product(field, high, low, 0)
    next_half[...] = halfway
    before = second[:cases] * (scale / second[cases : cases + 1])
    both = jnp.concatenate([half[...], halfway], axis=0)
    cross = inner_prod(jnp.concatenate([before, both], axis=0), both)
    resid = state[:cases]
    next_sums[: 2 * cases] = cross[: 2 * cases]
    next_sums[2 * cases :, :cases] = inner_prod(weighting * resid, resid)
    next_sums[2 * cases :, cases:] = cross[2 * cases :, cases:]


def next_lift_kernel(place, small, half, high, low, out, *sends):
    cases = out.shape[0]
    lifted = product(half[...], high, low, 1)
    out[...] = lifted
    write_faces(place, small[cases + 1 : cases + 2] * lifted, sends)


def last_kernel(
    place, small, sums, next_sums, state, inverse, image0, image1, next_image0, out1,
    x0, x1, y0, y1, face_map, solution_out, resid_out
):
    cases = image0.shape[0]
    _, weighting, _ = rows_of(small[...], cases)
    first_resid, resid = small[:cases], state[:cases]
    steps = state[cases : 2 * cases, : 2 * cases]
    scale = sums[2 * cases : 2 * cases + 1, :1]
    total = next_sums[...]
    along = jnp.concatenate(
        [
            jnp.concatenate([jnp.zeros((cases, cases), jnp.float32), total[:cases, :cases]], axis=1),
            total[:cases],
        ],
        axis=0,
    )
    conjugating = times(inverse[...], along)
    gram00 = total[cases : 2 * cases, :cases]
    gram = square(gram00, total[cases : 2 * cases, cases:], total[2 * cases :, cases:])
    gram = gram - times(along.T, conjugating)
    right = jnp.concatenate([total[2 * cases :, :cases], scale * gram00], axis=0)
    right = jnp.concatenate([right, jnp.zeros_like(right)], axis=1)
    _, next_steps = eliminate(gram, right, False)
    old_steps = -times(conjugating, next_steps).T[:cases]
    next_steps = next_steps.T[:cases]
    next_image1 = out1[...] + 0.5 * read_faces(place, (x0, x1, y0, y1))
    images = jnp.concatenate(
        [image0[...], image1[...], next_image0[...], next_image1], axis=0
    )
    resid = resid - times(jnp.concatenate([old_steps, next_steps], axis=1), images)
    fields = weighting * jnp.concatenate(
        [first_resid, scale * image0[...], state[:cases], scale * next_image0[...]], axis=0
    )
    answer = times(jnp.concatenate([steps + old_steps, next_steps], axis=1), fields)
    both = exact_pick(
        jnp.concatenate([answer, resid], axis=0), pick_rows(face_map[...])
    )
    solution_out[...] = both[:cases]
    resid_out[...] = both[cases:]


def call(kernel, name, outs, *operands, scratch=(), mebibytes=24, smem=1):
    shapes = [
        jax.ShapeDtypeStruct(one[0], one[1]) if isinstance(one[0], tuple)
        else jax.ShapeDtypeStruct(one, jnp.float32)
        for one in outs
    ]
    return pl.pallas_call(
        kernel,
        out_shape=shapes,
        in_specs=[SMEM] * smem + [VMEM] * (len(operands) - smem),
        out_specs=[VMEM] * len(shapes),
        scratch_shapes=list(scratch),
        compiler_params=pltpu.CompilerParams(vmem_limit_bytes=mebibytes * 2**20),
        name=name,
    )(*operands)


def swap_pairs(rows, columns, along, parity):
    pairs = []
    for x in range(rows):
        for y in range(columns):
            index, count = (x, rows) if along == "gx" else (y, columns)
            other = index + 1 if index % 2 == parity else index - 1
            if 0 <= other < count:
                target = (other, y) if along == "gx" else (x, other)
            else:
                target = (x, y ^ 1) if along == "gx" else (x ^ 1, y)
                if not (target[0] < rows and target[1] < columns):
                    target = (x, y)
            pairs.append((x * columns + y, target[0] * columns + target[1]))
    return pairs


def swap_faces(sends):
    rows, columns = lax.axis_size("gx"), lax.axis_size("gy")
    received = []
    for send, (along, parity) in zip(sends, (("gx", 0), ("gx", 1), ("gy", 0), ("gy", 1))):
        pairs = swap_pairs(rows, columns, along, parity)
        received.append(lax.ppermute(send, ("gx", "gy"), pairs))
    return received


def stage_masks():
    stages = []
    for axis in ("gy", "gx"):
        count = lax.axis_size(axis)
        step = 1
        if axis == "gy":
            stages.append((axis, (1,)))
            step = 2
        while step < count:
            if step * 2 < count:
                stages.append((axis, (step, 2 * step, 3 * step)))
            else:
                stages.append((axis, (step,)))
            step *= 4
    return stages


def sum_over_devices(value, prepare):
    for axis, masks in stage_masks():
        count = lax.axis_size(axis)
        parts = [value] + [
            lax.ppermute(value, axis, [(source, source ^ mask) for source in range(count)])
            for mask in masks
        ]
        parts, scale = prepare(parts)
        value = parts[0] + parts[1]
        if len(parts) == 4:
            value = value + (parts[2] + parts[3])
        if scale is not None:
            value = jnp.concatenate([value, scale], axis=0)
    return value


def plain(parts):
    return parts, None


def rescaled(parts):
    cases = (parts[0].shape[0] - PAD) // 2
    scales = [part[2 * cases :] for part in parts]
    scale = functools.reduce(jnp.minimum, scales)
    lane = lax.broadcasted_iota(jnp.int32, (cases, 2 * cases), 1)
    ready = []
    for part, own in zip(parts, scales):
        ratio = (scale / own)[:1]
        factor = jnp.where(lane < cases, ratio, ratio * ratio)
        ready.append(
            jnp.concatenate([part[:cases], part[cases : 2 * cases] * factor], axis=0)
        )
    return ready, scale


def local(right_side, weights, signs, face_map, pattern, factor):
    cases, size = right_side.shape[1:]
    blocks = pattern.shape[1]
    place = jnp.stack(
        [
            lax.axis_index("gx"),
            lax.axis_index("gy"),
            jnp.int32(lax.axis_size("gx")),
            jnp.int32(lax.axis_size("gy")),
        ]
    )
    field, padded = (cases, size), (cases + PAD, size)
    face, padded_face = (cases, size // 4), (cases + PAD, size // 4)
    half_type = ((size, size), jnp.bfloat16)

    small, *sends = call(
        start_kernel, "start_fields", [padded] + [padded_face] * 4,
        place, right_side[0], weights, signs, face_map,
    )
    received = swap_faces(sends)
    high, low = call(
        functools.partial(factor_kernel, blocks), "masked_factor", [half_type, half_type],
        pattern[0], factor[0], face_map,
        scratch=[pltpu.VMEM((size, size), jnp.bfloat16)] * 2, mebibytes=40,
    )
    ghosts, half0, out0, *sends = call(
        first_kernel, "first_operator", [padded, field, field] + [face] * 4,
        place, small, *received, high, low,
    )
    received = swap_faces(sends)
    image0, ghost_image0, second, sums = call(
        gram_kernel, "first_gram", [field, field, padded, (2 * cases + PAD, 2 * cases)],
        place, small, ghosts, half0, out0, *received, high, low,
    )
    out1, *sends = call(
        lift_kernel, "second_operator", [field] + [padded_face] * 4,
        place, small, second, high, low,
    )
    sums = sum_over_devices(sums, rescaled)
    received = swap_faces(sends)
    state, inverse, image1, next_half0, next_out0, *sends = call(
        step_kernel, "first_step",
        [(2 * cases, size), (2 * cases, 2 * cases), field, field, field] + [face] * 4,
        place, small, ghosts, sums, image0, ghost_image0, second, out1, *received, high, low,
    )
    received = swap_faces(sends)
    next_image0, next_half1, next_sums = call(
        next_gram_kernel, "second_gram", [field, field, (3 * cases, 2 * cases)],
        place, small, ghosts, sums, second, state, next_half0, next_out0, *received, high, low,
    )
    next_out1, *sends = call(
        next_lift_kernel, "last_operator", [field] + [face] * 4,
        place, small, next_half1, high, low,
    )
    next_sums = sum_over_devices(next_sums, plain)
    received = swap_faces(sends)
    answer, resid = call(
        last_kernel, "last_step", [field, field],
        place, small, sums, next_sums, state, inverse, image0, image1, next_image0, next_out1,
        *received, face_map,
    )
    return (answer[None], resid[None])


def solution(mesh):
    return jax.shard_map(
        local,
        mesh=mesh,
        in_specs=(
            P("gx", None, "gy"),
            P("gx", "gy"),
            P("gx", "gy"),
            P("gx", "gy"),
            P("gx", None, "gy"),
            P("gx", None, "gy"),
        ),
        out_specs=(P("gx", None, "gy"), P("gx", None, "gy")),
        check_vma=False,
    )
```

```python
import functools

import jax
import jax.numpy as jnp
from jax import lax
from jax.experimental import pallas as pl
from jax.experimental.pallas import tpu as pltpu
from jax.sharding import PartitionSpec as P

HIGH = lax.Precision.HIGHEST
VMEM = pl.BlockSpec(memory_space=pltpu.VMEM)
SMEM = pl.BlockSpec(memory_space=pltpu.SMEM)
HBM = pl.BlockSpec(memory_space=pltpu.HBM)
PAD = 8
PIVOT = 4
SUBLANES = 8
LANES = 128


def halves(value):
    high = value.astype(jnp.bfloat16)
    low = (value - high.astype(jnp.float32)).astype(jnp.bfloat16)
    return high, low


def thirds(value):
    high = value.astype(jnp.bfloat16)
    rest = value - high.astype(jnp.float32)
    middle = rest.astype(jnp.bfloat16)
    low = (rest - middle.astype(jnp.float32)).astype(jnp.bfloat16)
    return jnp.concatenate([high, middle, low], axis=0)


def bf16_dot(left, right, right_dim):
    return lax.dot_general(
        left, right, (((1,), (right_dim,)), ((), ())), preferred_element_type=jnp.float32
    )


def exact_pick(value, pick):
    rows = value.shape[0]
    parts = bf16_dot(thirds(value), pick, 0)
    return parts[:rows] + (parts[rows : 2 * rows] + parts[2 * rows :])


def product(value, high, low, dim):
    rows = value.shape[0]
    value_high, value_low = halves(value)
    both = bf16_dot(jnp.concatenate([value_high, value_low], axis=0), high[...], dim)
    return both[:rows] + (both[rows:] + bf16_dot(value_high, low[...], dim))


def inner_prod(left, right):
    return lax.dot_general(
        left, right, (((1,), (1,)), ((), ())), precision=HIGH, preferred_element_type=jnp.float32
    )


def times(left, right):
    return jnp.dot(left, right, precision=HIGH, preferred_element_type=jnp.float32)


def row_to_square(row, size):
    return jnp.broadcast_to(row, (LANES, size)).T


def pick_columns(face_row):
    size = face_row.shape[1]
    unknown = lax.broadcasted_iota(jnp.int32, (size, size), 0)
    return jnp.where(unknown == face_row, 1.0, 0.0).astype(jnp.bfloat16)


def pick_rows(face_row):
    size = face_row.shape[1]
    face = row_to_square(face_row, size)
    lane = lax.broadcasted_iota(jnp.int32, (size, LANES), 1)
    return jnp.concatenate(
        [
            jnp.where(face == lane + start, 1.0, 0.0).astype(jnp.bfloat16)
            for start in range(0, size, LANES)
        ],
        axis=1,
    )


def faces_of(field):
    face_len = field.shape[1] // 4
    return [field[:, face * face_len : (face + 1) * face_len] for face in range(4)]


def write_faces(place, field, outs):
    north, south, west, east = faces_of(field)
    even_x, even_y = place[0] % 2 == 0, place[1] % 2 == 0
    outs[0][...] = jnp.where(even_x, south, north)
    outs[1][...] = jnp.where(even_x, north, south)
    outs[2][...] = jnp.where(even_y, east, west)
    outs[3][...] = jnp.where(even_y, west, east)


def read_faces(place, received):
    x_first, x_second, y_first, y_second = [one[...] for one in received]
    even_x, even_y = place[0] % 2 == 0, place[1] % 2 == 0
    north = jnp.where(place[0] > 0, jnp.where(even_x, x_second, x_first), 0.0)
    south = jnp.where(place[0] + 1 < place[2], jnp.where(even_x, x_first, x_second), 0.0)
    west = jnp.where(place[1] > 0, jnp.where(even_y, y_second, y_first), 0.0)
    east = jnp.where(place[1] + 1 < place[3], jnp.where(even_y, y_first, y_second), 0.0)
    return jnp.concatenate([north, south, west, east], axis=1)


def rows_of(small, cases):
    return small[:cases], small[cases : cases + 1], small[cases + 1 : cases + 2]


def images_of(out, signed_ghost, jump, ghost_jump):
    image = out + 0.5 * signed_ghost
    ghost = ghost_jump * signed_ghost + (0.5 * jump * jnp.abs(ghost_jump)) * out
    return image, ghost


def lane_splat(tile, lane):
    return jnp.broadcast_to(tile[:, lane : lane + 1], (SUBLANES, LANES))


def row_splat(tile, row):
    return jnp.broadcast_to(tile[row : row + 1], (SUBLANES, LANES))


def eliminate(matrix, beside):
    size = matrix.shape[0]
    work = jnp.concatenate([matrix, beside], axis=1)
    row = lax.broadcasted_iota(jnp.int32, work.shape, 0)
    column = lax.broadcasted_iota(jnp.int32, work.shape, 1)
    diagonal = jnp.where(row == column, work, 0.0)
    by_row = lax.rsqrt(jnp.sum(diagonal, axis=1, keepdims=True))
    by_column = lax.rsqrt(
        jnp.where(column[:1] < size, jnp.sum(diagonal, axis=0, keepdims=True), 1.0)
    )
    work = work * by_row * by_column
    count = size // SUBLANES
    tiles = [work[t * SUBLANES : (t + 1) * SUBLANES] for t in range(count)]
    lane = lax.broadcasted_iota(jnp.int32, (SUBLANES, LANES), 1)
    sublane = lax.broadcasted_iota(jnp.int32, (SUBLANES, LANES), 0)
    for start in range(0, size, PIVOT):
        home, first = start // SUBLANES, start % SUBLANES
        columns = [[lane_splat(one, start + k) for k in range(PIVOT)] for one in tiles]
        p = [[row_splat(columns[home][k], first + i) for k in range(PIVOT)] for i in range(PIVOT)]
        block = (lane >= start) & (lane < start + PIVOT)
        r = [
            jnp.where(
                block, jnp.where(lane == start + i, 1.0, 0.0), row_splat(tiles[home], first + i)
            )
            for i in range(PIVOT)
        ]
        a, b, d = p[0][0], p[0][1], p[1][1]
        inv = 1.0 / (a * d - b * b)
        a, b, d = a * inv, b * inv, d * inv
        t00 = d * p[0][2] - b * p[1][2]
        t01 = d * p[0][3] - b * p[1][3]
        t10 = a * p[1][2] - b * p[0][2]
        t11 = a * p[1][3] - b * p[0][3]
        s00 = p[2][2] - (p[0][2] * t00 + p[1][2] * t10)
        s01 = p[2][3] - (p[0][2] * t01 + p[1][2] * t11)
        s11 = p[3][3] - (p[0][3] * t01 + p[1][3] * t11)
        inv = 1.0 / (s00 * s11 - s01 * s01)
        s00, s01, s11 = s00 * inv, s01 * inv, s11 * inv
        y0 = d * r[0] - b * r[1]
        y1 = a * r[1] - b * r[0]
        z2 = r[2] - (p[0][2] * y0 + p[1][2] * y1)
        z3 = r[3] - (p[0][3] * y0 + p[1][3] * y1)
        n2 = s11 * z2 - s01 * z3
        n3 = s00 * z3 - s01 * z2
        solved = [y0 - (t00 * n2 + t01 * n3), y1 - (t10 * n2 + t11 * n3), n2, n3]
        for t in range(count):
            c = columns[t]
            new = jnp.where(block, 0.0, tiles[t]) - (
                (c[0] * solved[0] + c[1] * solved[1]) + (c[2] * solved[2] + c[3] * solved[3])
            )
            if t == home:
                for i in range(PIVOT):
                    new = jnp.where(sublane == first + i, solved[i], new)
            tiles[t] = new
    return jnp.concatenate(tiles, axis=0) * by_row * by_column


def solve_halves(a00, a01, a11, b0, b1):
    size = a00.shape[0]
    first = eliminate(a00, a01)
    along = first[:, size:]
    part = times(first[:, :size], b0)
    taken = times(a01.T, jnp.concatenate([along, part], axis=1))
    second = eliminate(a11 - taken[:, :size], b1 - taken[:, size:])
    x1 = second[:, size:]
    return first, second, part - times(along, x1), x1


def fetch_all(sources, targets, semaphores):
    copies = [
        pltpu.make_async_copy(source, target, semaphores.at[index])
        for index, (source, target) in enumerate(zip(sources, targets))
    ]
    for copy in copies:
        copy.start()
    return copies


def start_kernel(
    place, loads_in, weights_in, signs_in, faces_in, small, *rest
):
    sends, (loads, weights, signs, faces, semaphores) = rest[:4], rest[4:]
    copies = fetch_all(
        (faces_in, loads_in, weights_in, signs_in), (faces, loads, weights, signs), semaphores
    )
    cases, size = loads.shape
    copies[0].wait()
    pick = pick_columns(faces[...])
    for copy in copies[1:]:
        copy.wait()
    jump = (2 * signs[...] - 1).astype(jnp.float32)
    rest = jnp.concatenate(
        [weights[...], jump, jnp.zeros((PAD - 2, size), jnp.float32)], axis=0
    )
    value = exact_pick(jnp.concatenate([loads[...], rest], axis=0), pick)
    small[...] = value
    write_faces(place, value, sends)


def factor_kernel(
    blocks, pattern_in, factor_in, faces_in, high, low, pick_out,
    factor, pattern, faces, masked_high, masked_low, semaphores
):
    size = factor.shape[0]
    length = size // blocks
    bands = [pl.ds(i * length, length) for i in range(blocks)]
    copies = fetch_all(
        [faces_in, pattern_in] + [factor_in.at[band] for band in bands],
        [faces, pattern] + [factor.at[band] for band in bands],
        semaphores,
    )
    copies[0].wait()
    pick = pick_rows(faces[...])
    pick_out[...] = pick
    copies[1].wait()
    for i in range(blocks):
        copies[2 + i].wait()
        for j in range(blocks):
            columns = pl.ds(j * length, length)
            value = factor[bands[i], columns]
            if i != j:
                keep = jnp.broadcast_to(pattern[i : i + 1, j : j + 1], value.shape)
                value = jnp.where(keep == 1, value, 0.0)
            masked_high[bands[i], columns], masked_low[bands[i], columns] = halves(value)
    high[...] = bf16_dot(pick, masked_high[...], 0).astype(jnp.bfloat16)
    low[...] = bf16_dot(pick, masked_low[...], 0).astype(jnp.bfloat16)


def split_sums(place, first, second, more, keep, send):
    even = place[1] % 2 == 0
    rows = first.shape[0]
    keep[:rows] = jnp.where(even, first, second)
    send[:rows] = jnp.where(even, second, first)
    if more is not None:
        keep[rows:] = more
        send[rows:] = more


def join_sums(place, mine, other):
    even = place[1] % 2 == 0
    mine, other = mine[...], other[...]
    return jnp.where(even, mine, other), jnp.where(even, other, mine)


def first_kernel(place, small, x0, x1, y0, y1, high, low, ghosts, half, out, *sends):
    value, ghost = small[...], read_faces(place, (x0, x1, y0, y1))
    ghosts[...] = ghost
    cases = half.shape[0]
    resid, weighting, jump = rows_of(value, cases)
    ghost_resid, ghost_weighting, _ = rows_of(ghost, cases)
    field = weighting * resid + (0.5 * jump) * (ghost_weighting * ghost_resid)
    halfway = product(field, high, low, 0)
    half[...] = halfway
    lifted = product(halfway, high, low, 1)
    out[...] = lifted
    write_faces(place, jump * lifted, sends)


def gram_kernel(
    place, small, ghosts, half, out, x0, x1, y0, y1, high, low, image, ghost_image, second, keep, send
):
    cases = half.shape[0]
    resid, weighting, jump = rows_of(small[...], cases)
    _, ghost_weighting, ghost_jump = rows_of(ghosts[...], cases)
    own, ghost = images_of(out[...], read_faces(place, (x0, x1, y0, y1)), jump, ghost_jump)
    image[...] = own
    ghost_image[...] = ghost
    field = weighting * own + (0.5 * jump) * (ghost_weighting * ghost)
    largest = jnp.max(jnp.max(jnp.abs(field), axis=1, keepdims=True), axis=0, keepdims=True)
    scale = 1.0 / jnp.maximum(largest, 1e-30)
    second_half = product(field * scale, high, low, 0)
    second[:cases] = second_half
    second[cases:] = jnp.broadcast_to(scale, (PAD, field.shape[1]))
    first_half = half[...]
    cross = inner_prod(second_half, jnp.concatenate([first_half, second_half], axis=0))
    split_sums(
        place,
        jnp.concatenate(
            [inner_prod(first_half, first_half), inner_prod(weighting * resid, resid)], axis=1
        ),
        jnp.concatenate([cross[:, :cases].T, cross[:, cases:]], axis=1),
        jnp.broadcast_to(scale, (PAD, 2 * cases)),
        keep,
        send,
    )


def lift_kernel(place, small, second, high, low, out, *sends):
    cases = out.shape[0]
    jump = small[cases + 1 : cases + 2]
    lifted = product(second[:cases], high, low, 1)
    out[...] = lifted
    write_faces(place, jnp.concatenate([jump * lifted, second[cases:]], axis=0), sends)


def step_kernel(
    place, small, ghosts, mine, other, image0, ghost_image0, second, out1, x0, x1, y0, y1, high, low,
    state, inverse, image1, half, out, *sends
):
    cases = half.shape[0]
    resid, weighting, jump = rows_of(small[...], cases)
    ghost_resid, ghost_weighting, ghost_jump = rows_of(ghosts[...], cases)
    scale = mine[cases : cases + 1, :1]
    top, bottom = join_sums(place, mine, other)
    gram00, gram01, gram11 = top[:cases, :cases], bottom[:cases, :cases], bottom[:cases, cases:]
    first, second_part, steps0, steps1 = solve_halves(
        gram00, gram01, gram11, top[:cases, cases:], scale * gram00
    )
    inverse[:cases] = first
    inverse[cases:] = second_part
    steps = jnp.concatenate([steps0, steps1], axis=0).T
    received = read_faces(place, (x0, x1, y0, y1))
    own_ratio = scale / second[cases : cases + 1]
    there = received[cases : cases + 1]
    ghost_ratio = jnp.where(there > 0.0, scale / jnp.where(there > 0.0, there, 1.0), 0.0)
    own1, ghost1 = images_of(
        out1[...] * own_ratio, received[:cases] * ghost_ratio, jump, ghost_jump
    )
    image1[...] = own1
    resid = resid - times(steps, jnp.concatenate([image0[...], own1], axis=0))
    ghost_resid = ghost_resid - times(
        steps, jnp.concatenate([ghost_image0[...], ghost1], axis=0)
    )
    state[:cases] = resid
    state[cases : 2 * cases, : 2 * cases] = steps
    field = weighting * resid + (0.5 * jump) * (ghost_weighting * ghost_resid)
    halfway = product(field, high, low, 0)
    half[...] = halfway
    lifted = product(halfway, high, low, 1)
    out[...] = lifted
    write_faces(place, jump * lifted, sends)


def next_gram_kernel(
    place, small, ghosts, mine, second, state, half, out, x0, x1, y0, y1, high, low,
    image, next_half, keep, send
):
    cases = half.shape[0]
    _, weighting, jump = rows_of(small[...], cases)
    _, ghost_weighting, ghost_jump = rows_of(ghosts[...], cases)
    scale = mine[cases : cases + 1, :1]
    own, ghost = images_of(out[...], read_faces(place, (x0, x1, y0, y1)), jump, ghost_jump)
    image[...] = own
    field = scale * (weighting * own + (0.5 * jump) * (ghost_weighting * ghost))
    halfway = product(field, high, low, 0)
    next_half[...] = halfway
    before = second[:cases] * (scale / second[cases : cases + 1])
    both = jnp.concatenate([half[...], halfway], axis=0)
    cross = inner_prod(jnp.concatenate([before, both], axis=0), both)
    resid = state[:cases]
    total = jnp.concatenate(
        [
            cross[: 2 * cases],
            jnp.concatenate(
                [inner_prod(weighting * resid, resid), cross[2 * cases :, cases:]], axis=1
            ),
        ],
        axis=0,
    )
    middle = total.shape[0] // 2
    split_sums(place, total[:middle], total[middle:], None, keep, send)


def next_lift_kernel(place, small, half, high, low, out, *sends):
    cases = out.shape[0]
    lifted = product(half[...], high, low, 1)
    out[...] = lifted
    write_faces(place, small[cases + 1 : cases + 2] * lifted, sends)


def last_kernel(
    place, small, first_sums, mine, other, state, inverse, image0, image1, next_image0, out1,
    x0, x1, y0, y1, pick, solution_out, resid_out
):
    cases = image0.shape[0]
    _, weighting, _ = rows_of(small[...], cases)
    first_resid, resid = small[:cases], state[:cases]
    steps = state[cases : 2 * cases, : 2 * cases]
    scale = first_sums[cases : cases + 1, :1]
    total = jnp.concatenate(join_sums(place, mine, other), axis=0)
    along0 = jnp.concatenate(
        [jnp.zeros((cases, cases), jnp.float32), total[:cases, :cases]], axis=1
    )
    along1 = total[:cases]
    first, second = inverse[:cases], inverse[cases:]
    beside = first[:, cases:]
    part = times(first[:, :cases], along0)
    against1 = times(second[:, :cases], along1 - times(beside.T, along0))
    conjugating = jnp.concatenate([part - times(beside, against1), against1], axis=0)
    taken = times(jnp.concatenate([along0, along1], axis=0).T, conjugating)
    gram00 = total[cases : 2 * cases, :cases]
    _, _, next0, next1 = solve_halves(
        gram00 - taken[:cases, :cases],
        total[cases : 2 * cases, cases:] - taken[:cases, cases:],
        total[2 * cases :, cases:] - taken[cases:, cases:],
        total[2 * cases :, :cases],
        scale * gram00,
    )
    next_steps = jnp.concatenate([next0, next1], axis=0)
    old_steps = -times(conjugating, next_steps).T
    next_steps = next_steps.T
    next_image1 = out1[...] + 0.5 * read_faces(place, (x0, x1, y0, y1))
    images = jnp.concatenate(
        [image0[...], image1[...], next_image0[...], next_image1], axis=0
    )
    resid = resid - times(jnp.concatenate([old_steps, next_steps], axis=1), images)
    fields = weighting * jnp.concatenate(
        [first_resid, scale * image0[...], state[:cases], scale * next_image0[...]], axis=0
    )
    answer = times(jnp.concatenate([steps + old_steps, next_steps], axis=1), fields)
    both = exact_pick(jnp.concatenate([answer, resid], axis=0), pick[...])
    solution_out[...] = both[:cases]
    resid_out[...] = both[cases:]


def call(kernel, name, outs, *operands, scratch=(), mebibytes=24, smem=1, fetched=False, flops=0):
    shapes = [
        jax.ShapeDtypeStruct(one[0], one[1]) if isinstance(one[0], tuple)
        else jax.ShapeDtypeStruct(one, jnp.float32)
        for one in outs
    ]
    return pl.pallas_call(
        kernel,
        out_shape=shapes,
        in_specs=[SMEM] * smem + [HBM if fetched else VMEM] * (len(operands) - smem),
        out_specs=[VMEM] * len(shapes),
        scratch_shapes=list(scratch),
        compiler_params=pltpu.CompilerParams(vmem_limit_bytes=mebibytes * 2**20),
        cost_estimate=pl.CostEstimate(flops=flops, bytes_accessed=2**20, transcendentals=0),
        name=name,
    )(*operands)


def swap_pairs(rows, columns, along, parity):
    pairs = []
    for x in range(rows):
        for y in range(columns):
            index, count = (x, rows) if along == "gx" else (y, columns)
            other = index + 1 if index % 2 == parity else index - 1
            if 0 <= other < count:
                target = (other, y) if along == "gx" else (x, other)
            else:
                target = (x, y ^ 1) if along == "gx" else (x ^ 1, y)
                if not (target[0] < rows and target[1] < columns):
                    target = (x, y)
            pairs.append((x * columns + y, target[0] * columns + target[1]))
    return pairs


def swap_faces(sends, axes=("gx", "gy")):
    rows, columns = lax.axis_size("gx"), lax.axis_size("gy")
    order = [(along, parity) for along in axes for parity in (0, 1)]
    return [
        lax.ppermute(send, ("gx", "gy"), swap_pairs(rows, columns, along, parity))
        for send, (along, parity) in zip(sends, order)
    ]


def stage_masks(axis, first):
    count = lax.axis_size(axis)
    stages = []
    step = first
    while step < count:
        last = step * 2 >= count
        stages.append((axis, (step,) if last else (step, 2 * step, 3 * step)))
        step *= 4
    return stages


def from_mask(value, axis, mask):
    count = lax.axis_size(axis)
    return lax.ppermute(value, axis, [(source, source ^ mask) for source in range(count)])


def sum_over_devices(keep, send, add, sends):
    value = add([keep, from_mask(send, "gy", 1)])
    beside = {"gy": ("gx", sends[:2]), "gx": ("gy", sends[2:])}
    received = {}
    for axis, masks in stage_masks("gy", 2) + stage_masks("gx", 1):
        along, pair = beside.pop(axis, (None, ()))
        if pair:
            value, *pair = lax.optimization_barrier((value, *pair))
        parts = [value] + [from_mask(value, axis, mask) for mask in masks]
        if pair:
            received[along] = swap_faces(pair, (along,))
        value = add(parts)
        if pair:
            value, *received[along] = lax.optimization_barrier((value, *received[along]))
    for along, pair in beside.values():
        received[along] = swap_faces(pair, (along,))
    return value, from_mask(value, "gy", 1), received["gx"] + received["gy"]


def plain(parts):
    value = parts[0] + parts[1]
    return value + (parts[2] + parts[3]) if len(parts) == 4 else value


def rescaled(parts):
    cases = parts[0].shape[0] - PAD
    scales = [part[cases:] for part in parts]
    scale = functools.reduce(jnp.minimum, scales)
    lane = lax.broadcasted_iota(jnp.int32, (cases, 2 * cases), 1)
    even = lax.axis_index("gy") % 2 == 0
    ready = []
    for part, own in zip(parts, scales):
        ratio = jnp.where(even, 1.0, (scale / own)[:1])
        ready.append(part[:cases] * jnp.where(lane < cases, ratio, ratio * ratio))
    return jnp.concatenate([plain(ready), scale], axis=0)


def local(right_side, weights, signs, face_map, pattern, factor):
    cases, size = right_side.shape[1:]
    blocks = pattern.shape[1]
    place = jnp.stack(
        [
            lax.axis_index("gx"),
            lax.axis_index("gy"),
            jnp.int32(lax.axis_size("gx")),
            jnp.int32(lax.axis_size("gy")),
        ]
    )
    field, padded = (cases, size), (cases + PAD, size)
    face, padded_face = (cases, size // 4), (cases + PAD, size // 4)
    half_type = ((size, size), jnp.bfloat16)

    work = 6 * cases * size * size
    small, *sends = call(
        start_kernel, "start_fields", [padded] + [padded_face] * 4,
        place, right_side[0], weights, signs, face_map,
        scratch=[
            pltpu.VMEM(field, jnp.float32),
            pltpu.VMEM((1, size), jnp.float32),
            pltpu.VMEM((1, size), jnp.int32),
            pltpu.VMEM((1, size), jnp.int32),
            pltpu.SemaphoreType.DMA((4,)),
        ],
        fetched=True, flops=work,
    )
    received = swap_faces(sends)
    high, low, pick = call(
        functools.partial(factor_kernel, blocks), "masked_factor", [half_type] * 3,
        pattern[0], factor[0], face_map,
        scratch=[
            pltpu.VMEM((size, size), jnp.float32),
            pltpu.VMEM((blocks, blocks), jnp.int32),
            pltpu.VMEM((1, size), jnp.int32),
            pltpu.VMEM((size, size), jnp.bfloat16),
            pltpu.VMEM((size, size), jnp.bfloat16),
            pltpu.SemaphoreType.DMA((2 + blocks,)),
        ],
        mebibytes=40, smem=0, fetched=True, flops=4 * size**3,
    )
    ghosts, half0, out0, *sends = call(
        first_kernel, "first_operator", [padded, field, field] + [face] * 4,
        place, small, *received, high, low, flops=2 * work,
    )
    received = swap_faces(sends)
    image0, ghost_image0, second, keep, send = call(
        gram_kernel, "first_gram", [field, field, padded] + [(cases + PAD, 2 * cases)] * 2,
        place, small, ghosts, half0, out0, *received, high, low, flops=2 * work,
    )
    out1, *sends = call(
        lift_kernel, "second_operator", [field] + [padded_face] * 4,
        place, small, second, high, low, flops=work,
    )
    mine, other, faces = sum_over_devices(keep, send, rescaled, sends)
    state, inverse, image1, next_half0, next_out0, *next_sends = call(
        step_kernel, "first_step",
        [(2 * cases, size), (2 * cases, 2 * cases), field, field, field] + [face] * 4,
        place, small, ghosts, mine, other, image0, ghost_image0, second, out1,
        *faces, high, low, flops=4 * work,
    )
    faces = swap_faces(next_sends)
    next_image0, next_half1, keep, send = call(
        next_gram_kernel, "second_gram", [field, field] + [(3 * cases // 2, 2 * cases)] * 2,
        place, small, ghosts, mine, second, state, next_half0, next_out0, *faces, high, low,
        flops=2 * work,
    )
    next_out1, *sends = call(
        next_lift_kernel, "last_operator", [field] + [face] * 4,
        place, small, next_half1, high, low, flops=work,
    )
    next_mine, next_other, faces = sum_over_devices(keep, send, plain, sends)
    answer, resid = call(
        last_kernel, "last_step", [field, field],
        place, small, mine, next_mine, next_other, state, inverse, image0, image1,
        next_image0, next_out1, *faces, pick, flops=4 * work,
    )
    return (answer[None], resid[None])


def solution(mesh):
    return jax.shard_map(
        local,
        mesh=mesh,
        in_specs=(
            P("gx", None, "gy"),
            P("gx", "gy"),
            P("gx", "gy"),
            P("gx", "gy"),
            P("gx", None, "gy"),
            P("gx", None, "gy"),
        ),
        out_specs=(P("gx", None, "gy"), P("gx", None, "gy")),
        check_vma=False,
    )
```

```python
import functools

import jax
import jax.numpy as jnp
from jax import lax
from jax.experimental import pallas as pl
from jax.experimental.pallas import tpu as pltpu
from jax.sharding import PartitionSpec as P

HIGH = lax.Precision.HIGHEST
VMEM = pl.BlockSpec(memory_space=pltpu.VMEM)
SMEM = pl.BlockSpec(memory_space=pltpu.SMEM)
HBM = pl.BlockSpec(memory_space=pltpu.HBM)
PAD = 8
PIVOT = 8
LANES = 128


def halves(value):
    high = value.astype(jnp.bfloat16)
    low = (value - high.astype(jnp.float32)).astype(jnp.bfloat16)
    return high, low


def thirds(value):
    high = value.astype(jnp.bfloat16)
    rest = value - high.astype(jnp.float32)
    middle = rest.astype(jnp.bfloat16)
    low = (rest - middle.astype(jnp.float32)).astype(jnp.bfloat16)
    return jnp.concatenate([high, middle, low], axis=0)


def bf16_dot(left, right, right_dim):
    return lax.dot_general(
        left, right, (((1,), (right_dim,)), ((), ())), preferred_element_type=jnp.float32
    )


def exact_pick(value, pick):
    rows = value.shape[0]
    parts = bf16_dot(thirds(value), pick, 0)
    return parts[:rows] + (parts[rows : 2 * rows] + parts[2 * rows :])


def product(value, high, low, dim):
    rows = value.shape[0]
    value_high, value_low = halves(value)
    both = bf16_dot(jnp.concatenate([value_high, value_low], axis=0), high[...], dim)
    return both[:rows] + (both[rows:] + bf16_dot(value_high, low[...], dim))


def inner_prod(left, right):
    return lax.dot_general(
        left, right, (((1,), (1,)), ((), ())), precision=HIGH, preferred_element_type=jnp.float32
    )


def times(left, right):
    return jnp.dot(left, right, precision=HIGH, preferred_element_type=jnp.float32)


def row_to_square(row, size):
    return jnp.broadcast_to(row, (LANES, size)).T


def pick_columns(face_row):
    size = face_row.shape[1]
    unknown = lax.broadcasted_iota(jnp.int32, (size, size), 0)
    return jnp.where(unknown == face_row, 1.0, 0.0).astype(jnp.bfloat16)


def pick_rows(face_row):
    size = face_row.shape[1]
    face = row_to_square(face_row, size)
    lane = lax.broadcasted_iota(jnp.int32, (size, LANES), 1)
    return jnp.concatenate(
        [
            jnp.where(face == lane + start, 1.0, 0.0).astype(jnp.bfloat16)
            for start in range(0, size, LANES)
        ],
        axis=1,
    )


def faces_of(field):
    face_len = field.shape[1] // 4
    return [field[:, face * face_len : (face + 1) * face_len] for face in range(4)]


def write_faces(place, field, outs):
    north, south, west, east = faces_of(field)
    even_x, even_y = place[0] % 2 == 0, place[1] % 2 == 0
    outs[0][...] = jnp.where(even_x, south, north)
    outs[1][...] = jnp.where(even_x, north, south)
    outs[2][...] = jnp.where(even_y, east, west)
    outs[3][...] = jnp.where(even_y, west, east)


def read_faces(place, received):
    x_first, x_second, y_first, y_second = [one[...] for one in received]
    even_x, even_y = place[0] % 2 == 0, place[1] % 2 == 0
    north = jnp.where(place[0] > 0, jnp.where(even_x, x_second, x_first), 0.0)
    south = jnp.where(place[0] + 1 < place[2], jnp.where(even_x, x_first, x_second), 0.0)
    west = jnp.where(place[1] > 0, jnp.where(even_y, y_second, y_first), 0.0)
    east = jnp.where(place[1] + 1 < place[3], jnp.where(even_y, y_first, y_second), 0.0)
    return jnp.concatenate([north, south, west, east], axis=1)


def rows_of(small, cases):
    return small[:cases], small[cases : cases + 1], small[cases + 1 : cases + 2]


def images_of(out, signed_ghost, jump, ghost_jump):
    image = out + 0.5 * signed_ghost
    ghost = ghost_jump * signed_ghost + (0.5 * jump * jnp.abs(ghost_jump)) * out
    return image, ghost


def lane_splat(tile, lane):
    return jnp.broadcast_to(tile[:, lane : lane + 1], (PIVOT, LANES))


def row_splat(tile, row):
    return jnp.broadcast_to(tile[row : row + 1], (PIVOT, LANES))


def reciprocal(value):
    guess = pl.reciprocal(value, approx=True)
    guess = guess * (2.0 - value * guess)
    return guess * (2.0 - value * guess)


def tree_sum(terms):
    while len(terms) > 1:
        terms = [sum(terms[i + 1 : i + 2], terms[i]) for i in range(0, len(terms), 2)]
    return terms[0]


def block_solve(p, rows):
    size = len(p)
    if size == 2:
        a, b, d = p[0][0], p[0][1], p[1][1]
        inverse = reciprocal(a * d - b * b)
        a, b, d = a * inverse, b * inverse, d * inverse
        return [
            [d * up - b * down for up, down in zip(*rows)],
            [a * down - b * up for up, down in zip(*rows)],
        ]
    half = size // 2
    beside = [p[i][half:] for i in range(half)]
    upper = block_solve(
        [p[i][:half] for i in range(half)], [beside[i] + rows[i] for i in range(half)]
    )
    along, upper = [one[:half] for one in upper], [one[half:] for one in upper]

    def without(value, i, columns):
        return value - tree_sum([beside[m][i] * columns[m] for m in range(half)])

    schur = [
        [
            without(p[half + i][half + j], i, [one[j] for one in along]) if j >= i else None
            for j in range(half)
        ]
        for i in range(half)
    ]
    count = len(rows[0])
    lower = block_solve(
        schur,
        [
            [without(rows[half + i][c], i, [one[c] for one in upper]) for c in range(count)]
            for i in range(half)
        ],
    )
    upper = [
        [
            upper[i][c] - tree_sum([along[i][m] * lower[m][c] for m in range(half)])
            for c in range(count)
        ]
        for i in range(half)
    ]
    return upper + lower


def eliminate(matrix, beside):
    size = matrix.shape[0]
    work = jnp.concatenate([matrix, beside], axis=1)
    row = lax.broadcasted_iota(jnp.int32, work.shape, 0)
    column = lax.broadcasted_iota(jnp.int32, work.shape, 1)
    diagonal = jnp.where(row == column, work, 0.0)
    by_row = lax.rsqrt(jnp.sum(diagonal, axis=1, keepdims=True))
    by_column = lax.rsqrt(
        jnp.where(column[:1] < size, jnp.sum(diagonal, axis=0, keepdims=True), 1.0)
    )
    work = work * by_row * by_column
    count = size // PIVOT
    tiles = [work[t * PIVOT : (t + 1) * PIVOT] for t in range(count)]
    lane = lax.broadcasted_iota(jnp.int32, (PIVOT, LANES), 1)
    sublane = lax.broadcasted_iota(jnp.int32, (PIVOT, LANES), 0)
    for home in range(count):
        start = home * PIVOT
        block = (lane >= start) & (lane < start + PIVOT)
        at_home = [lane_splat(tiles[home], start + k) for k in range(PIVOT)]
        p = [
            [row_splat(at_home[k], i) if k >= i else None for k in range(PIVOT)]
            for i in range(PIVOT)
        ]
        own = jnp.where(block, jnp.where(lane == start + sublane, 1.0, 0.0), tiles[home])
        solved = [one[0] for one in block_solve(p, [[row_splat(own, i)] for i in range(PIVOT)])]
        for t in range(count):
            if t == home:
                new = solved[0]
                for i in range(1, PIVOT):
                    new = jnp.where(sublane == i, solved[i], new)
            else:
                new = jnp.where(block, 0.0, tiles[t]) - tree_sum(
                    [lane_splat(tiles[t], start + k) * solved[k] for k in range(PIVOT)]
                )
            tiles[t] = new
    return jnp.concatenate(tiles, axis=0) * by_row * by_column


def solve_halves(a00, a01, a11, b0, b1):
    size = a00.shape[0]
    first = eliminate(a00, a01)
    along = first[:, size:]
    part = times(first[:, :size], b0)
    taken = times(a01.T, jnp.concatenate([along, part], axis=1))
    second = eliminate(a11 - taken[:, :size], b1 - taken[:, size:])
    x1 = second[:, size:]
    return first, second, part - times(along, x1), x1


def fetch_all(sources, targets, semaphores):
    copies = [
        pltpu.make_async_copy(source, target, semaphores.at[index])
        for index, (source, target) in enumerate(zip(sources, targets))
    ]
    for copy in copies:
        copy.start()
    return copies


def start_kernel(
    place, loads_in, weights_in, signs_in, faces_in, pattern_in, small, *rest
):
    sends, (loads, weights, signs, faces, pattern, semaphores) = rest[:4], rest[4:]
    copies = fetch_all(
        (faces_in, loads_in, weights_in, signs_in, pattern_in),
        (faces, loads, weights, signs, pattern),
        semaphores,
    )
    cases, size = loads.shape
    copies[0].wait()
    pick = pick_columns(faces[...])
    for copy in copies[1:]:
        copy.wait()
    jump = (2 * signs[...] - 1).astype(jnp.float32)
    more = jnp.concatenate(
        [weights[...], jump, jnp.zeros((PAD - 2, size), jnp.float32)], axis=0
    )
    value = exact_pick(jnp.concatenate([loads[...], more], axis=0), pick)
    write_faces(place, value, sends)
    small[: cases + 2] = value[: cases + 2]
    small[cases + 2 : cases + 3] = faces[...].astype(jnp.float32)
    small[cases + 3 :] = jnp.zeros((small.shape[0] - cases - 3, size), jnp.float32)
    small[cases + PAD :, : pattern.shape[1]] = pattern[...].astype(jnp.float32)


def face_row(small, cases):
    return small[cases + 2 : cases + 3].astype(jnp.int32)


def factor_kernel(
    cases, blocks, small, factor_in, high, low, factor, masked_high, masked_low, semaphores
):
    size = factor.shape[0]
    length = size // blocks
    bands = [pl.ds(i * length, length) for i in range(blocks)]
    copies = fetch_all(
        [factor_in.at[band] for band in bands], [factor.at[band] for band in bands], semaphores
    )
    pick = pick_rows(face_row(small, cases))
    pattern = small[cases + PAD :, :LANES]
    for i in range(blocks):
        copies[i].wait()
        for j in range(blocks):
            columns = pl.ds(j * length, length)
            value = factor[bands[i], columns]
            if i != j:
                keep = jnp.broadcast_to(pattern[i : i + 1, j : j + 1], value.shape)
                value = jnp.where(keep == 1.0, value, 0.0)
            masked_high[bands[i], columns], masked_low[bands[i], columns] = halves(value)
    chunk = size // 4
    for masked, out in ((masked_high, high), (masked_low, low)):
        for start in range(0, size, chunk):
            out[start : start + chunk] = bf16_dot(
                pick[start : start + chunk], masked[...], 0
            ).astype(jnp.bfloat16)


def prepare_kernel(cases, small, inverse, pick, gram_inverse):
    pick[...] = pick_rows(face_row(small, cases))
    first, second = inverse[:cases], inverse[cases:]
    beside, lower = first[:, cases:], second[:, :cases]
    corner = -times(beside, lower)
    gram_inverse[:cases, :cases] = first[:, :cases] - times(corner, beside.T)
    gram_inverse[:cases, cases:] = corner
    gram_inverse[cases:, :cases] = corner.T
    gram_inverse[cases:, cases:] = lower


def split_sums(place, first, second, more, keep, send):
    even = place[1] % 2 == 0
    rows = first.shape[0]
    keep[:rows] = jnp.where(even, first, second)
    send[:rows] = jnp.where(even, second, first)
    if more is not None:
        keep[rows:] = more
        send[rows:] = more


def join_sums(place, mine, other):
    even = place[1] % 2 == 0
    mine, other = mine[...], other[...]
    return jnp.where(even, mine, other), jnp.where(even, other, mine)


def first_kernel(place, small, x0, x1, y0, y1, high, low, ghosts, half, out, *sends):
    value, ghost = small[...], read_faces(place, (x0, x1, y0, y1))
    ghosts[...] = ghost
    cases = half.shape[0]
    resid, weighting, jump = rows_of(value, cases)
    ghost_resid, ghost_weighting, _ = rows_of(ghost, cases)
    field = weighting * resid + (0.5 * jump) * (ghost_weighting * ghost_resid)
    halfway = product(field, high, low, 0)
    half[...] = halfway
    lifted = product(halfway, high, low, 1)
    out[...] = lifted
    write_faces(place, jump * lifted, sends)


def gram_kernel(
    place, small, ghosts, half, out, x0, x1, y0, y1, high, low, image, ghost_image, second, keep, send
):
    cases = half.shape[0]
    resid, weighting, jump = rows_of(small[...], cases)
    _, ghost_weighting, ghost_jump = rows_of(ghosts[...], cases)
    own, ghost = images_of(out[...], read_faces(place, (x0, x1, y0, y1)), jump, ghost_jump)
    image[...] = own
    ghost_image[...] = ghost
    field = weighting * own + (0.5 * jump) * (ghost_weighting * ghost)
    largest = jnp.max(jnp.max(jnp.abs(field), axis=1, keepdims=True), axis=0, keepdims=True)
    scale = 1.0 / jnp.maximum(largest, 1e-30)
    second_half = product(field * scale, high, low, 0)
    second[:cases] = second_half
    second[cases:] = jnp.broadcast_to(scale, (PAD, field.shape[1]))
    first_half = half[...]
    cross = inner_prod(second_half, jnp.concatenate([first_half, second_half], axis=0))
    split_sums(
        place,
        jnp.concatenate(
            [inner_prod(first_half, first_half), inner_prod(weighting * resid, resid)], axis=1
        ),
        jnp.concatenate([cross[:, :cases].T, cross[:, cases:]], axis=1),
        jnp.broadcast_to(scale, (PAD, 2 * cases)),
        keep,
        send,
    )


def lift_kernel(place, small, second, high, low, out, *sends):
    cases = out.shape[0]
    jump = small[cases + 1 : cases + 2]
    lifted = product(second[:cases], high, low, 1)
    out[...] = lifted
    write_faces(place, jnp.concatenate([jump * lifted, second[cases:]], axis=0), sends)


def step_kernel(
    place, small, ghosts, mine, other, image0, ghost_image0, second, out1, x0, x1, y0, y1, high, low,
    state, inverse, image1, half, out, *sends
):
    cases = half.shape[0]
    resid, weighting, jump = rows_of(small[...], cases)
    ghost_resid, ghost_weighting, ghost_jump = rows_of(ghosts[...], cases)
    scale = mine[cases : cases + 1, :1]
    top, bottom = join_sums(place, mine, other)
    gram00, gram01, gram11 = top[:cases, :cases], bottom[:cases, :cases], bottom[:cases, cases:]
    first, second_part, steps0, steps1 = solve_halves(
        gram00, gram01, gram11, top[:cases, cases:], scale * gram00
    )
    inverse[:cases] = first
    inverse[cases:] = second_part
    steps = jnp.concatenate([steps0, steps1], axis=0).T
    received = read_faces(place, (x0, x1, y0, y1))
    own_ratio = scale / second[cases : cases + 1]
    there = received[cases : cases + 1]
    ghost_ratio = jnp.where(there > 0.0, scale / jnp.where(there > 0.0, there, 1.0), 0.0)
    own1, ghost1 = images_of(
        out1[...] * own_ratio, received[:cases] * ghost_ratio, jump, ghost_jump
    )
    image1[...] = own1
    resid = resid - times(steps, jnp.concatenate([image0[...], own1], axis=0))
    ghost_resid = ghost_resid - times(
        steps, jnp.concatenate([ghost_image0[...], ghost1], axis=0)
    )
    state[:cases] = resid
    state[cases : 2 * cases, : 2 * cases] = steps
    field = weighting * resid + (0.5 * jump) * (ghost_weighting * ghost_resid)
    halfway = product(field, high, low, 0)
    half[...] = halfway
    lifted = product(halfway, high, low, 1)
    out[...] = lifted
    write_faces(place, jump * lifted, sends)


def next_gram_kernel(
    place, small, ghosts, mine, second, state, half, out, x0, x1, y0, y1, high, low,
    image, next_half, keep, send
):
    cases = half.shape[0]
    _, weighting, jump = rows_of(small[...], cases)
    _, ghost_weighting, ghost_jump = rows_of(ghosts[...], cases)
    scale = mine[cases : cases + 1, :1]
    own, ghost = images_of(out[...], read_faces(place, (x0, x1, y0, y1)), jump, ghost_jump)
    image[...] = own
    field = scale * (weighting * own + (0.5 * jump) * (ghost_weighting * ghost))
    halfway = product(field, high, low, 0)
    next_half[...] = halfway
    before = second[:cases] * (scale / second[cases : cases + 1])
    both = jnp.concatenate([half[...], halfway], axis=0)
    cross = inner_prod(jnp.concatenate([before, both], axis=0), both)
    resid = state[:cases]
    total = jnp.concatenate(
        [
            cross[: 2 * cases],
            jnp.concatenate(
                [inner_prod(weighting * resid, resid), cross[2 * cases :, cases:]], axis=1
            ),
        ],
        axis=0,
    )
    middle = total.shape[0] // 2
    split_sums(place, total[:middle], total[middle:], None, keep, send)


def next_lift_kernel(place, small, half, high, low, out, *sends):
    cases = out.shape[0]
    lifted = product(half[...], high, low, 1)
    out[...] = lifted
    write_faces(place, small[cases + 1 : cases + 2] * lifted, sends)


def last_kernel(
    place, small, first_sums, mine, other, state, gram_inverse, image0, image1, next_image0, out1,
    x0, x1, y0, y1, pick, solution_out, resid_out
):
    cases = image0.shape[0]
    _, weighting, _ = rows_of(small[...], cases)
    first_resid, resid = small[:cases], state[:cases]
    steps = state[cases : 2 * cases, : 2 * cases]
    scale = first_sums[cases : cases + 1, :1]
    total = jnp.concatenate(join_sums(place, mine, other), axis=0)
    along = jnp.concatenate(
        [
            jnp.concatenate([jnp.zeros((cases, cases), jnp.float32), total[:cases, :cases]], axis=1),
            total[:cases],
        ],
        axis=0,
    )
    conjugating = times(gram_inverse[...], along)
    taken = times(along.T, conjugating)
    gram00 = total[cases : 2 * cases, :cases]
    _, _, next0, next1 = solve_halves(
        gram00 - taken[:cases, :cases],
        total[cases : 2 * cases, cases:] - taken[:cases, cases:],
        total[2 * cases :, cases:] - taken[cases:, cases:],
        total[2 * cases :, :cases],
        scale * gram00,
    )
    next_steps = jnp.concatenate([next0, next1], axis=0)
    old_steps = -times(conjugating, next_steps).T
    next_steps = next_steps.T
    next_image1 = out1[...] + 0.5 * read_faces(place, (x0, x1, y0, y1))
    images = jnp.concatenate(
        [image0[...], image1[...], next_image0[...], next_image1], axis=0
    )
    resid = resid - times(jnp.concatenate([old_steps, next_steps], axis=1), images)
    fields = weighting * jnp.concatenate(
        [first_resid, scale * image0[...], state[:cases], scale * next_image0[...]], axis=0
    )
    answer = times(jnp.concatenate([steps + old_steps, next_steps], axis=1), fields)
    both = exact_pick(jnp.concatenate([answer, resid], axis=0), pick[...])
    solution_out[...] = both[:cases]
    resid_out[...] = both[cases:]


def call(kernel, name, outs, *operands, scratch=(), mebibytes=24, smem=1, fetched=0, flops=0):
    shapes = [
        jax.ShapeDtypeStruct(one[0], one[1]) if isinstance(one[0], tuple)
        else jax.ShapeDtypeStruct(one, jnp.float32)
        for one in outs
    ]
    return pl.pallas_call(
        kernel,
        out_shape=shapes,
        in_specs=[SMEM] * smem + [VMEM] * (len(operands) - smem - fetched) + [HBM] * fetched,
        out_specs=[VMEM] * len(shapes),
        scratch_shapes=list(scratch),
        compiler_params=pltpu.CompilerParams(vmem_limit_bytes=mebibytes * 2**20),
        cost_estimate=pl.CostEstimate(flops=flops, bytes_accessed=2**20, transcendentals=0),
        name=name,
    )(*operands)


def swap_pairs(rows, columns, along, parity):
    pairs = []
    for x in range(rows):
        for y in range(columns):
            index, count = (x, rows) if along == "gx" else (y, columns)
            other = index + 1 if index % 2 == parity else index - 1
            if 0 <= other < count:
                target = (other, y) if along == "gx" else (x, other)
            else:
                target = (x, y ^ 1) if along == "gx" else (x ^ 1, y)
                if not (target[0] < rows and target[1] < columns):
                    target = (x, y)
            pairs.append((x * columns + y, target[0] * columns + target[1]))
    return pairs


def swap_faces(sends, axes=("gx", "gy")):
    rows, columns = lax.axis_size("gx"), lax.axis_size("gy")
    order = [(along, parity) for along in axes for parity in (0, 1)]
    return [
        lax.ppermute(send, ("gx", "gy"), swap_pairs(rows, columns, along, parity))
        for send, (along, parity) in zip(sends, order)
    ]


def stage_masks(axis, first):
    count = lax.axis_size(axis)
    stages = []
    step = first
    while step < count:
        last = step * 2 >= count
        stages.append((axis, (step,) if last else (step, 2 * step, 3 * step)))
        step *= 4
    return stages


def from_mask(value, axis, mask):
    count = lax.axis_size(axis)
    return lax.ppermute(value, axis, [(source, source ^ mask) for source in range(count)])


def sum_over_devices(keep, send, add, sends, work=None, inputs=()):
    value = add([keep, from_mask(send, "gy", 1)])
    beside = {"gy": ("gx", sends[:2]), "gx": ("gy", sends[2:])}
    received, done = {}, ()
    for axis, masks in stage_masks("gy", 2) + stage_masks("gx", 1):
        along, pair = beside.pop(axis, (None, ()))
        if pair:
            value, inputs, pair = lax.optimization_barrier((value, inputs, pair))
        parts = [value] + [from_mask(value, axis, mask) for mask in masks]
        if pair:
            received[along] = swap_faces(pair, (along,))
        if work is not None:
            done, work = work(*inputs), None
        value = add(parts)
        if pair:
            value, done, received[along] = lax.optimization_barrier(
                (value, done, received[along])
            )
    for along, pair in beside.values():
        received[along] = swap_faces(pair, (along,))
    if work is not None:
        done = work(*inputs)
    return value, from_mask(value, "gy", 1), received["gx"] + received["gy"], done


def plain(parts):
    value = parts[0] + parts[1]
    return value + (parts[2] + parts[3]) if len(parts) == 4 else value


def rescaled(parts):
    cases = parts[0].shape[0] - PAD
    scales = [part[cases:] for part in parts]
    scale = functools.reduce(jnp.minimum, scales)
    lane = lax.broadcasted_iota(jnp.int32, (cases, 2 * cases), 1)
    even = lax.axis_index("gy") % 2 == 0
    ready = []
    for part, own in zip(parts, scales):
        ratio = jnp.where(even, 1.0, (scale / own)[:1])
        ready.append(part[:cases] * jnp.where(lane < cases, ratio, ratio * ratio))
    return jnp.concatenate([plain(ready), scale], axis=0)


def local(right_side, weights, signs, face_map, pattern, factor):
    cases, size = right_side.shape[1:]
    blocks = pattern.shape[1]
    place = jnp.stack(
        [
            lax.axis_index("gx"),
            lax.axis_index("gy"),
            jnp.int32(lax.axis_size("gx")),
            jnp.int32(lax.axis_size("gy")),
        ]
    )
    field, padded = (cases, size), (cases + PAD, size)
    face, padded_face = (cases, size // 4), (cases + PAD, size // 4)
    half_type = ((size, size), jnp.bfloat16)

    work = 6 * cases * size * size
    small, *sends = call(
        start_kernel, "start_fields", [(cases + PAD + blocks, size)] + [padded_face] * 4,
        place, right_side[0], weights, signs, face_map, pattern[0],
        scratch=[
            pltpu.VMEM(field, jnp.float32),
            pltpu.VMEM((1, size), jnp.float32),
            pltpu.VMEM((1, size), jnp.int32),
            pltpu.VMEM((1, size), jnp.int32),
            pltpu.VMEM((blocks, blocks), jnp.int32),
            pltpu.SemaphoreType.DMA((5,)),
        ],
        mebibytes=60, fetched=5, flops=work,
    )
    received = swap_faces(sends)
    high, low = call(
        functools.partial(factor_kernel, cases, blocks), "masked_factor", [half_type] * 2,
        small, factor[0],
        scratch=[
            pltpu.VMEM((size, size), jnp.float32),
            pltpu.VMEM((size, size), jnp.bfloat16),
            pltpu.VMEM((size, size), jnp.bfloat16),
            pltpu.SemaphoreType.DMA((blocks,)),
        ],
        mebibytes=48, smem=0, fetched=1, flops=4 * size**3,
    )
    ghosts, half0, out0, *sends = call(
        first_kernel, "first_operator", [padded, field, field] + [face] * 4,
        place, small, *received, high, low, flops=2 * work,
    )
    received = swap_faces(sends)
    image0, ghost_image0, second, keep, send = call(
        gram_kernel, "first_gram", [field, field, padded] + [(cases + PAD, 2 * cases)] * 2,
        place, small, ghosts, half0, out0, *received, high, low, flops=2 * work,
    )
    out1, *sends = call(
        lift_kernel, "second_operator", [field] + [padded_face] * 4,
        place, small, second, high, low, flops=work,
    )
    mine, other, faces, _ = sum_over_devices(keep, send, rescaled, sends)
    state, inverse, image1, next_half0, next_out0, *next_sends = call(
        step_kernel, "first_step",
        [(2 * cases, size), (2 * cases, 2 * cases), field, field, field] + [face] * 4,
        place, small, ghosts, mine, other, image0, ghost_image0, second, out1,
        *faces, high, low, flops=4 * work,
    )
    faces = swap_faces(next_sends)
    next_image0, next_half1, keep, send = call(
        next_gram_kernel, "second_gram", [field, field] + [(3 * cases // 2, 2 * cases)] * 2,
        place, small, ghosts, mine, second, state, next_half0, next_out0, *faces, high, low,
        flops=2 * work,
    )
    next_out1, *sends = call(
        next_lift_kernel, "last_operator", [field] + [face] * 4,
        place, small, next_half1, high, low, flops=work,
    )

    def prepare(small, inverse):
        return call(
            functools.partial(prepare_kernel, cases), "prepare_last",
            [half_type, (2 * cases, 2 * cases)], small, inverse, smem=0, flops=work,
        )

    next_mine, next_other, faces, (pick, gram_inverse) = sum_over_devices(
        keep, send, plain, sends, prepare, (small, inverse)
    )
    answer, resid = call(
        last_kernel, "last_step", [field, field],
        place, small, mine, next_mine, next_other, state, gram_inverse, image0, image1,
        next_image0, next_out1, *faces, pick, flops=4 * work,
    )
    return (answer[None], resid[None])


def solution(mesh):
    return jax.shard_map(
        local,
        mesh=mesh,
        in_specs=(
            P("gx", None, "gy"),
            P("gx", "gy"),
            P("gx", "gy"),
            P("gx", "gy"),
            P("gx", None, "gy"),
            P("gx", None, "gy"),
        ),
        out_specs=(P("gx", None, "gy"), P("gx", None, "gy")),
        check_vma=False,
    )
```

```python
import functools

import jax
import jax.numpy as jnp
from jax import lax
from jax.experimental import pallas as pl
from jax.experimental.pallas import tpu as pltpu
from jax.sharding import PartitionSpec as P

HIGH = lax.Precision.HIGHEST
VMEM = pl.BlockSpec(memory_space=pltpu.VMEM)
SMEM = pl.BlockSpec(memory_space=pltpu.SMEM)
PAD = 8
SMALL = 4e-4
LANES = 128


def halves(value):
    high = value.astype(jnp.bfloat16)
    low = (value - high.astype(jnp.float32)).astype(jnp.bfloat16)
    return high, low


def thirds(value):
    high = value.astype(jnp.bfloat16)
    rest = value - high.astype(jnp.float32)
    middle = rest.astype(jnp.bfloat16)
    low = (rest - middle.astype(jnp.float32)).astype(jnp.bfloat16)
    return jnp.concatenate([high, middle, low], axis=0)


def bf16_dot(left, right, right_dim):
    return lax.dot_general(
        left, right, (((1,), (right_dim,)), ((), ())), preferred_element_type=jnp.float32
    )


def exact_pick(value, pick):
    rows = value.shape[0]
    parts = bf16_dot(thirds(value), pick, 0)
    return parts[:rows] + (parts[rows : 2 * rows] + parts[2 * rows :])


def product(value, high, low, dim):
    rows = value.shape[0]
    value_high, value_low = halves(value)
    both = bf16_dot(jnp.concatenate([value_high, value_low], axis=0), high[...], dim)
    return both[:rows] + (both[rows:] + bf16_dot(value_high, low[...], dim))


def inner_prod(left, right):
    return lax.dot_general(
        left, right, (((1,), (1,)), ((), ())), precision=HIGH, preferred_element_type=jnp.float32
    )


def times(left, right):
    return jnp.dot(left, right, precision=HIGH, preferred_element_type=jnp.float32)


def row_to_square(row, size):
    return jnp.broadcast_to(row, (LANES, size)).T


def pick_columns(face_row):
    size = face_row.shape[1]
    unknown = lax.broadcasted_iota(jnp.int32, (size, size), 0)
    return jnp.where(unknown == face_row, 1.0, 0.0).astype(jnp.bfloat16)


def pick_rows(face_row):
    size = face_row.shape[1]
    face = row_to_square(face_row, size)
    lane = lax.broadcasted_iota(jnp.int32, (size, LANES), 1)
    return jnp.concatenate(
        [
            jnp.where(face == lane + start, 1.0, 0.0).astype(jnp.bfloat16)
            for start in range(0, size, LANES)
        ],
        axis=1,
    )


def faces_of(field):
    face_len = field.shape[1] // 4
    return [field[:, face * face_len : (face + 1) * face_len] for face in range(4)]


def write_faces(place, field, outs):
    north, south, west, east = faces_of(field)
    even_x, even_y = place[0] % 2 == 0, place[1] % 2 == 0
    outs[0][...] = jnp.where(even_x, south, north)
    outs[1][...] = jnp.where(even_x, north, south)
    outs[2][...] = jnp.where(even_y, east, west)
    outs[3][...] = jnp.where(even_y, west, east)


def read_faces(place, received):
    x_first, x_second, y_first, y_second = [one[...] for one in received]
    even_x, even_y = place[0] % 2 == 0, place[1] % 2 == 0
    north = jnp.where(place[0] > 0, jnp.where(even_x, x_second, x_first), 0.0)
    south = jnp.where(place[0] + 1 < place[2], jnp.where(even_x, x_first, x_second), 0.0)
    west = jnp.where(place[1] > 0, jnp.where(even_y, y_second, y_first), 0.0)
    east = jnp.where(place[1] + 1 < place[3], jnp.where(even_y, y_first, y_second), 0.0)
    return jnp.concatenate([north, south, west, east], axis=1)


def rows_of(small, cases):
    return small[:cases], small[cases : cases + 1], small[cases + 1 : cases + 2]


def images_of(out, signed_ghost, jump, ghost_jump):
    image = out + 0.5 * signed_ghost
    ghost = ghost_jump * signed_ghost + (0.5 * jump * jnp.abs(ghost_jump)) * out
    return image, ghost


def inverse_of(matrix):
    size = matrix.shape[0]
    eye = lax.broadcasted_iota(jnp.int32, matrix.shape, 0) == lax.broadcasted_iota(
        jnp.int32, matrix.shape, 1
    )
    diagonal = jnp.where(eye, matrix, 0.0)
    by_row = lax.rsqrt(jnp.sum(diagonal, axis=1, keepdims=True))
    by_column = lax.rsqrt(jnp.sum(diagonal, axis=0, keepdims=True))
    scaled = matrix * by_row * by_column
    bound = jnp.max(jnp.sum(jnp.abs(scaled), axis=0, keepdims=True), axis=1, keepdims=True)
    one = jnp.where(eye, 1.0, 0.0)

    def again(state):
        _, before, now, count = state
        return (count < 2) | ((now > SMALL) & ((now < before) | (now > 1.0)) & (count < 64))

    def better(state):
        x, _, now, count = state
        left = one - times(scaled, x)
        norm = jnp.sum(left * left)
        nearer = x + times(x, left)
        return nearer + times(nearer, times(left, left)), now, norm, count + 1

    start = one * (1.0 / bound)
    x, _, _, _ = lax.while_loop(
        again, better, (start, jnp.float32(size), jnp.float32(size), jnp.int32(0))
    )
    return x * by_row * by_column


def solve_halves(a00, a01, a11, b0, b1):
    size = a00.shape[0]
    first = inverse_of(a00)
    both = times(first, jnp.concatenate([a01, b0], axis=1))
    along, part = both[:, :size], both[:, size:]
    taken = times(a01.T, both)
    second = inverse_of(a11 - taken[:, :size])
    x1 = times(second, b1 - taken[:, size:])
    return first, along, second, part - times(along, x1), x1


def start_kernel(place, loads, weights, signs, faces, small, *sends):
    cases, size = loads.shape
    jump = (2 * signs[...] - 1).astype(jnp.float32)
    more = jnp.concatenate(
        [weights[...], jump, jnp.zeros((PAD - 2, size), jnp.float32)], axis=0
    )
    value = exact_pick(
        jnp.concatenate([loads[...], more], axis=0), pick_columns(faces[...])
    )
    write_faces(place, value, sends)
    small[...] = value
    small[cases + 2 : cases + 3] = faces[...].astype(jnp.float32)


def face_row(small, cases):
    return small[cases + 2 : cases + 3].astype(jnp.int32)


def factor_kernel(blocks, pattern, factor, faces, high, low, masked_high, masked_low):
    size = factor.shape[0]
    length = size // blocks
    for i in range(blocks):
        for j in range(blocks):
            rows, columns = pl.ds(i * length, length), pl.ds(j * length, length)
            value = factor[rows, columns]
            if i != j:
                keep = jnp.broadcast_to(pattern[i : i + 1, j : j + 1], value.shape)
                value = jnp.where(keep == 1, value, 0.0)
            masked_high[rows, columns], masked_low[rows, columns] = halves(value)
    pick = pick_rows(faces[...])
    chunk = size // 4
    for masked, out in ((masked_high, high), (masked_low, low)):
        for start in range(0, size, chunk):
            out[start : start + chunk] = bf16_dot(
                pick[start : start + chunk], masked[...], 0
            ).astype(jnp.bfloat16)


def prepare_kernel(cases, small, inverse, pick, gram_inverse):
    pick[...] = pick_rows(face_row(small, cases))
    first, second = inverse[:cases], inverse[cases:]
    beside, lower = first[:, cases:], second[:, :cases]
    corner = -times(beside, lower)
    gram_inverse[:cases, :cases] = first[:, :cases] - times(corner, beside.T)
    gram_inverse[:cases, cases:] = corner
    gram_inverse[cases:, :cases] = corner.T
    gram_inverse[cases:, cases:] = lower


def split_sums(place, first, second, more, keep, send):
    even = place[1] % 2 == 0
    rows = first.shape[0]
    keep[:rows] = jnp.where(even, first, second)
    send[:rows] = jnp.where(even, second, first)
    if more is not None:
        keep[rows:] = more
        send[rows:] = more


def join_sums(place, mine, other):
    even = place[1] % 2 == 0
    mine, other = mine[...], other[...]
    return jnp.where(even, mine, other), jnp.where(even, other, mine)


def first_kernel(place, small, x0, x1, y0, y1, high, low, ghosts, half, out, *sends):
    value, ghost = small[...], read_faces(place, (x0, x1, y0, y1))
    ghosts[...] = ghost
    cases = half.shape[0]
    resid, weighting, jump = rows_of(value, cases)
    ghost_resid, ghost_weighting, _ = rows_of(ghost, cases)
    field = weighting * resid + (0.5 * jump) * (ghost_weighting * ghost_resid)
    halfway = product(field, high, low, 0)
    half[...] = halfway
    lifted = product(halfway, high, low, 1)
    out[...] = lifted
    write_faces(place, jump * lifted, sends)


def gram_kernel(
    place, small, ghosts, half, out, x0, x1, y0, y1, high, low, image, ghost_image, second, keep, send
):
    cases = half.shape[0]
    resid, weighting, jump = rows_of(small[...], cases)
    _, ghost_weighting, ghost_jump = rows_of(ghosts[...], cases)
    own, ghost = images_of(out[...], read_faces(place, (x0, x1, y0, y1)), jump, ghost_jump)
    image[...] = own
    ghost_image[...] = ghost
    field = weighting * own + (0.5 * jump) * (ghost_weighting * ghost)
    largest = jnp.max(jnp.max(jnp.abs(field), axis=1, keepdims=True), axis=0, keepdims=True)
    scale = 1.0 / jnp.maximum(largest, 1e-30)
    second_half = product(field * scale, high, low, 0)
    second[:cases] = second_half
    second[cases:] = jnp.broadcast_to(scale, (PAD, field.shape[1]))
    first_half = half[...]
    cross = inner_prod(second_half, jnp.concatenate([first_half, second_half], axis=0))
    split_sums(
        place,
        jnp.concatenate(
            [inner_prod(first_half, first_half), inner_prod(weighting * resid, resid)], axis=1
        ),
        jnp.concatenate([cross[:, :cases].T, cross[:, cases:]], axis=1),
        jnp.broadcast_to(scale, (PAD, 2 * cases)),
        keep,
        send,
    )


def lift_kernel(place, small, second, high, low, out, *sends):
    cases = out.shape[0]
    jump = small[cases + 1 : cases + 2]
    lifted = product(second[:cases], high, low, 1)
    out[...] = lifted
    write_faces(place, jnp.concatenate([jump * lifted, second[cases:]], axis=0), sends)


def step_kernel(
    place, small, ghosts, mine, other, image0, ghost_image0, second, out1, x0, x1, y0, y1, high, low,
    state, inverse, image1, half, out, *sends
):
    cases = half.shape[0]
    resid, weighting, jump = rows_of(small[...], cases)
    ghost_resid, ghost_weighting, ghost_jump = rows_of(ghosts[...], cases)
    scale = mine[cases : cases + 1, :1]
    top, bottom = join_sums(place, mine, other)
    gram00, gram01, gram11 = top[:cases, :cases], bottom[:cases, :cases], bottom[:cases, cases:]
    first, along, corner, steps0, steps1 = solve_halves(
        gram00, gram01, gram11, top[:cases, cases:], scale * gram00
    )
    inverse[:cases, :cases] = first
    inverse[:cases, cases:] = along
    inverse[cases:, :cases] = corner
    inverse[cases:, cases:] = corner
    steps = jnp.concatenate([steps0, steps1], axis=0).T
    received = read_faces(place, (x0, x1, y0, y1))
    own_ratio = scale / second[cases : cases + 1]
    there = received[cases : cases + 1]
    ghost_ratio = jnp.where(there > 0.0, scale / jnp.where(there > 0.0, there, 1.0), 0.0)
    own1, ghost1 = images_of(
        out1[...] * own_ratio, received[:cases] * ghost_ratio, jump, ghost_jump
    )
    image1[...] = own1
    resid = resid - times(steps, jnp.concatenate([image0[...], own1], axis=0))
    ghost_resid = ghost_resid - times(
        steps, jnp.concatenate([ghost_image0[...], ghost1], axis=0)
    )
    state[:cases] = resid
    state[cases : 2 * cases, : 2 * cases] = steps
    field = weighting * resid + (0.5 * jump) * (ghost_weighting * ghost_resid)
    halfway = product(field, high, low, 0)
    half[...] = halfway
    lifted = product(halfway, high, low, 1)
    out[...] = lifted
    write_faces(place, jump * lifted, sends)


def next_gram_kernel(
    place, small, ghosts, mine, second, state, half, out, x0, x1, y0, y1, high, low,
    image, next_half, keep, send
):
    cases = half.shape[0]
    _, weighting, jump = rows_of(small[...], cases)
    _, ghost_weighting, ghost_jump = rows_of(ghosts[...], cases)
    scale = mine[cases : cases + 1, :1]
    own, ghost = images_of(out[...], read_faces(place, (x0, x1, y0, y1)), jump, ghost_jump)
    image[...] = own
    field = scale * (weighting * own + (0.5 * jump) * (ghost_weighting * ghost))
    halfway = product(field, high, low, 0)
    next_half[...] = halfway
    before = second[:cases] * (scale / second[cases : cases + 1])
    both = jnp.concatenate([half[...], halfway], axis=0)
    cross = inner_prod(jnp.concatenate([before, both], axis=0), both)
    resid = state[:cases]
    total = jnp.concatenate(
        [
            cross[: 2 * cases],
            jnp.concatenate(
                [inner_prod(weighting * resid, resid), cross[2 * cases :, cases:]], axis=1
            ),
        ],
        axis=0,
    )
    middle = total.shape[0] // 2
    split_sums(place, total[:middle], total[middle:], None, keep, send)


def next_lift_kernel(place, small, half, high, low, out, *sends):
    cases = out.shape[0]
    lifted = product(half[...], high, low, 1)
    out[...] = lifted
    write_faces(place, small[cases + 1 : cases + 2] * lifted, sends)


def last_kernel(
    place, small, first_sums, mine, other, state, gram_inverse, image0, image1, next_image0, out1,
    x0, x1, y0, y1, pick, solution_out, resid_out
):
    cases = image0.shape[0]
    _, weighting, _ = rows_of(small[...], cases)
    first_resid, resid = small[:cases], state[:cases]
    steps = state[cases : 2 * cases, : 2 * cases]
    scale = first_sums[cases : cases + 1, :1]
    total = jnp.concatenate(join_sums(place, mine, other), axis=0)
    along = jnp.concatenate(
        [
            jnp.concatenate([jnp.zeros((cases, cases), jnp.float32), total[:cases, :cases]], axis=1),
            total[:cases],
        ],
        axis=0,
    )
    conjugating = times(gram_inverse[...], along)
    taken = times(along.T, conjugating)
    gram00 = total[cases : 2 * cases, :cases]
    _, _, _, next0, next1 = solve_halves(
        gram00 - taken[:cases, :cases],
        total[cases : 2 * cases, cases:] - taken[:cases, cases:],
        total[2 * cases :, cases:] - taken[cases:, cases:],
        total[2 * cases :, :cases],
        scale * gram00,
    )
    next_steps = jnp.concatenate([next0, next1], axis=0)
    old_steps = -times(conjugating, next_steps).T
    next_steps = next_steps.T
    next_image1 = out1[...] + 0.5 * read_faces(place, (x0, x1, y0, y1))
    images = jnp.concatenate(
        [image0[...], image1[...], next_image0[...], next_image1], axis=0
    )
    resid = resid - times(jnp.concatenate([old_steps, next_steps], axis=1), images)
    fields = weighting * jnp.concatenate(
        [first_resid, scale * image0[...], state[:cases], scale * next_image0[...]], axis=0
    )
    answer = times(jnp.concatenate([steps + old_steps, next_steps], axis=1), fields)
    both = exact_pick(jnp.concatenate([answer, resid], axis=0), pick[...])
    solution_out[...] = both[:cases]
    resid_out[...] = both[cases:]


def call(kernel, name, outs, *operands, scratch=(), mebibytes=24, smem=1, flops=0):
    shapes = [
        jax.ShapeDtypeStruct(one[0], one[1]) if isinstance(one[0], tuple)
        else jax.ShapeDtypeStruct(one, jnp.float32)
        for one in outs
    ]
    return pl.pallas_call(
        kernel,
        out_shape=shapes,
        in_specs=[SMEM] * smem + [VMEM] * (len(operands) - smem),
        out_specs=[VMEM] * len(shapes),
        scratch_shapes=list(scratch),
        compiler_params=pltpu.CompilerParams(vmem_limit_bytes=mebibytes * 2**20),
        cost_estimate=pl.CostEstimate(flops=flops, bytes_accessed=2**20, transcendentals=0),
        name=name,
    )(*operands)


def swap_pairs(rows, columns, along, parity):
    pairs = []
    for x in range(rows):
        for y in range(columns):
            index, count = (x, rows) if along == "gx" else (y, columns)
            other = index + 1 if index % 2 == parity else index - 1
            if 0 <= other < count:
                target = (other, y) if along == "gx" else (x, other)
            else:
                target = (x, y ^ 1) if along == "gx" else (x ^ 1, y)
                if not (target[0] < rows and target[1] < columns):
                    target = (x, y)
            pairs.append((x * columns + y, target[0] * columns + target[1]))
    return pairs


def swap_faces(sends, axes=("gx", "gy")):
    rows, columns = lax.axis_size("gx"), lax.axis_size("gy")
    order = [(along, parity) for along in axes for parity in (0, 1)]
    return [
        lax.ppermute(send, ("gx", "gy"), swap_pairs(rows, columns, along, parity))
        for send, (along, parity) in zip(sends, order)
    ]


def stage_masks(axis, first):
    count = lax.axis_size(axis)
    stages = []
    step = first
    while step < count:
        last = step * 2 >= count
        stages.append((axis, (step,) if last else (step, 2 * step, 3 * step)))
        step *= 4
    return stages


def from_mask(value, axis, mask):
    count = lax.axis_size(axis)
    return lax.ppermute(value, axis, [(source, source ^ mask) for source in range(count)])


def sum_over_devices(keep, send, add, sends, work=None, inputs=()):
    value = add([keep, from_mask(send, "gy", 1)])
    beside = {"gy": ("gx", sends[:2]), "gx": ("gy", sends[2:])}
    received, done = {}, ()
    for axis, masks in stage_masks("gy", 2) + stage_masks("gx", 1):
        along, pair = beside.pop(axis, (None, ()))
        if pair:
            value, inputs, pair = lax.optimization_barrier((value, inputs, pair))
        parts = [value] + [from_mask(value, axis, mask) for mask in masks]
        if pair:
            received[along] = swap_faces(pair, (along,))
        if work is not None:
            done, work = work(*inputs), None
        value = add(parts)
        if pair:
            value, done, received[along] = lax.optimization_barrier(
                (value, done, received[along])
            )
    for along, pair in beside.values():
        received[along] = swap_faces(pair, (along,))
    if work is not None:
        done = work(*inputs)
    return value, from_mask(value, "gy", 1), received["gx"] + received["gy"], done


def plain(parts):
    value = parts[0] + parts[1]
    return value + (parts[2] + parts[3]) if len(parts) == 4 else value


def rescaled(parts):
    cases = parts[0].shape[0] - PAD
    scales = [part[cases:] for part in parts]
    scale = functools.reduce(jnp.minimum, scales)
    lane = lax.broadcasted_iota(jnp.int32, (cases, 2 * cases), 1)
    even = lax.axis_index("gy") % 2 == 0
    ready = []
    for part, own in zip(parts, scales):
        ratio = jnp.where(even, 1.0, (scale / own)[:1])
        ready.append(part[:cases] * jnp.where(lane < cases, ratio, ratio * ratio))
    return jnp.concatenate([plain(ready), scale], axis=0)


def local(right_side, weights, signs, face_map, pattern, factor):
    cases, size = right_side.shape[1:]
    blocks = pattern.shape[1]
    place = jnp.stack(
        [
            lax.axis_index("gx"),
            lax.axis_index("gy"),
            jnp.int32(lax.axis_size("gx")),
            jnp.int32(lax.axis_size("gy")),
        ]
    )
    field, padded = (cases, size), (cases + PAD, size)
    face, padded_face = (cases, size // 4), (cases + PAD, size // 4)
    half_type = ((size, size), jnp.bfloat16)

    work = 6 * cases * size * size
    small, *sends = call(
        start_kernel, "start_fields", [padded] + [padded_face] * 4,
        place, right_side[0], weights, signs, face_map, flops=20 * work,
    )
    received = swap_faces(sends)
    high, low = call(
        functools.partial(factor_kernel, blocks), "masked_factor", [half_type] * 2,
        pattern[0], factor[0], face_map,
        scratch=[pltpu.VMEM((size, size), jnp.bfloat16)] * 2,
        smem=0, flops=4 * size**3,
    )
    ghosts, half0, out0, *sends = call(
        first_kernel, "first_operator", [padded, field, field] + [face] * 4,
        place, small, *received, high, low, flops=2 * work,
    )
    received = swap_faces(sends)
    image0, ghost_image0, second, keep, send = call(
        gram_kernel, "first_gram", [field, field, padded] + [(cases + PAD, 2 * cases)] * 2,
        place, small, ghosts, half0, out0, *received, high, low, flops=2 * work,
    )
    out1, *sends = call(
        lift_kernel, "second_operator", [field] + [padded_face] * 4,
        place, small, second, high, low, flops=work,
    )
    mine, other, faces, _ = sum_over_devices(keep, send, rescaled, sends)
    state, inverse, image1, next_half0, next_out0, *next_sends = call(
        step_kernel, "first_step",
        [(2 * cases, size), (2 * cases, 2 * cases), field, field, field] + [face] * 4,
        place, small, ghosts, mine, other, image0, ghost_image0, second, out1,
        *faces, high, low, flops=4 * work,
    )
    faces = swap_faces(next_sends)
    next_image0, next_half1, keep, send = call(
        next_gram_kernel, "second_gram", [field, field] + [(3 * cases // 2, 2 * cases)] * 2,
        place, small, ghosts, mine, second, state, next_half0, next_out0, *faces, high, low,
        flops=2 * work,
    )
    next_out1, *sends = call(
        next_lift_kernel, "last_operator", [field] + [face] * 4,
        place, small, next_half1, high, low, flops=work,
    )

    def prepare(small, inverse):
        return call(
            functools.partial(prepare_kernel, cases), "prepare_last",
            [half_type, (2 * cases, 2 * cases)], small, inverse, smem=0, flops=work,
        )

    next_mine, next_other, faces, (pick, gram_inverse) = sum_over_devices(
        keep, send, plain, sends, prepare, (small, inverse)
    )
    answer, resid = call(
        last_kernel, "last_step", [field, field],
        place, small, mine, next_mine, next_other, state, gram_inverse, image0, image1,
        next_image0, next_out1, *faces, pick, flops=4 * work,
    )
    return (answer[None], resid[None])


def solution(mesh):
    return jax.shard_map(
        local,
        mesh=mesh,
        in_specs=(
            P("gx", None, "gy"),
            P("gx", "gy"),
            P("gx", "gy"),
            P("gx", "gy"),
            P("gx", None, "gy"),
            P("gx", None, "gy"),
        ),
        out_specs=(P("gx", None, "gy"), P("gx", None, "gy")),
        check_vma=False,
    )
```

```python
import functools

import jax
import jax.numpy as jnp
from jax import lax
from jax.experimental import pallas as pl
from jax.experimental.pallas import tpu as pltpu
from jax.sharding import PartitionSpec as P

HIGH = lax.Precision.HIGHEST
VMEM = pl.BlockSpec(memory_space=pltpu.VMEM)
SMEM = pl.BlockSpec(memory_space=pltpu.SMEM)
PAD = 8
SMALL = 4e-4
LANES = 128


def halves(value):
    high = value.astype(jnp.bfloat16)
    low = (value - high.astype(jnp.float32)).astype(jnp.bfloat16)
    return high, low


def thirds(value):
    high = value.astype(jnp.bfloat16)
    rest = value - high.astype(jnp.float32)
    middle = rest.astype(jnp.bfloat16)
    low = (rest - middle.astype(jnp.float32)).astype(jnp.bfloat16)
    return jnp.concatenate([high, middle, low], axis=0)


def bf16_dot(left, right, right_dim):
    return lax.dot_general(
        left, right, (((1,), (right_dim,)), ((), ())), preferred_element_type=jnp.float32
    )


def exact_pick(value, pick):
    rows = value.shape[0]
    parts = bf16_dot(thirds(value), pick, 0)
    return parts[:rows] + (parts[rows : 2 * rows] + parts[2 * rows :])


def product(value, high, low, dim):
    rows = value.shape[0]
    value_high, value_low = halves(value)
    both = bf16_dot(jnp.concatenate([value_high, value_low], axis=0), high[...], dim)
    return both[:rows] + (both[rows:] + bf16_dot(value_high, low[...], dim))


def inner_prod(left, right):
    return lax.dot_general(
        left, right, (((1,), (1,)), ((), ())), precision=HIGH, preferred_element_type=jnp.float32
    )


def times(left, right):
    return jnp.dot(left, right, precision=HIGH, preferred_element_type=jnp.float32)


def row_to_square(row, size):
    return jnp.broadcast_to(row, (LANES, size)).T


def pick_columns(face_row):
    size = face_row.shape[1]
    unknown = lax.broadcasted_iota(jnp.int32, (size, size), 0)
    return jnp.where(unknown == face_row, 1.0, 0.0).astype(jnp.bfloat16)


def pick_rows(face_row):
    size = face_row.shape[1]
    face = row_to_square(face_row, size)
    lane = lax.broadcasted_iota(jnp.int32, (size, LANES), 1)
    return jnp.concatenate(
        [
            jnp.where(face == lane + start, 1.0, 0.0).astype(jnp.bfloat16)
            for start in range(0, size, LANES)
        ],
        axis=1,
    )


def faces_of(field):
    face_len = field.shape[1] // 4
    return [field[:, face * face_len : (face + 1) * face_len] for face in range(4)]


def write_faces(place, field, outs):
    north, south, west, east = faces_of(field)
    even_x, even_y = place[0] % 2 == 0, place[1] % 2 == 0
    outs[0][...] = jnp.where(even_x, south, north)
    outs[1][...] = jnp.where(even_x, north, south)
    outs[2][...] = jnp.where(even_y, east, west)
    outs[3][...] = jnp.where(even_y, west, east)


def read_faces(place, received):
    x_first, x_second, y_first, y_second = [one[...] for one in received]
    even_x, even_y = place[0] % 2 == 0, place[1] % 2 == 0
    north = jnp.where(place[0] > 0, jnp.where(even_x, x_second, x_first), 0.0)
    south = jnp.where(place[0] + 1 < place[2], jnp.where(even_x, x_first, x_second), 0.0)
    west = jnp.where(place[1] > 0, jnp.where(even_y, y_second, y_first), 0.0)
    east = jnp.where(place[1] + 1 < place[3], jnp.where(even_y, y_first, y_second), 0.0)
    return jnp.concatenate([north, south, west, east], axis=1)


def rows_of(small, cases):
    return small[:cases], small[cases : cases + 1], small[cases + 1 : cases + 2]


def images_of(out, signed_ghost, jump, ghost_jump):
    image = out + 0.5 * signed_ghost
    ghost = ghost_jump * signed_ghost + (0.5 * jump * jnp.abs(ghost_jump)) * out
    return image, ghost


def inverse_of(matrix):
    size = matrix.shape[0]
    eye = lax.broadcasted_iota(jnp.int32, matrix.shape, 0) == lax.broadcasted_iota(
        jnp.int32, matrix.shape, 1
    )
    diagonal = jnp.where(eye, matrix, 0.0)
    by_row = lax.rsqrt(jnp.sum(diagonal, axis=1, keepdims=True))
    by_column = lax.rsqrt(jnp.sum(diagonal, axis=0, keepdims=True))
    scaled = matrix * by_row * by_column
    bound = jnp.max(jnp.sum(jnp.abs(scaled), axis=0, keepdims=True), axis=1, keepdims=True)
    one = jnp.where(eye, 1.0, 0.0)

    def again(state):
        _, before, now, count = state
        return (count < 2) | ((now > SMALL) & ((now < before) | (now > 1.0)) & (count < 64))

    def better(state):
        x, _, now, count = state
        left = one - times(scaled, x)
        norm = jnp.sum(left * left)
        nearer = x + times(x, left)
        return nearer + times(nearer, times(left, left)), now, norm, count + 1

    start = one * (1.0 / bound)
    x, _, _, _ = lax.while_loop(
        again, better, (start, jnp.float32(size), jnp.float32(size), jnp.int32(0))
    )
    return x * by_row * by_column


def solve_halves(a00, a01, a11, b0, b1):
    size = a00.shape[0]
    first = inverse_of(a00)
    both = times(first, jnp.concatenate([a01, b0], axis=1))
    along, part = both[:, :size], both[:, size:]
    taken = times(a01.T, both)
    second = inverse_of(a11 - taken[:, :size])
    x1 = times(second, b1 - taken[:, size:])
    return first, along, second, part - times(along, x1), x1


def start_kernel(place, packed, small, *sends):
    value = packed[...]
    size = value.shape[1]
    cases = value.shape[0] - PAD
    faces = value[cases + 2 : cases + 3]
    value = exact_pick(value, pick_columns(faces.astype(jnp.int32)))
    write_faces(place, value, sends)
    small[...] = value
    small[cases + 2 : cases + 3] = faces


def face_row(small, cases):
    return small[cases + 2 : cases + 3].astype(jnp.int32)


def factor_kernel(blocks, pattern, factor, faces, high, low, masked_high, masked_low):
    size = factor.shape[0]
    length = size // blocks
    for i in range(blocks):
        for j in range(blocks):
            rows, columns = pl.ds(i * length, length), pl.ds(j * length, length)
            value = factor[rows, columns]
            if i != j:
                keep = jnp.broadcast_to(pattern[i : i + 1, j : j + 1], value.shape)
                value = jnp.where(keep == 1, value, 0.0)
            masked_high[rows, columns], masked_low[rows, columns] = halves(value)
    pick = pick_rows(faces[...])
    chunk = size // 4
    for masked, out in ((masked_high, high), (masked_low, low)):
        for start in range(0, size, chunk):
            out[start : start + chunk] = bf16_dot(
                pick[start : start + chunk], masked[...], 0
            ).astype(jnp.bfloat16)


def prepare_kernel(cases, small, inverse, pick, gram_inverse):
    pick[...] = pick_rows(face_row(small, cases))
    first, second = inverse[:cases], inverse[cases:]
    beside, lower = first[:, cases:], second[:, :cases]
    corner = -times(beside, lower)
    gram_inverse[:cases, :cases] = first[:, :cases] - times(corner, beside.T)
    gram_inverse[:cases, cases:] = corner
    gram_inverse[cases:, :cases] = corner.T
    gram_inverse[cases:, cases:] = lower


def split_sums(place, first, second, more, keep, send):
    even = place[1] % 2 == 0
    rows = first.shape[0]
    keep[:rows] = jnp.where(even, first, second)
    send[:rows] = jnp.where(even, second, first)
    if more is not None:
        keep[rows:] = more
        send[rows:] = more


def join_sums(place, mine, other):
    even = place[1] % 2 == 0
    mine, other = mine[...], other[...]
    return jnp.where(even, mine, other), jnp.where(even, other, mine)


def first_kernel(place, small, x0, x1, y0, y1, high, low, ghosts, half, out, *sends):
    value, ghost = small[...], read_faces(place, (x0, x1, y0, y1))
    ghosts[...] = ghost
    cases = half.shape[0]
    resid, weighting, jump = rows_of(value, cases)
    ghost_resid, ghost_weighting, _ = rows_of(ghost, cases)
    field = weighting * resid + (0.5 * jump) * (ghost_weighting * ghost_resid)
    halfway = product(field, high, low, 0)
    half[...] = halfway
    lifted = product(halfway, high, low, 1)
    out[...] = lifted
    write_faces(place, jump * lifted, sends)


def gram_kernel(
    place, small, ghosts, half, out, x0, x1, y0, y1, high, low, image, ghost_image, second, keep, send
):
    cases = half.shape[0]
    resid, weighting, jump = rows_of(small[...], cases)
    _, ghost_weighting, ghost_jump = rows_of(ghosts[...], cases)
    own, ghost = images_of(out[...], read_faces(place, (x0, x1, y0, y1)), jump, ghost_jump)
    image[...] = own
    ghost_image[...] = ghost
    field = weighting * own + (0.5 * jump) * (ghost_weighting * ghost)
    largest = jnp.max(jnp.max(jnp.abs(field), axis=1, keepdims=True), axis=0, keepdims=True)
    scale = 1.0 / jnp.maximum(largest, 1e-30)
    second_half = product(field * scale, high, low, 0)
    second[:cases] = second_half
    second[cases:] = jnp.broadcast_to(scale, (PAD, field.shape[1]))
    first_half = half[...]
    cross = inner_prod(second_half, jnp.concatenate([first_half, second_half], axis=0))
    split_sums(
        place,
        jnp.concatenate(
            [inner_prod(first_half, first_half), inner_prod(weighting * resid, resid)], axis=1
        ),
        jnp.concatenate([cross[:, :cases].T, cross[:, cases:]], axis=1),
        jnp.broadcast_to(scale, (PAD, 2 * cases)),
        keep,
        send,
    )


def lift_kernel(place, small, second, high, low, out, *sends):
    cases = out.shape[0]
    jump = small[cases + 1 : cases + 2]
    lifted = product(second[:cases], high, low, 1)
    out[...] = lifted
    write_faces(place, jnp.concatenate([jump * lifted, second[cases:]], axis=0), sends)


def step_kernel(
    place, small, ghosts, mine, other, image0, ghost_image0, second, out1, x0, x1, y0, y1, high, low,
    state, inverse, image1, half, out, *sends
):
    cases = half.shape[0]
    resid, weighting, jump = rows_of(small[...], cases)
    ghost_resid, ghost_weighting, ghost_jump = rows_of(ghosts[...], cases)
    scale = mine[cases : cases + 1, :1]
    top, bottom = join_sums(place, mine, other)
    gram00, gram01, gram11 = top[:cases, :cases], bottom[:cases, :cases], bottom[:cases, cases:]
    first, along, corner, steps0, steps1 = solve_halves(
        gram00, gram01, gram11, top[:cases, cases:], scale * gram00
    )
    inverse[:cases, :cases] = first
    inverse[:cases, cases:] = along
    inverse[cases:, :cases] = corner
    inverse[cases:, cases:] = corner
    steps = jnp.concatenate([steps0, steps1], axis=0).T
    received = read_faces(place, (x0, x1, y0, y1))
    own_ratio = scale / second[cases : cases + 1]
    there = received[cases : cases + 1]
    ghost_ratio = jnp.where(there > 0.0, scale / jnp.where(there > 0.0, there, 1.0), 0.0)
    own1, ghost1 = images_of(
        out1[...] * own_ratio, received[:cases] * ghost_ratio, jump, ghost_jump
    )
    image1[...] = own1
    resid = resid - times(steps, jnp.concatenate([image0[...], own1], axis=0))
    ghost_resid = ghost_resid - times(
        steps, jnp.concatenate([ghost_image0[...], ghost1], axis=0)
    )
    state[:cases] = resid
    state[cases : 2 * cases, : 2 * cases] = steps
    field = weighting * resid + (0.5 * jump) * (ghost_weighting * ghost_resid)
    halfway = product(field, high, low, 0)
    half[...] = halfway
    lifted = product(halfway, high, low, 1)
    out[...] = lifted
    write_faces(place, jump * lifted, sends)


def next_gram_kernel(
    place, small, ghosts, mine, second, state, half, out, x0, x1, y0, y1, high, low,
    image, next_half, keep, send
):
    cases = half.shape[0]
    _, weighting, jump = rows_of(small[...], cases)
    _, ghost_weighting, ghost_jump = rows_of(ghosts[...], cases)
    scale = mine[cases : cases + 1, :1]
    own, ghost = images_of(out[...], read_faces(place, (x0, x1, y0, y1)), jump, ghost_jump)
    image[...] = own
    field = scale * (weighting * own + (0.5 * jump) * (ghost_weighting * ghost))
    halfway = product(field, high, low, 0)
    next_half[...] = halfway
    before = second[:cases] * (scale / second[cases : cases + 1])
    both = jnp.concatenate([half[...], halfway], axis=0)
    cross = inner_prod(jnp.concatenate([before, both], axis=0), both)
    resid = state[:cases]
    total = jnp.concatenate(
        [
            cross[: 2 * cases],
            jnp.concatenate(
                [inner_prod(weighting * resid, resid), cross[2 * cases :, cases:]], axis=1
            ),
        ],
        axis=0,
    )
    middle = total.shape[0] // 2
    split_sums(place, total[:middle], total[middle:], None, keep, send)


def next_lift_kernel(place, small, half, high, low, out, *sends):
    cases = out.shape[0]
    lifted = product(half[...], high, low, 1)
    out[...] = lifted
    write_faces(place, small[cases + 1 : cases + 2] * lifted, sends)


def last_kernel(
    place, small, first_sums, mine, other, state, gram_inverse, image0, image1, next_image0, out1,
    x0, x1, y0, y1, pick, solution_out, resid_out
):
    cases = image0.shape[0]
    _, weighting, _ = rows_of(small[...], cases)
    first_resid, resid = small[:cases], state[:cases]
    steps = state[cases : 2 * cases, : 2 * cases]
    scale = first_sums[cases : cases + 1, :1]
    total = jnp.concatenate(join_sums(place, mine, other), axis=0)
    along = jnp.concatenate(
        [
            jnp.concatenate([jnp.zeros((cases, cases), jnp.float32), total[:cases, :cases]], axis=1),
            total[:cases],
        ],
        axis=0,
    )
    conjugating = times(gram_inverse[...], along)
    taken = times(along.T, conjugating)
    gram00 = total[cases : 2 * cases, :cases]
    _, _, _, next0, next1 = solve_halves(
        gram00 - taken[:cases, :cases],
        total[cases : 2 * cases, cases:] - taken[:cases, cases:],
        total[2 * cases :, cases:] - taken[cases:, cases:],
        total[2 * cases :, :cases],
        scale * gram00,
    )
    next_steps = jnp.concatenate([next0, next1], axis=0)
    old_steps = -times(conjugating, next_steps).T
    next_steps = next_steps.T
    next_image1 = out1[...] + 0.5 * read_faces(place, (x0, x1, y0, y1))
    images = jnp.concatenate(
        [image0[...], image1[...], next_image0[...], next_image1], axis=0
    )
    resid = resid - times(jnp.concatenate([old_steps, next_steps], axis=1), images)
    fields = weighting * jnp.concatenate(
        [first_resid, scale * image0[...], state[:cases], scale * next_image0[...]], axis=0
    )
    answer = times(jnp.concatenate([steps + old_steps, next_steps], axis=1), fields)
    both = exact_pick(jnp.concatenate([answer, resid], axis=0), pick[...])
    solution_out[...] = both[:cases]
    resid_out[...] = both[cases:]


def call(kernel, name, outs, *operands, scratch=(), mebibytes=24, smem=1, flops=0):
    shapes = [
        jax.ShapeDtypeStruct(one[0], one[1]) if isinstance(one[0], tuple)
        else jax.ShapeDtypeStruct(one, jnp.float32)
        for one in outs
    ]
    touched = sum(one.size * one.dtype.itemsize for one in (*operands, *shapes))
    return pl.pallas_call(
        kernel,
        out_shape=shapes,
        in_specs=[SMEM] * smem + [VMEM] * (len(operands) - smem),
        out_specs=[VMEM] * len(shapes),
        scratch_shapes=list(scratch),
        compiler_params=pltpu.CompilerParams(vmem_limit_bytes=mebibytes * 2**20),
        cost_estimate=pl.CostEstimate(flops=flops, bytes_accessed=touched, transcendentals=0),
        name=name,
    )(*operands)


def swap_pairs(rows, columns, along, parity):
    pairs = []
    for x in range(rows):
        for y in range(columns):
            index, count = (x, rows) if along == "gx" else (y, columns)
            other = index + 1 if index % 2 == parity else index - 1
            if 0 <= other < count:
                target = (other, y) if along == "gx" else (x, other)
            else:
                target = (x, y ^ 1) if along == "gx" else (x ^ 1, y)
                if not (target[0] < rows and target[1] < columns):
                    target = (x, y)
            pairs.append((x * columns + y, target[0] * columns + target[1]))
    return pairs


def swap_faces(sends, axes=("gx", "gy")):
    rows, columns = lax.axis_size("gx"), lax.axis_size("gy")
    order = [(along, parity) for along in axes for parity in (0, 1)]
    return [
        lax.ppermute(send, ("gx", "gy"), swap_pairs(rows, columns, along, parity))
        for send, (along, parity) in zip(sends, order)
    ]


def stage_masks(axis, first):
    count = lax.axis_size(axis)
    stages = []
    step = first
    while step < count:
        last = step * 2 >= count
        stages.append((axis, (step,) if last else (step, 2 * step, 3 * step)))
        step *= 4
    return stages


def from_mask(value, axis, mask):
    count = lax.axis_size(axis)
    return lax.ppermute(value, axis, [(source, source ^ mask) for source in range(count)])


def sum_over_devices(keep, send, add, work, inputs):
    value = add([keep, from_mask(send, "gy", 1)])
    stages = stage_masks("gy", 2) + stage_masks("gx", 1)
    done, sends, received = (), (), []
    for index, (axis, masks) in enumerate(stages):
        value, inputs, sends = lax.optimization_barrier((value, inputs, sends))
        parts = [value] + [from_mask(value, axis, mask) for mask in masks]
        if index == 0:
            done, sends = work(*inputs)
        if index == len(stages) - 1:
            received = swap_faces(sends)
        value = add(parts)
        value, done, sends = lax.optimization_barrier((value, done, sends))
    return value, from_mask(value, "gy", 1), received, done


def plain(parts):
    value = parts[0] + parts[1]
    return value + (parts[2] + parts[3]) if len(parts) == 4 else value


def rescaled(parts):
    cases = parts[0].shape[0] - PAD
    scales = [part[cases:] for part in parts]
    scale = functools.reduce(jnp.minimum, scales)
    lane = lax.broadcasted_iota(jnp.int32, (cases, 2 * cases), 1)
    even = lax.axis_index("gy") % 2 == 0
    ready = []
    for part, own in zip(parts, scales):
        ratio = jnp.where(even, 1.0, (scale / own)[:1])
        ready.append(part[:cases] * jnp.where(lane < cases, ratio, ratio * ratio))
    return jnp.concatenate([plain(ready), scale], axis=0)


def local(right_side, weights, signs, face_map, pattern, factor):
    cases, size = right_side.shape[1:]
    blocks = pattern.shape[1]
    place = jnp.stack(
        [
            lax.axis_index("gx"),
            lax.axis_index("gy"),
            jnp.int32(lax.axis_size("gx")),
            jnp.int32(lax.axis_size("gy")),
        ]
    )
    field, padded = (cases, size), (cases + PAD, size)
    face, padded_face = (cases, size // 4), (cases + PAD, size // 4)
    half_type = ((size, size), jnp.bfloat16)

    work = 6 * cases * size * size
    packed = jnp.concatenate(
        [
            right_side[0],
            weights,
            (2 * signs - 1).astype(jnp.float32),
            face_map.astype(jnp.float32),
            jnp.zeros((PAD - 3, size), jnp.float32),
        ],
        axis=0,
    )
    small, *sends = call(
        start_kernel, "start_fields", [padded] + [padded_face] * 4, place, packed,
        flops=20 * work,
    )
    received = swap_faces(sends)
    high, low = call(
        functools.partial(factor_kernel, blocks), "masked_factor", [half_type] * 2,
        pattern[0], factor[0], face_map,
        scratch=[pltpu.VMEM((size, size), jnp.bfloat16)] * 2,
        smem=0, flops=4 * size**3,
    )
    ghosts, half0, out0, *sends = call(
        first_kernel, "first_operator", [padded, field, field] + [face] * 4,
        place, small, *received, high, low, flops=2 * work,
    )
    received = swap_faces(sends)
    image0, ghost_image0, second, keep, send = call(
        gram_kernel, "first_gram", [field, field, padded] + [(cases + PAD, 2 * cases)] * 2,
        place, small, ghosts, half0, out0, *received, high, low, flops=2 * work,
    )

    def lift(small, second, high, low):
        out, *sends = call(
            lift_kernel, "second_operator", [field] + [padded_face] * 4,
            place, small, second, high, low, flops=work,
        )
        return out, sends

    mine, other, faces, out1 = sum_over_devices(
        keep, send, rescaled, lift, (small, second, high, low)
    )
    state, inverse, image1, next_half0, next_out0, *next_sends = call(
        step_kernel, "first_step",
        [(2 * cases, size), (2 * cases, 2 * cases), field, field, field] + [face] * 4,
        place, small, ghosts, mine, other, image0, ghost_image0, second, out1,
        *faces, high, low, flops=4 * work,
    )
    faces = swap_faces(next_sends)
    next_image0, next_half1, keep, send = call(
        next_gram_kernel, "second_gram", [field, field] + [(3 * cases // 2, 2 * cases)] * 2,
        place, small, ghosts, mine, second, state, next_half0, next_out0, *faces, high, low,
        flops=2 * work,
    )

    def prepare(small, inverse, half, high, low):
        pick, gram_inverse = call(
            functools.partial(prepare_kernel, cases), "prepare_last",
            [half_type, (2 * cases, 2 * cases)], small, inverse, smem=0, flops=work,
        )
        out, *sends = call(
            next_lift_kernel, "last_operator", [field] + [face] * 4,
            place, small, half, high, low, flops=work,
        )
        return (pick, gram_inverse, out), sends

    next_mine, next_other, faces, (pick, gram_inverse, next_out1) = sum_over_devices(
        keep, send, plain, prepare, (small, inverse, next_half1, high, low)
    )
    answer, resid = call(
        last_kernel, "last_step", [field, field],
        place, small, mine, next_mine, next_other, state, gram_inverse, image0, image1,
        next_image0, next_out1, *faces, pick, flops=4 * work,
    )
    return (answer[None], resid[None])


def solution(mesh):
    return jax.shard_map(
        local,
        mesh=mesh,
        in_specs=(
            P("gx", None, "gy"),
            P("gx", "gy"),
            P("gx", "gy"),
            P("gx", "gy"),
            P("gx", None, "gy"),
            P("gx", None, "gy"),
        ),
        out_specs=(P("gx", None, "gy"), P("gx", None, "gy")),
        check_vma=False,
    )
```

```python
import functools

import jax
import jax.numpy as jnp
from jax import lax
from jax.experimental import pallas as pl
from jax.experimental.pallas import tpu as pltpu
from jax.sharding import PartitionSpec as P

HIGH = lax.Precision.HIGHEST
VMEM = pl.BlockSpec(memory_space=pltpu.VMEM)
SMEM = pl.BlockSpec(memory_space=pltpu.SMEM)
PAD = 8
SMALL = 1e-6
LANES = 128


def halves(value):
    high = value.astype(jnp.bfloat16)
    low = (value - high.astype(jnp.float32)).astype(jnp.bfloat16)
    return high, low


def thirds(value):
    high = value.astype(jnp.bfloat16)
    rest = value - high.astype(jnp.float32)
    middle = rest.astype(jnp.bfloat16)
    low = (rest - middle.astype(jnp.float32)).astype(jnp.bfloat16)
    return jnp.concatenate([high, middle, low], axis=0)


def bf16_dot(left, right, right_dim):
    return lax.dot_general(
        left, right, (((1,), (right_dim,)), ((), ())), preferred_element_type=jnp.float32
    )


def exact_pick(value, pick):
    rows = value.shape[0]
    parts = bf16_dot(thirds(value), pick, 0)
    return parts[:rows] + (parts[rows : 2 * rows] + parts[2 * rows :])


def product(value, high, low, dim):
    rows = value.shape[0]
    value_high, value_low = halves(value)
    both = bf16_dot(jnp.concatenate([value_high, value_low], axis=0), high[...], dim)
    return both[:rows] + (both[rows:] + bf16_dot(value_high, low[...], dim))


def inner_prod(left, right):
    return lax.dot_general(
        left, right, (((1,), (1,)), ((), ())), precision=HIGH, preferred_element_type=jnp.float32
    )


def times(left, right):
    return jnp.dot(left, right, precision=HIGH, preferred_element_type=jnp.float32)


def row_to_square(row, size):
    return jnp.broadcast_to(row, (LANES, size)).T


def pick_columns(face_row):
    size = face_row.shape[1]
    unknown = lax.broadcasted_iota(jnp.int32, (size, size), 0)
    return jnp.where(unknown == face_row, 1.0, 0.0).astype(jnp.bfloat16)


def pick_rows(face_row):
    size = face_row.shape[1]
    face = row_to_square(face_row, size)
    lane = lax.broadcasted_iota(jnp.int32, (size, LANES), 1)
    return jnp.concatenate(
        [
            jnp.where(face == lane + start, 1.0, 0.0).astype(jnp.bfloat16)
            for start in range(0, size, LANES)
        ],
        axis=1,
    )


def faces_of(field):
    face_len = field.shape[1] // 4
    return [field[:, face * face_len : (face + 1) * face_len] for face in range(4)]


def write_faces(place, field, outs):
    north, south, west, east = faces_of(field)
    even_x, even_y = place[0] % 2 == 0, place[1] % 2 == 0
    outs[0][...] = jnp.where(even_x, south, north)
    outs[1][...] = jnp.where(even_x, north, south)
    outs[2][...] = jnp.where(even_y, east, west)
    outs[3][...] = jnp.where(even_y, west, east)


def read_faces(place, received):
    x_first, x_second, y_first, y_second = [one[...] for one in received]
    even_x, even_y = place[0] % 2 == 0, place[1] % 2 == 0
    north = jnp.where(place[0] > 0, jnp.where(even_x, x_second, x_first), 0.0)
    south = jnp.where(place[0] + 1 < place[2], jnp.where(even_x, x_first, x_second), 0.0)
    west = jnp.where(place[1] > 0, jnp.where(even_y, y_second, y_first), 0.0)
    east = jnp.where(place[1] + 1 < place[3], jnp.where(even_y, y_first, y_second), 0.0)
    return jnp.concatenate([north, south, west, east], axis=1)


def rows_of(small, cases):
    return small[:cases], small[cases : cases + 1], small[cases + 1 : cases + 2]


def images_of(out, signed_ghost, jump, ghost_jump):
    image = out + 0.5 * signed_ghost
    ghost = ghost_jump * signed_ghost + (0.5 * jump * jnp.abs(ghost_jump)) * out
    return image, ghost


def inverse_of(matrix):
    size = matrix.shape[0]
    eye = lax.broadcasted_iota(jnp.int32, matrix.shape, 0) == lax.broadcasted_iota(
        jnp.int32, matrix.shape, 1
    )
    diagonal = jnp.where(eye, matrix, 0.0)
    by_row = lax.rsqrt(jnp.sum(diagonal, axis=1, keepdims=True))
    by_column = lax.rsqrt(jnp.sum(diagonal, axis=0, keepdims=True))
    scaled = matrix * by_row * by_column
    bound = jnp.max(jnp.sum(jnp.abs(scaled), axis=0, keepdims=True), axis=1, keepdims=True)
    square = jnp.sum(jnp.sum(scaled * scaled, axis=0, keepdims=True), axis=1, keepdims=True)
    one = jnp.where(eye, 1.0, 0.0)

    def again(state):
        _, before, now, count = state
        return (now > SMALL) & ((now < before) | (now > 1.0)) & (count < 64)

    def better(state):
        x, _, now, count = state
        left = one - times(scaled, x)
        twice = times(left, left)
        nearer = x + times(x, left)
        return nearer + times(nearer, twice), now, jnp.sum(twice * twice), count + 1

    start = one * jnp.minimum(size / square, 1.9 / bound)
    large = jnp.float32(4 * size)
    x, _, _, _ = lax.while_loop(again, better, (start, large, large, jnp.int32(0)))
    return x * by_row * by_column


def solve_halves(a00, a01, a11, b0, b1):
    size = a00.shape[0]
    first = inverse_of(a00)
    both = times(first, jnp.concatenate([a01, b0], axis=1))
    along, part = both[:, :size], both[:, size:]
    taken = times(a01.T, both)
    second = inverse_of(a11 - taken[:, :size])
    x1 = times(second, b1 - taken[:, size:])
    return first, along, second, part - times(along, x1), x1


def start_kernel(place, loads, rows, small, *sends):
    cases = loads.shape[0]
    faces = rows[2:3]
    value = exact_pick(
        jnp.concatenate([loads[...], rows[...]], axis=0), pick_columns(faces.astype(jnp.int32))
    )
    write_faces(place, value, sends)
    small[...] = value
    small[cases + 2 : cases + 3] = faces


def face_row(small, cases):
    return small[cases + 2 : cases + 3].astype(jnp.int32)


def factor_kernel(blocks, pattern, factor, faces, high, low, masked_high, masked_low):
    size = factor.shape[0]
    length = size // blocks
    for i in range(blocks):
        for j in range(blocks):
            rows, columns = pl.ds(i * length, length), pl.ds(j * length, length)
            value = factor[rows, columns]
            if i != j:
                keep = jnp.broadcast_to(pattern[i : i + 1, j : j + 1], value.shape)
                value = jnp.where(keep == 1, value, 0.0)
            masked_high[rows, columns], masked_low[rows, columns] = halves(value)
    pick = pick_rows(faces[...])
    chunk = size // 4
    for masked, out in ((masked_high, high), (masked_low, low)):
        for start in range(0, size, chunk):
            out[start : start + chunk] = bf16_dot(
                pick[start : start + chunk], masked[...], 0
            ).astype(jnp.bfloat16)


def prepare_kernel(cases, small, inverse, pick, gram_inverse):
    pick[...] = pick_rows(face_row(small, cases))
    first, second = inverse[:cases], inverse[cases:]
    beside, lower = first[:, cases:], second[:, :cases]
    corner = -times(beside, lower)
    gram_inverse[:cases, :cases] = first[:, :cases] - times(corner, beside.T)
    gram_inverse[:cases, cases:] = corner
    gram_inverse[cases:, :cases] = corner.T
    gram_inverse[cases:, cases:] = lower


def split_sums(place, first, second, more, keep, send):
    even = place[1] % 2 == 0
    rows = first.shape[0]
    keep[:rows] = jnp.where(even, first, second)
    send[:rows] = jnp.where(even, second, first)
    if more is not None:
        keep[rows:] = more
        send[rows:] = more


def join_sums(place, mine, other):
    even = place[1] % 2 == 0
    mine, other = mine[...], other[...]
    return jnp.where(even, mine, other), jnp.where(even, other, mine)


def first_kernel(place, small, x0, x1, y0, y1, high, low, ghosts, half, out, *sends):
    value, ghost = small[...], read_faces(place, (x0, x1, y0, y1))
    ghosts[...] = ghost
    cases = half.shape[0]
    resid, weighting, jump = rows_of(value, cases)
    ghost_resid, ghost_weighting, _ = rows_of(ghost, cases)
    field = weighting * resid + (0.5 * jump) * (ghost_weighting * ghost_resid)
    halfway = product(field, high, low, 0)
    half[...] = halfway
    lifted = product(halfway, high, low, 1)
    out[...] = lifted
    write_faces(place, jump * lifted, sends)


def gram_kernel(
    place, small, ghosts, half, out, x0, x1, y0, y1, high, low, image, ghost_image, second, keep, send
):
    cases = half.shape[0]
    resid, weighting, jump = rows_of(small[...], cases)
    _, ghost_weighting, ghost_jump = rows_of(ghosts[...], cases)
    own, ghost = images_of(out[...], read_faces(place, (x0, x1, y0, y1)), jump, ghost_jump)
    image[...] = own
    ghost_image[...] = ghost
    field = weighting * own + (0.5 * jump) * (ghost_weighting * ghost)
    largest = jnp.max(jnp.max(jnp.abs(field), axis=1, keepdims=True), axis=0, keepdims=True)
    scale = 1.0 / jnp.maximum(largest, 1e-30)
    second_half = product(field * scale, high, low, 0)
    second[:cases] = second_half
    second[cases:] = jnp.broadcast_to(scale, (PAD, field.shape[1]))
    first_half = half[...]
    cross = inner_prod(second_half, jnp.concatenate([first_half, second_half], axis=0))
    split_sums(
        place,
        jnp.concatenate(
            [inner_prod(first_half, first_half), inner_prod(weighting * resid, resid)], axis=1
        ),
        jnp.concatenate([cross[:, :cases].T, cross[:, cases:]], axis=1),
        jnp.broadcast_to(scale, (PAD, 2 * cases)),
        keep,
        send,
    )


def lift_kernel(place, small, second, high, low, out, *sends):
    cases = out.shape[0]
    jump = small[cases + 1 : cases + 2]
    lifted = product(second[:cases], high, low, 1)
    out[...] = lifted
    write_faces(place, jnp.concatenate([jump * lifted, second[cases:]], axis=0), sends)


def step_kernel(
    place, small, ghosts, mine, other, image0, ghost_image0, second, out1, x0, x1, y0, y1, high, low,
    state, inverse, image1, half, out, *sends
):
    cases = half.shape[0]
    resid, weighting, jump = rows_of(small[...], cases)
    ghost_resid, ghost_weighting, ghost_jump = rows_of(ghosts[...], cases)
    scale = mine[cases : cases + 1, :1]
    top, bottom = join_sums(place, mine, other)
    gram00, gram01, gram11 = top[:cases, :cases], bottom[:cases, :cases], bottom[:cases, cases:]
    first, along, corner, steps0, steps1 = solve_halves(
        gram00, gram01, gram11, top[:cases, cases:], scale * gram00
    )
    inverse[:cases, :cases] = first
    inverse[:cases, cases:] = along
    inverse[cases:, :cases] = corner
    inverse[cases:, cases:] = corner
    steps = jnp.concatenate([steps0, steps1], axis=0).T
    received = read_faces(place, (x0, x1, y0, y1))
    own_ratio = scale / second[cases : cases + 1]
    there = received[cases : cases + 1]
    ghost_ratio = jnp.where(there > 0.0, scale / jnp.where(there > 0.0, there, 1.0), 0.0)
    own1, ghost1 = images_of(
        out1[...] * own_ratio, received[:cases] * ghost_ratio, jump, ghost_jump
    )
    image1[...] = own1
    resid = resid - times(steps, jnp.concatenate([image0[...], own1], axis=0))
    ghost_resid = ghost_resid - times(
        steps, jnp.concatenate([ghost_image0[...], ghost1], axis=0)
    )
    state[:cases] = resid
    state[cases : 2 * cases, : 2 * cases] = steps
    field = weighting * resid + (0.5 * jump) * (ghost_weighting * ghost_resid)
    halfway = product(field, high, low, 0)
    half[...] = halfway
    lifted = product(halfway, high, low, 1)
    out[...] = lifted
    write_faces(place, jump * lifted, sends)


def next_gram_kernel(
    place, small, ghosts, mine, second, state, half, out, x0, x1, y0, y1, high, low,
    image, next_half, keep, send
):
    cases = half.shape[0]
    _, weighting, jump = rows_of(small[...], cases)
    _, ghost_weighting, ghost_jump = rows_of(ghosts[...], cases)
    scale = mine[cases : cases + 1, :1]
    own, ghost = images_of(out[...], read_faces(place, (x0, x1, y0, y1)), jump, ghost_jump)
    image[...] = own
    field = scale * (weighting * own + (0.5 * jump) * (ghost_weighting * ghost))
    halfway = product(field, high, low, 0)
    next_half[...] = halfway
    before = second[:cases] * (scale / second[cases : cases + 1])
    both = jnp.concatenate([half[...], halfway], axis=0)
    cross = inner_prod(jnp.concatenate([before, both], axis=0), both)
    resid = state[:cases]
    total = jnp.concatenate(
        [
            cross[: 2 * cases],
            jnp.concatenate(
                [inner_prod(weighting * resid, resid), cross[2 * cases :, cases:]], axis=1
            ),
        ],
        axis=0,
    )
    middle = total.shape[0] // 2
    split_sums(place, total[:middle], total[middle:], None, keep, send)


def next_lift_kernel(place, small, half, high, low, out, *sends):
    cases = out.shape[0]
    lifted = product(half[...], high, low, 1)
    out[...] = lifted
    write_faces(place, small[cases + 1 : cases + 2] * lifted, sends)


def last_kernel(
    place, small, first_sums, mine, other, state, gram_inverse, image0, image1, next_image0, out1,
    x0, x1, y0, y1, pick, solution_out, resid_out
):
    cases = image0.shape[0]
    _, weighting, _ = rows_of(small[...], cases)
    first_resid, resid = small[:cases], state[:cases]
    steps = state[cases : 2 * cases, : 2 * cases]
    scale = first_sums[cases : cases + 1, :1]
    total = jnp.concatenate(join_sums(place, mine, other), axis=0)
    along = jnp.concatenate(
        [
            jnp.concatenate([jnp.zeros((cases, cases), jnp.float32), total[:cases, :cases]], axis=1),
            total[:cases],
        ],
        axis=0,
    )
    conjugating = times(gram_inverse[...], along)
    taken = times(along.T, conjugating)
    gram00 = total[cases : 2 * cases, :cases]
    _, _, _, next0, next1 = solve_halves(
        gram00 - taken[:cases, :cases],
        total[cases : 2 * cases, cases:] - taken[:cases, cases:],
        total[2 * cases :, cases:] - taken[cases:, cases:],
        total[2 * cases :, :cases],
        scale * gram00,
    )
    next_steps = jnp.concatenate([next0, next1], axis=0)
    old_steps = -times(conjugating, next_steps).T
    next_steps = next_steps.T
    next_image1 = out1[...] + 0.5 * read_faces(place, (x0, x1, y0, y1))
    images = jnp.concatenate(
        [image0[...], image1[...], next_image0[...], next_image1], axis=0
    )
    resid = resid - times(jnp.concatenate([old_steps, next_steps], axis=1), images)
    fields = weighting * jnp.concatenate(
        [first_resid, scale * image0[...], state[:cases], scale * next_image0[...]], axis=0
    )
    answer = times(jnp.concatenate([steps + old_steps, next_steps], axis=1), fields)
    both = exact_pick(jnp.concatenate([answer, resid], axis=0), pick[...])
    solution_out[...] = both[:cases]
    resid_out[...] = both[cases:]


def call(kernel, name, outs, *operands, scratch=(), mebibytes=8, smem=1, flops=0):
    shapes = [
        jax.ShapeDtypeStruct(one[0], one[1]) if isinstance(one[0], tuple)
        else jax.ShapeDtypeStruct(one, jnp.float32)
        for one in outs
    ]
    touched = sum(one.size * one.dtype.itemsize for one in (*operands, *shapes))
    return pl.pallas_call(
        kernel,
        out_shape=shapes,
        in_specs=[SMEM] * smem + [VMEM] * (len(operands) - smem),
        out_specs=[VMEM] * len(shapes),
        scratch_shapes=list(scratch),
        compiler_params=pltpu.CompilerParams(vmem_limit_bytes=mebibytes * 2**20),
        cost_estimate=pl.CostEstimate(flops=flops, bytes_accessed=touched, transcendentals=0),
        name=name,
    )(*operands)


def swap_pairs(rows, columns, along, parity):
    pairs = []
    for x in range(rows):
        for y in range(columns):
            index, count = (x, rows) if along == "gx" else (y, columns)
            other = index + 1 if index % 2 == parity else index - 1
            if 0 <= other < count:
                target = (other, y) if along == "gx" else (x, other)
            else:
                target = (x, y ^ 1) if along == "gx" else (x ^ 1, y)
                if not (target[0] < rows and target[1] < columns):
                    target = (x, y)
            pairs.append((x * columns + y, target[0] * columns + target[1]))
    return pairs


def swap_faces(sends, axes=("gx", "gy")):
    rows, columns = lax.axis_size("gx"), lax.axis_size("gy")
    order = [(along, parity) for along in axes for parity in (0, 1)]
    return [
        lax.ppermute(send, ("gx", "gy"), swap_pairs(rows, columns, along, parity))
        for send, (along, parity) in zip(sends, order)
    ]


def stage_masks(axis, first):
    count = lax.axis_size(axis)
    stages = []
    step = first
    while step < count:
        last = step * 2 >= count
        stages.append((axis, (step,) if last else (step, 2 * step, 3 * step)))
        step *= 4
    return stages


def from_mask(value, axis, mask):
    count = lax.axis_size(axis)
    return lax.ppermute(value, axis, [(source, source ^ mask) for source in range(count)])


def sum_over_devices(keep, send, add, work, inputs):
    value = add([keep, from_mask(send, "gy", 1)])
    stages = stage_masks("gy", 2) + stage_masks("gx", 1)
    done, sends, received = (), (), []
    for index, (axis, masks) in enumerate(stages):
        value, inputs, sends = lax.optimization_barrier((value, inputs, sends))
        parts = [value] + [from_mask(value, axis, mask) for mask in masks]
        if index == 0:
            done, sends = work(*inputs)
        if index == len(stages) - 1:
            received = swap_faces(sends)
        value = add(parts)
        value, done, sends = lax.optimization_barrier((value, done, sends))
    return value, from_mask(value, "gy", 1), received, done


def plain(parts):
    value = parts[0] + parts[1]
    return value + (parts[2] + parts[3]) if len(parts) == 4 else value


def rescaled(parts):
    cases = parts[0].shape[0] - PAD
    scales = [part[cases:] for part in parts]
    scale = functools.reduce(jnp.minimum, scales)
    lane = lax.broadcasted_iota(jnp.int32, (cases, 2 * cases), 1)
    even = lax.axis_index("gy") % 2 == 0
    ready = []
    for part, own in zip(parts, scales):
        ratio = jnp.where(even, 1.0, (scale / own)[:1])
        ready.append(part[:cases] * jnp.where(lane < cases, ratio, ratio * ratio))
    return jnp.concatenate([plain(ready), scale], axis=0)


def local(right_side, weights, signs, face_map, pattern, factor):
    cases, size = right_side.shape[1:]
    blocks = pattern.shape[1]
    place = jnp.stack(
        [
            lax.axis_index("gx"),
            lax.axis_index("gy"),
            jnp.int32(lax.axis_size("gx")),
            jnp.int32(lax.axis_size("gy")),
        ]
    )
    field, padded = (cases, size), (cases + PAD, size)
    face, padded_face = (cases, size // 4), (cases + PAD, size // 4)
    half_type = ((size, size), jnp.bfloat16)

    work = 6 * cases * size * size
    row = lax.broadcasted_iota(jnp.int32, (PAD, size), 0)
    rows = jnp.where(
        row == 0,
        weights,
        jnp.where(
            row == 1, (2 * signs - 1).astype(jnp.float32), face_map.astype(jnp.float32)
        ),
    )
    small, *sends = call(
        start_kernel, "start_fields", [padded] + [padded_face] * 4, place, right_side[0], rows,
        flops=20 * work,
    )
    received = swap_faces(sends)
    high, low = call(
        functools.partial(factor_kernel, blocks), "masked_factor", [half_type] * 2,
        pattern[0], factor[0], face_map,
        scratch=[pltpu.VMEM((size, size), jnp.bfloat16)] * 2,
        smem=0, flops=4 * size**3,
    )
    ghosts, half0, out0, *sends = call(
        first_kernel, "first_operator", [padded, field, field] + [face] * 4,
        place, small, *received, high, low, flops=2 * work,
    )
    received = swap_faces(sends)
    image0, ghost_image0, second, keep, send = call(
        gram_kernel, "first_gram", [field, field, padded] + [(cases + PAD, 2 * cases)] * 2,
        place, small, ghosts, half0, out0, *received, high, low, flops=2 * work,
    )

    def lift(small, second, high, low):
        out, *sends = call(
            lift_kernel, "second_operator", [field] + [padded_face] * 4,
            place, small, second, high, low, flops=work,
        )
        return out, sends

    mine, other, faces, out1 = sum_over_devices(
        keep, send, rescaled, lift, (small, second, high, low)
    )
    state, inverse, image1, next_half0, next_out0, *next_sends = call(
        step_kernel, "first_step",
        [(2 * cases, size), (2 * cases, 2 * cases), field, field, field] + [face] * 4,
        place, small, ghosts, mine, other, image0, ghost_image0, second, out1,
        *faces, high, low, flops=4 * work,
    )
    faces = swap_faces(next_sends)
    next_image0, next_half1, keep, send = call(
        next_gram_kernel, "second_gram", [field, field] + [(3 * cases // 2, 2 * cases)] * 2,
        place, small, ghosts, mine, second, state, next_half0, next_out0, *faces, high, low,
        flops=2 * work,
    )

    def prepare(small, inverse, half, high, low):
        pick, gram_inverse = call(
            functools.partial(prepare_kernel, cases), "prepare_last",
            [half_type, (2 * cases, 2 * cases)], small, inverse, smem=0, flops=work,
        )
        out, *sends = call(
            next_lift_kernel, "last_operator", [field] + [face] * 4,
            place, small, half, high, low, flops=work,
        )
        return (pick, gram_inverse, out), sends

    next_mine, next_other, faces, (pick, gram_inverse, next_out1) = sum_over_devices(
        keep, send, plain, prepare, (small, inverse, next_half1, high, low)
    )
    answer, resid = call(
        last_kernel, "last_step", [field, field],
        place, small, mine, next_mine, next_other, state, gram_inverse, image0, image1,
        next_image0, next_out1, *faces, pick, flops=4 * work,
    )
    return (answer[None], resid[None])


def solution(mesh):
    return jax.shard_map(
        local,
        mesh=mesh,
        in_specs=(
            P("gx", None, "gy"),
            P("gx", "gy"),
            P("gx", "gy"),
            P("gx", "gy"),
            P("gx", None, "gy"),
            P("gx", None, "gy"),
        ),
        out_specs=(P("gx", None, "gy"), P("gx", None, "gy")),
        check_vma=False,
    )
```

```python
import functools

import jax
import jax.numpy as jnp
from jax import lax
from jax.experimental import pallas as pl
from jax.experimental.pallas import tpu as pltpu
from jax.sharding import PartitionSpec as P

HIGH = lax.Precision.HIGHEST
VMEM = pl.BlockSpec(memory_space=pltpu.VMEM)
SMEM = pl.BlockSpec(memory_space=pltpu.SMEM)
PAD = 8
SMALL = 1e-6
LANES = 128


def halves(value):
    high = value.astype(jnp.bfloat16)
    low = (value - high.astype(jnp.float32)).astype(jnp.bfloat16)
    return high, low


def thirds(value):
    high = value.astype(jnp.bfloat16)
    rest = value - high.astype(jnp.float32)
    middle = rest.astype(jnp.bfloat16)
    low = (rest - middle.astype(jnp.float32)).astype(jnp.bfloat16)
    return jnp.concatenate([high, middle, low], axis=0)


def bf16_dot(left, right, right_dim):
    return lax.dot_general(
        left, right, (((1,), (right_dim,)), ((), ())), preferred_element_type=jnp.float32
    )


def exact_pick(value, pick):
    rows = value.shape[0]
    parts = bf16_dot(thirds(value), pick, 0)
    return parts[:rows] + (parts[rows : 2 * rows] + parts[2 * rows :])


def product(value, high, low, dim):
    rows = value.shape[0]
    value_high, value_low = halves(value)
    both = bf16_dot(jnp.concatenate([value_high, value_low], axis=0), high[...], dim)
    return both[:rows] + (both[rows:] + bf16_dot(value_high, low[...], dim))


def inner_prod(left, right):
    return lax.dot_general(
        left, right, (((1,), (1,)), ((), ())), precision=HIGH, preferred_element_type=jnp.float32
    )


def times(left, right):
    return jnp.dot(left, right, precision=HIGH, preferred_element_type=jnp.float32)


def row_to_square(row, size):
    return jnp.broadcast_to(row, (LANES, size)).T


def pick_columns(face_row):
    size = face_row.shape[1]
    unknown = lax.broadcasted_iota(jnp.int32, (size, size), 0)
    return jnp.where(unknown == face_row, 1.0, 0.0).astype(jnp.bfloat16)


def pick_rows(face_row):
    size = face_row.shape[1]
    face = row_to_square(face_row, size)
    lane = lax.broadcasted_iota(jnp.int32, (size, LANES), 1)
    return jnp.concatenate(
        [
            jnp.where(face == lane + start, 1.0, 0.0).astype(jnp.bfloat16)
            for start in range(0, size, LANES)
        ],
        axis=1,
    )


def faces_of(field):
    face_len = field.shape[1] // 4
    return [field[:, face * face_len : (face + 1) * face_len] for face in range(4)]


def write_faces(place, field, outs):
    north, south, west, east = faces_of(field)
    even_x, even_y = place[0] % 2 == 0, place[1] % 2 == 0
    outs[0][...] = jnp.where(even_x, south, north)
    outs[1][...] = jnp.where(even_x, north, south)
    outs[2][...] = jnp.where(even_y, east, west)
    outs[3][...] = jnp.where(even_y, west, east)


def read_faces(place, received):
    x_first, x_second, y_first, y_second = [one[...] for one in received]
    even_x, even_y = place[0] % 2 == 0, place[1] % 2 == 0
    north = jnp.where(place[0] > 0, jnp.where(even_x, x_second, x_first), 0.0)
    south = jnp.where(place[0] + 1 < place[2], jnp.where(even_x, x_first, x_second), 0.0)
    west = jnp.where(place[1] > 0, jnp.where(even_y, y_second, y_first), 0.0)
    east = jnp.where(place[1] + 1 < place[3], jnp.where(even_y, y_first, y_second), 0.0)
    return jnp.concatenate([north, south, west, east], axis=1)


def rows_of(small, cases):
    return small[:cases], small[cases : cases + 1], small[cases + 1 : cases + 2]


def images_of(out, signed_ghost, jump, ghost_jump):
    image = out + 0.5 * signed_ghost
    ghost = ghost_jump * signed_ghost + (0.5 * jump * jnp.abs(ghost_jump)) * out
    return image, ghost


def inverse_of(matrix):
    size = matrix.shape[0]
    eye = lax.broadcasted_iota(jnp.int32, matrix.shape, 0) == lax.broadcasted_iota(
        jnp.int32, matrix.shape, 1
    )
    diagonal = jnp.where(eye, matrix, 0.0)
    by_row = lax.rsqrt(jnp.sum(diagonal, axis=1, keepdims=True))
    by_column = lax.rsqrt(jnp.sum(diagonal, axis=0, keepdims=True))
    scaled = matrix * by_row * by_column
    bound = jnp.max(jnp.sum(jnp.abs(scaled), axis=0, keepdims=True), axis=1, keepdims=True)
    square = jnp.sum(jnp.sum(scaled * scaled, axis=0, keepdims=True), axis=1, keepdims=True)
    one = jnp.where(eye, 1.0, 0.0)

    def again(state):
        _, before, now, count = state
        return (now > SMALL) & ((now < before) | (now > 1.0)) & (count < 64)

    def better(state):
        x, _, now, count = state
        left = one - times(scaled, x)
        twice = times(left, left)
        nearer = x + times(x, left)
        return nearer + times(nearer, twice), now, jnp.sum(twice * twice), count + 1

    start = one * jnp.minimum(size / square, 1.9 / bound)
    large = jnp.float32(4 * size)
    x, _, _, _ = lax.while_loop(again, better, (start, large, large, jnp.int32(0)))
    return x * by_row * by_column


def solve_halves(a00, a01, a11, b0, b1):
    size = a00.shape[0]
    first = inverse_of(a00)
    both = times(first, jnp.concatenate([a01, b0], axis=1))
    along, part = both[:, :size], both[:, size:]
    taken = times(a01.T, both)
    second = inverse_of(a11 - taken[:, :size])
    x1 = times(second, b1 - taken[:, size:])
    return first, along, second, part - times(along, x1), x1


def pick_kernel(faces, pick):
    pick[...] = pick_columns(faces[...])


def start_kernel(place, loads, weights, signs, faces, pick, small, *sends):
    cases, size = loads.shape
    jump = (2 * signs[...] - 1).astype(jnp.float32)
    more = jnp.concatenate(
        [weights[...], jump, jnp.zeros((PAD - 2, size), jnp.float32)], axis=0
    )
    value = exact_pick(jnp.concatenate([loads[...], more], axis=0), pick[...])
    write_faces(place, value, sends)
    small[...] = value
    small[cases + 2 : cases + 3] = faces[...].astype(jnp.float32)


def face_row(small, cases):
    return small[cases + 2 : cases + 3].astype(jnp.int32)


def factor_kernel(blocks, pattern, factor, faces, high, low, masked_high, masked_low):
    size = factor.shape[0]
    length = size // blocks
    for i in range(blocks):
        for j in range(blocks):
            rows, columns = pl.ds(i * length, length), pl.ds(j * length, length)
            value = factor[rows, columns]
            if i != j:
                keep = jnp.broadcast_to(pattern[i : i + 1, j : j + 1], value.shape)
                value = jnp.where(keep == 1, value, 0.0)
            masked_high[rows, columns], masked_low[rows, columns] = halves(value)
    pick = pick_rows(faces[...])
    chunk = size // 4
    for masked, out in ((masked_high, high), (masked_low, low)):
        for start in range(0, size, chunk):
            out[start : start + chunk] = bf16_dot(
                pick[start : start + chunk], masked[...], 0
            ).astype(jnp.bfloat16)


def prepare_kernel(cases, small, inverse, pick, gram_inverse):
    pick[...] = pick_rows(face_row(small, cases))
    first, second = inverse[:cases], inverse[cases:]
    beside, lower = first[:, cases:], second[:, :cases]
    corner = -times(beside, lower)
    gram_inverse[:cases, :cases] = first[:, :cases] - times(corner, beside.T)
    gram_inverse[:cases, cases:] = corner
    gram_inverse[cases:, :cases] = corner.T
    gram_inverse[cases:, cases:] = lower


def split_sums(place, first, second, more, keep, send):
    even = place[1] % 2 == 0
    rows = first.shape[0]
    keep[:rows] = jnp.where(even, first, second)
    send[:rows] = jnp.where(even, second, first)
    if more is not None:
        keep[rows:] = more
        send[rows:] = more


def join_sums(place, mine, other):
    even = place[1] % 2 == 0
    mine, other = mine[...], other[...]
    return jnp.where(even, mine, other), jnp.where(even, other, mine)


def first_kernel(place, small, x0, x1, y0, y1, high, low, ghosts, half, out, *sends):
    value, ghost = small[...], read_faces(place, (x0, x1, y0, y1))
    ghosts[...] = ghost
    cases = half.shape[0]
    resid, weighting, jump = rows_of(value, cases)
    ghost_resid, ghost_weighting, _ = rows_of(ghost, cases)
    field = weighting * resid + (0.5 * jump) * (ghost_weighting * ghost_resid)
    halfway = product(field, high, low, 0)
    half[...] = halfway
    lifted = product(halfway, high, low, 1)
    out[...] = lifted
    write_faces(place, jump * lifted, sends)


def gram_kernel(
    place, small, ghosts, half, out, x0, x1, y0, y1, high, low, image, ghost_image, second, keep, send
):
    cases = half.shape[0]
    resid, weighting, jump = rows_of(small[...], cases)
    _, ghost_weighting, ghost_jump = rows_of(ghosts[...], cases)
    own, ghost = images_of(out[...], read_faces(place, (x0, x1, y0, y1)), jump, ghost_jump)
    image[...] = own
    ghost_image[...] = ghost
    field = weighting * own + (0.5 * jump) * (ghost_weighting * ghost)
    largest = jnp.max(jnp.max(jnp.abs(field), axis=1, keepdims=True), axis=0, keepdims=True)
    scale = 1.0 / jnp.maximum(largest, 1e-30)
    second_half = product(field * scale, high, low, 0)
    second[:cases] = second_half
    second[cases:] = jnp.broadcast_to(scale, (PAD, field.shape[1]))
    first_half = half[...]
    cross = inner_prod(second_half, jnp.concatenate([first_half, second_half], axis=0))
    split_sums(
        place,
        jnp.concatenate(
            [inner_prod(first_half, first_half), inner_prod(weighting * resid, resid)], axis=1
        ),
        jnp.concatenate([cross[:, :cases].T, cross[:, cases:]], axis=1),
        jnp.broadcast_to(scale, (PAD, 2 * cases)),
        keep,
        send,
    )


def lift_kernel(place, small, second, high, low, out, *sends):
    cases = out.shape[0]
    jump = small[cases + 1 : cases + 2]
    lifted = product(second[:cases], high, low, 1)
    out[...] = lifted
    write_faces(place, jnp.concatenate([jump * lifted, second[cases:]], axis=0), sends)


def step_kernel(
    place, small, ghosts, mine, other, image0, ghost_image0, second, out1, x0, x1, y0, y1, high, low,
    state, inverse, image1, half, out, *sends
):
    cases = half.shape[0]
    resid, weighting, jump = rows_of(small[...], cases)
    ghost_resid, ghost_weighting, ghost_jump = rows_of(ghosts[...], cases)
    scale = mine[cases : cases + 1, :1]
    top, bottom = join_sums(place, mine, other)
    gram00, gram01, gram11 = top[:cases, :cases], bottom[:cases, :cases], bottom[:cases, cases:]
    first, along, corner, steps0, steps1 = solve_halves(
        gram00, gram01, gram11, top[:cases, cases:], scale * gram00
    )
    inverse[:cases, :cases] = first
    inverse[:cases, cases:] = along
    inverse[cases:, :cases] = corner
    inverse[cases:, cases:] = corner
    steps = jnp.concatenate([steps0, steps1], axis=0).T
    received = read_faces(place, (x0, x1, y0, y1))
    own_ratio = scale / second[cases : cases + 1]
    there = received[cases : cases + 1]
    ghost_ratio = jnp.where(there > 0.0, scale / jnp.where(there > 0.0, there, 1.0), 0.0)
    own1, ghost1 = images_of(
        out1[...] * own_ratio, received[:cases] * ghost_ratio, jump, ghost_jump
    )
    image1[...] = own1
    resid = resid - times(steps, jnp.concatenate([image0[...], own1], axis=0))
    ghost_resid = ghost_resid - times(
        steps, jnp.concatenate([ghost_image0[...], ghost1], axis=0)
    )
    state[:cases] = resid
    state[cases : 2 * cases, : 2 * cases] = steps
    field = weighting * resid + (0.5 * jump) * (ghost_weighting * ghost_resid)
    halfway = product(field, high, low, 0)
    half[...] = halfway
    lifted = product(halfway, high, low, 1)
    out[...] = lifted
    write_faces(place, jump * lifted, sends)


def next_gram_kernel(
    place, small, ghosts, mine, second, state, half, out, x0, x1, y0, y1, high, low,
    image, next_half, keep, send
):
    cases = half.shape[0]
    _, weighting, jump = rows_of(small[...], cases)
    _, ghost_weighting, ghost_jump = rows_of(ghosts[...], cases)
    scale = mine[cases : cases + 1, :1]
    own, ghost = images_of(out[...], read_faces(place, (x0, x1, y0, y1)), jump, ghost_jump)
    image[...] = own
    field = scale * (weighting * own + (0.5 * jump) * (ghost_weighting * ghost))
    halfway = product(field, high, low, 0)
    next_half[...] = halfway
    before = second[:cases] * (scale / second[cases : cases + 1])
    both = jnp.concatenate([half[...], halfway], axis=0)
    cross = inner_prod(jnp.concatenate([before, both], axis=0), both)
    resid = state[:cases]
    total = jnp.concatenate(
        [
            cross[: 2 * cases],
            jnp.concatenate(
                [inner_prod(weighting * resid, resid), cross[2 * cases :, cases:]], axis=1
            ),
        ],
        axis=0,
    )
    middle = total.shape[0] // 2
    split_sums(place, total[:middle], total[middle:], None, keep, send)


def next_lift_kernel(place, small, half, high, low, out, *sends):
    cases = out.shape[0]
    lifted = product(half[...], high, low, 1)
    out[...] = lifted
    write_faces(place, small[cases + 1 : cases + 2] * lifted, sends)


def last_kernel(
    place, small, first_sums, mine, other, state, gram_inverse, image0, image1, next_image0, out1,
    x0, x1, y0, y1, pick, solution_out, resid_out
):
    cases = image0.shape[0]
    _, weighting, _ = rows_of(small[...], cases)
    first_resid, resid = small[:cases], state[:cases]
    steps = state[cases : 2 * cases, : 2 * cases]
    scale = first_sums[cases : cases + 1, :1]
    total = jnp.concatenate(join_sums(place, mine, other), axis=0)
    along = jnp.concatenate(
        [
            jnp.concatenate([jnp.zeros((cases, cases), jnp.float32), total[:cases, :cases]], axis=1),
            total[:cases],
        ],
        axis=0,
    )
    conjugating = times(gram_inverse[...], along)
    taken = times(along.T, conjugating)
    gram00 = total[cases : 2 * cases, :cases]
    _, _, _, next0, next1 = solve_halves(
        gram00 - taken[:cases, :cases],
        total[cases : 2 * cases, cases:] - taken[:cases, cases:],
        total[2 * cases :, cases:] - taken[cases:, cases:],
        total[2 * cases :, :cases],
        scale * gram00,
    )
    next_steps = jnp.concatenate([next0, next1], axis=0)
    old_steps = -times(conjugating, next_steps).T
    next_steps = next_steps.T
    next_image1 = out1[...] + 0.5 * read_faces(place, (x0, x1, y0, y1))
    images = jnp.concatenate(
        [image0[...], image1[...], next_image0[...], next_image1], axis=0
    )
    resid = resid - times(jnp.concatenate([old_steps, next_steps], axis=1), images)
    fields = weighting * jnp.concatenate(
        [first_resid, scale * image0[...], state[:cases], scale * next_image0[...]], axis=0
    )
    answer = times(jnp.concatenate([steps + old_steps, next_steps], axis=1), fields)
    both = exact_pick(jnp.concatenate([answer, resid], axis=0), pick[...])
    solution_out[...] = both[:cases]
    resid_out[...] = both[cases:]


def call(kernel, name, outs, *operands, scratch=(), mebibytes=8, smem=1, flops=0):
    shapes = [
        jax.ShapeDtypeStruct(one[0], one[1]) if isinstance(one[0], tuple)
        else jax.ShapeDtypeStruct(one, jnp.float32)
        for one in outs
    ]
    touched = sum(one.size * one.dtype.itemsize for one in (*operands, *shapes))
    cost = pl.CostEstimate(flops=flops, bytes_accessed=touched, transcendentals=0)
    return pl.pallas_call(
        kernel,
        out_shape=shapes,
        in_specs=[SMEM] * smem + [VMEM] * (len(operands) - smem),
        out_specs=[VMEM] * len(shapes),
        scratch_shapes=list(scratch),
        compiler_params=pltpu.CompilerParams(vmem_limit_bytes=mebibytes * 2**20),
        cost_estimate=cost if flops else None,
        name=name,
    )(*operands)


def swap_pairs(rows, columns, along, parity):
    pairs = []
    for x in range(rows):
        for y in range(columns):
            index, count = (x, rows) if along == "gx" else (y, columns)
            other = index + 1 if index % 2 == parity else index - 1
            if 0 <= other < count:
                target = (other, y) if along == "gx" else (x, other)
            else:
                target = (x, y ^ 1) if along == "gx" else (x ^ 1, y)
                if not (target[0] < rows and target[1] < columns):
                    target = (x, y)
            pairs.append((x * columns + y, target[0] * columns + target[1]))
    return pairs


def swap_faces(sends, axes=("gx", "gy")):
    rows, columns = lax.axis_size("gx"), lax.axis_size("gy")
    order = [(along, parity) for along in axes for parity in (0, 1)]
    return [
        lax.ppermute(send, ("gx", "gy"), swap_pairs(rows, columns, along, parity))
        for send, (along, parity) in zip(sends, order)
    ]


def stage_masks(axis, first):
    count = lax.axis_size(axis)
    stages = []
    step = first
    while step < count:
        last = step * 2 >= count
        stages.append((axis, (step,) if last else (step, 2 * step, 3 * step)))
        step *= 4
    return stages


def from_mask(value, axis, mask):
    count = lax.axis_size(axis)
    return lax.ppermute(value, axis, [(source, source ^ mask) for source in range(count)])


def sum_over_devices(keep, send, add, work, inputs):
    value = add([keep, from_mask(send, "gy", 1)])
    stages = stage_masks("gy", 2) + stage_masks("gx", 1)
    done, sends, received = (), (), []
    for index, (axis, masks) in enumerate(stages):
        value, inputs, sends = lax.optimization_barrier((value, inputs, sends))
        parts = [value] + [from_mask(value, axis, mask) for mask in masks]
        if index == 0:
            done, sends = work(*inputs)
        if index == len(stages) - 1:
            received = swap_faces(sends)
        value = add(parts)
        value, done, sends = lax.optimization_barrier((value, done, sends))
    return value, from_mask(value, "gy", 1), received, done


def plain(parts):
    value = parts[0] + parts[1]
    return value + (parts[2] + parts[3]) if len(parts) == 4 else value


def rescaled(parts):
    cases = parts[0].shape[0] - PAD
    scales = [part[cases:] for part in parts]
    scale = functools.reduce(jnp.minimum, scales)
    lane = lax.broadcasted_iota(jnp.int32, (cases, 2 * cases), 1)
    even = lax.axis_index("gy") % 2 == 0
    ready = []
    for part, own in zip(parts, scales):
        ratio = jnp.where(even, 1.0, (scale / own)[:1])
        ready.append(part[:cases] * jnp.where(lane < cases, ratio, ratio * ratio))
    return jnp.concatenate([plain(ready), scale], axis=0)


def local(right_side, weights, signs, face_map, pattern, factor):
    cases, size = right_side.shape[1:]
    blocks = pattern.shape[1]
    place = jnp.stack(
        [
            lax.axis_index("gx"),
            lax.axis_index("gy"),
            jnp.int32(lax.axis_size("gx")),
            jnp.int32(lax.axis_size("gy")),
        ]
    )
    field, padded = (cases, size), (cases + PAD, size)
    face, padded_face = (cases, size // 4), (cases + PAD, size // 4)
    half_type = ((size, size), jnp.bfloat16)

    work = 6 * cases * size * size
    (pick,) = call(pick_kernel, "pick", [half_type], face_map, smem=0, flops=20 * work)
    small, *sends = call(
        start_kernel, "start_fields", [padded] + [padded_face] * 4,
        place, right_side[0], weights, signs, face_map, pick,
    )
    received = swap_faces(sends)
    high, low = call(
        functools.partial(factor_kernel, blocks), "masked_factor", [half_type] * 2,
        pattern[0], factor[0], face_map,
        scratch=[pltpu.VMEM((size, size), jnp.bfloat16)] * 2,
        smem=0,
    )
    ghosts, half0, out0, *sends = call(
        first_kernel, "first_operator", [padded, field, field] + [face] * 4,
        place, small, *received, high, low,
    )
    received = swap_faces(sends)
    image0, ghost_image0, second, keep, send = call(
        gram_kernel, "first_gram", [field, field, padded] + [(cases + PAD, 2 * cases)] * 2,
        place, small, ghosts, half0, out0, *received, high, low,
    )

    def lift(small, second, high, low):
        out, *sends = call(
            lift_kernel, "second_operator", [field] + [padded_face] * 4,
            place, small, second, high, low,
        )
        return out, sends

    mine, other, faces, out1 = sum_over_devices(
        keep, send, rescaled, lift, (small, second, high, low)
    )
    state, inverse, image1, next_half0, next_out0, *next_sends = call(
        step_kernel, "first_step",
        [(2 * cases, size), (2 * cases, 2 * cases), field, field, field] + [face] * 4,
        place, small, ghosts, mine, other, image0, ghost_image0, second, out1,
        *faces, high, low,
    )
    faces = swap_faces(next_sends)
    next_image0, next_half1, keep, send = call(
        next_gram_kernel, "second_gram", [field, field] + [(3 * cases // 2, 2 * cases)] * 2,
        place, small, ghosts, mine, second, state, next_half0, next_out0, *faces, high, low,
    )

    def prepare(small, inverse, half, high, low):
        pick, gram_inverse = call(
            functools.partial(prepare_kernel, cases), "prepare_last",
            [half_type, (2 * cases, 2 * cases)], small, inverse, smem=0,
        )
        out, *sends = call(
            next_lift_kernel, "last_operator", [field] + [face] * 4,
            place, small, half, high, low,
        )
        return (pick, gram_inverse, out), sends

    next_mine, next_other, faces, (pick, gram_inverse, next_out1) = sum_over_devices(
        keep, send, plain, prepare, (small, inverse, next_half1, high, low)
    )
    answer, resid = call(
        last_kernel, "last_step", [field, field],
        place, small, mine, next_mine, next_other, state, gram_inverse, image0, image1,
        next_image0, next_out1, *faces, pick,
    )
    return (answer[None], resid[None])


def solution(mesh):
    return jax.shard_map(
        local,
        mesh=mesh,
        in_specs=(
            P("gx", None, "gy"),
            P("gx", "gy"),
            P("gx", "gy"),
            P("gx", "gy"),
            P("gx", None, "gy"),
            P("gx", None, "gy"),
        ),
        out_specs=(P("gx", None, "gy"), P("gx", None, "gy")),
        check_vma=False,
    )
```

```python
import functools

import jax
import jax.numpy as jnp
from jax import lax
from jax.experimental import pallas as pl
from jax.experimental.pallas import tpu as pltpu
from jax.sharding import PartitionSpec as P

HIGH = lax.Precision.HIGHEST
VMEM = pl.BlockSpec(memory_space=pltpu.VMEM)
SMEM = pl.BlockSpec(memory_space=pltpu.SMEM)
PAD = 8
SMALL = 1e-6
LANES = 128


def halves(value):
    high = value.astype(jnp.bfloat16)
    low = (value - high.astype(jnp.float32)).astype(jnp.bfloat16)
    return high, low


def thirds(value):
    high = value.astype(jnp.bfloat16)
    rest = value - high.astype(jnp.float32)
    middle = rest.astype(jnp.bfloat16)
    low = (rest - middle.astype(jnp.float32)).astype(jnp.bfloat16)
    return jnp.concatenate([high, middle, low], axis=0)


def bf16_dot(left, right, right_dim):
    return lax.dot_general(
        left, right, (((1,), (right_dim,)), ((), ())), preferred_element_type=jnp.float32
    )


def exact_pick(value, pick):
    rows = value.shape[0]
    parts = bf16_dot(thirds(value), pick, 0)
    return parts[:rows] + (parts[rows : 2 * rows] + parts[2 * rows :])


def product(value, high, low, dim):
    rows = value.shape[0]
    value_high, value_low = halves(value)
    both = bf16_dot(jnp.concatenate([value_high, value_low], axis=0), high[...], dim)
    return both[:rows] + (both[rows:] + bf16_dot(value_high, low[...], dim))


def inner_prod(left, right):
    return lax.dot_general(
        left, right, (((1,), (1,)), ((), ())), precision=HIGH, preferred_element_type=jnp.float32
    )


def times(left, right):
    return jnp.dot(left, right, precision=HIGH, preferred_element_type=jnp.float32)


def row_to_square(row, size):
    return jnp.broadcast_to(row, (LANES, size)).T


def pick_columns(face_row):
    size = face_row.shape[1]
    unknown = lax.broadcasted_iota(jnp.int32, (size, size), 0)
    return jnp.where(unknown == face_row, 1.0, 0.0).astype(jnp.bfloat16)


def pick_rows(face_row):
    size = face_row.shape[1]
    face = row_to_square(face_row, size)
    lane = lax.broadcasted_iota(jnp.int32, (size, LANES), 1)
    return jnp.concatenate(
        [
            jnp.where(face == lane + start, 1.0, 0.0).astype(jnp.bfloat16)
            for start in range(0, size, LANES)
        ],
        axis=1,
    )


def faces_of(field):
    face_len = field.shape[1] // 4
    return [field[:, face * face_len : (face + 1) * face_len] for face in range(4)]


def write_faces(place, field, outs):
    north, south, west, east = faces_of(field)
    even_x, even_y = place[0] % 2 == 0, place[1] % 2 == 0
    outs[0][...] = jnp.where(even_x, south, north)
    outs[1][...] = jnp.where(even_x, north, south)
    outs[2][...] = jnp.where(even_y, east, west)
    outs[3][...] = jnp.where(even_y, west, east)


def read_faces(place, received):
    x_first, x_second, y_first, y_second = [one[...] for one in received]
    even_x, even_y = place[0] % 2 == 0, place[1] % 2 == 0
    north = jnp.where(place[0] > 0, jnp.where(even_x, x_second, x_first), 0.0)
    south = jnp.where(place[0] + 1 < place[2], jnp.where(even_x, x_first, x_second), 0.0)
    west = jnp.where(place[1] > 0, jnp.where(even_y, y_second, y_first), 0.0)
    east = jnp.where(place[1] + 1 < place[3], jnp.where(even_y, y_first, y_second), 0.0)
    return jnp.concatenate([north, south, west, east], axis=1)


def rows_of(small, cases):
    return small[:cases], small[cases : cases + 1], small[cases + 1 : cases + 2]


def images_of(out, signed_ghost, jump, ghost_jump):
    image = out + 0.5 * signed_ghost
    ghost = ghost_jump * signed_ghost + (0.5 * jump * jnp.abs(ghost_jump)) * out
    return image, ghost


def inverse_of(matrix):
    size = matrix.shape[0]
    eye = lax.broadcasted_iota(jnp.int32, matrix.shape, 0) == lax.broadcasted_iota(
        jnp.int32, matrix.shape, 1
    )
    diagonal = jnp.where(eye, matrix, 0.0)
    by_row = lax.rsqrt(jnp.sum(diagonal, axis=1, keepdims=True))
    by_column = lax.rsqrt(jnp.sum(diagonal, axis=0, keepdims=True))
    scaled = matrix * by_row * by_column
    bound = jnp.max(jnp.sum(jnp.abs(scaled), axis=0, keepdims=True), axis=1, keepdims=True)
    square = jnp.sum(jnp.sum(scaled * scaled, axis=0, keepdims=True), axis=1, keepdims=True)
    one = jnp.where(eye, 1.0, 0.0)

    def again(state):
        _, before, now, count = state
        return (now > SMALL) & ((now < before) | (now > 1.0)) & (count < 64)

    def better(state):
        x, _, now, count = state
        left = one - times(scaled, x)
        twice = times(left, left)
        nearer = x + times(x, left)
        return nearer + times(nearer, twice), now, jnp.sum(twice * twice), count + 1

    start = one * jnp.minimum(size / square, 1.9 / bound)
    large = jnp.float32(4 * size)
    x, _, _, _ = lax.while_loop(again, better, (start, large, large, jnp.int32(0)))
    return x * by_row * by_column


def solve_halves(a00, a01, a11, b0, b1):
    size = a00.shape[0]
    first = inverse_of(a00)
    both = times(first, jnp.concatenate([a01, b0], axis=1))
    along, part = both[:, :size], both[:, size:]
    taken = times(a01.T, both)
    second = inverse_of(a11 - taken[:, :size])
    x1 = times(second, b1 - taken[:, size:])
    return first, along, second, part - times(along, x1), x1


def pick_kernel(faces, pick):
    pick[...] = pick_columns(faces[...])


def start_kernel(place, loads, weights, signs, faces, pick, small, *sends):
    cases, size = loads.shape
    jump = (2 * signs[...] - 1).astype(jnp.float32)
    more = jnp.concatenate(
        [weights[...], jump, jnp.zeros((PAD - 2, size), jnp.float32)], axis=0
    )
    value = exact_pick(jnp.concatenate([loads[...], more], axis=0), pick[...])
    write_faces(place, value, sends)
    small[...] = value
    small[cases + 2 : cases + 3] = faces[...].astype(jnp.float32)


def face_row(small, cases):
    return small[cases + 2 : cases + 3].astype(jnp.int32)


def factor_kernel(blocks, pattern, factor, faces, high, low, masked_high, masked_low):
    size = factor.shape[0]
    length = size // blocks
    for i in range(blocks):
        for j in range(blocks):
            rows, columns = pl.ds(i * length, length), pl.ds(j * length, length)
            value = factor[rows, columns]
            if i != j:
                keep = jnp.broadcast_to(pattern[i : i + 1, j : j + 1], value.shape)
                value = jnp.where(keep == 1, value, 0.0)
            masked_high[rows, columns], masked_low[rows, columns] = halves(value)
    pick = pick_rows(faces[...])
    chunk = size // 4
    for masked, out in ((masked_high, high), (masked_low, low)):
        for start in range(0, size, chunk):
            out[start : start + chunk] = bf16_dot(
                pick[start : start + chunk], masked[...], 0
            ).astype(jnp.bfloat16)


def prepare_kernel(cases, small, inverse, pick, gram_inverse):
    pick[...] = pick_rows(face_row(small, cases))
    first, second = inverse[:cases], inverse[cases:]
    beside, lower = first[:, cases:], second[:, :cases]
    corner = -times(beside, lower)
    gram_inverse[:cases, :cases] = first[:, :cases] - times(corner, beside.T)
    gram_inverse[:cases, cases:] = corner
    gram_inverse[cases:, :cases] = corner.T
    gram_inverse[cases:, cases:] = lower


def split_sums(place, first, second, more, keep, send):
    even = place[1] % 2 == 0
    rows = first.shape[0]
    keep[:rows] = jnp.where(even, first, second)
    send[:rows] = jnp.where(even, second, first)
    if more is not None:
        keep[rows:] = more
        send[rows:] = more


def join_sums(place, mine, other):
    even = place[1] % 2 == 0
    mine, other = mine[...], other[...]
    return jnp.where(even, mine, other), jnp.where(even, other, mine)


def first_kernel(place, small, x0, x1, y0, y1, high, low, ghosts, half, out, *sends):
    value, ghost = small[...], read_faces(place, (x0, x1, y0, y1))
    ghosts[...] = ghost
    cases = half.shape[0]
    resid, weighting, jump = rows_of(value, cases)
    ghost_resid, ghost_weighting, _ = rows_of(ghost, cases)
    field = weighting * resid + (0.5 * jump) * (ghost_weighting * ghost_resid)
    halfway = product(field, high, low, 0)
    half[...] = halfway
    lifted = product(halfway, high, low, 1)
    out[...] = lifted
    write_faces(place, jump * lifted, sends)


def gram_kernel(
    place, small, ghosts, half, out, x0, x1, y0, y1, high, low, image, ghost_image, second, keep, send, power
):
    cases = half.shape[0]
    resid, weighting, jump = rows_of(small[...], cases)
    _, ghost_weighting, ghost_jump = rows_of(ghosts[...], cases)
    own, ghost = images_of(out[...], read_faces(place, (x0, x1, y0, y1)), jump, ghost_jump)
    image[...] = own
    ghost_image[...] = ghost
    field = weighting * own + (0.5 * jump) * (ghost_weighting * ghost)
    largest = jnp.max(jnp.max(jnp.abs(field), axis=1, keepdims=True), axis=0, keepdims=True)
    scale = 1.0 / jnp.maximum(largest, 1e-30)
    second_half = product(field * scale, high, low, 0)
    second[:cases] = second_half
    second[cases:] = jnp.broadcast_to(scale, (PAD, field.shape[1]))
    first_half = half[...]
    cross = inner_prod(second_half, jnp.concatenate([first_half, second_half], axis=0))
    split_sums(
        place,
        jnp.concatenate(
            [inner_prod(first_half, first_half), inner_prod(weighting * resid, resid)], axis=1
        ),
        jnp.concatenate([cross[:, :cases].T, cross[:, cases:]], axis=1),
        jnp.broadcast_to(scale, (PAD, 2 * cases)),
        keep,
        send,
    )
    lane = lax.broadcasted_iota(jnp.int32, (1, 2 * cases), 1)
    scaled = jnp.where(lane < cases, 1.0, 2.0)
    power[...] = jnp.where(place[1] % 2 == 0, jnp.zeros_like(scaled), scaled)


def lift_kernel(place, small, second, high, low, out, *sends):
    cases = out.shape[0]
    jump = small[cases + 1 : cases + 2]
    lifted = product(second[:cases], high, low, 1)
    out[...] = lifted
    write_faces(place, jnp.concatenate([jump * lifted, second[cases:]], axis=0), sends)


def step_kernel(
    place, small, ghosts, mine, other, image0, ghost_image0, second, out1, x0, x1, y0, y1, high, low,
    state, inverse, image1, half, out, *sends
):
    cases = half.shape[0]
    resid, weighting, jump = rows_of(small[...], cases)
    ghost_resid, ghost_weighting, ghost_jump = rows_of(ghosts[...], cases)
    scale = mine[cases : cases + 1, :1]
    top, bottom = join_sums(place, mine, other)
    gram00, gram01, gram11 = top[:cases, :cases], bottom[:cases, :cases], bottom[:cases, cases:]
    first, along, corner, steps0, steps1 = solve_halves(
        gram00, gram01, gram11, top[:cases, cases:], scale * gram00
    )
    inverse[:cases, :cases] = first
    inverse[:cases, cases:] = along
    inverse[cases:, :cases] = corner
    inverse[cases:, cases:] = corner
    steps = jnp.concatenate([steps0, steps1], axis=0).T
    received = read_faces(place, (x0, x1, y0, y1))
    own_ratio = scale / second[cases : cases + 1]
    there = received[cases : cases + 1]
    ghost_ratio = jnp.where(there > 0.0, scale / jnp.where(there > 0.0, there, 1.0), 0.0)
    own1, ghost1 = images_of(
        out1[...] * own_ratio, received[:cases] * ghost_ratio, jump, ghost_jump
    )
    image1[...] = own1
    resid = resid - times(steps, jnp.concatenate([image0[...], own1], axis=0))
    ghost_resid = ghost_resid - times(
        steps, jnp.concatenate([ghost_image0[...], ghost1], axis=0)
    )
    state[:cases] = resid
    state[cases : 2 * cases, : 2 * cases] = steps
    field = weighting * resid + (0.5 * jump) * (ghost_weighting * ghost_resid)
    halfway = product(field, high, low, 0)
    half[...] = halfway
    lifted = product(halfway, high, low, 1)
    out[...] = lifted
    write_faces(place, jump * lifted, sends)


def next_gram_kernel(
    place, small, ghosts, mine, second, state, half, out, x0, x1, y0, y1, high, low,
    image, next_half, keep, send
):
    cases = half.shape[0]
    _, weighting, jump = rows_of(small[...], cases)
    _, ghost_weighting, ghost_jump = rows_of(ghosts[...], cases)
    scale = mine[cases : cases + 1, :1]
    own, ghost = images_of(out[...], read_faces(place, (x0, x1, y0, y1)), jump, ghost_jump)
    image[...] = own
    field = scale * (weighting * own + (0.5 * jump) * (ghost_weighting * ghost))
    halfway = product(field, high, low, 0)
    next_half[...] = halfway
    before = second[:cases] * (scale / second[cases : cases + 1])
    both = jnp.concatenate([half[...], halfway], axis=0)
    cross = inner_prod(jnp.concatenate([before, both], axis=0), both)
    resid = state[:cases]
    total = jnp.concatenate(
        [
            cross[: 2 * cases],
            jnp.concatenate(
                [inner_prod(weighting * resid, resid), cross[2 * cases :, cases:]], axis=1
            ),
        ],
        axis=0,
    )
    middle = total.shape[0] // 2
    split_sums(place, total[:middle], total[middle:], None, keep, send)


def next_lift_kernel(place, small, half, high, low, out, *sends):
    cases = out.shape[0]
    lifted = product(half[...], high, low, 1)
    out[...] = lifted
    write_faces(place, small[cases + 1 : cases + 2] * lifted, sends)


def last_kernel(
    place, small, first_sums, mine, other, state, gram_inverse, image0, image1, next_image0, out1,
    x0, x1, y0, y1, pick, solution_out, resid_out
):
    cases = image0.shape[0]
    _, weighting, _ = rows_of(small[...], cases)
    first_resid, resid = small[:cases], state[:cases]
    steps = state[cases : 2 * cases, : 2 * cases]
    scale = first_sums[cases : cases + 1, :1]
    total = jnp.concatenate(join_sums(place, mine, other), axis=0)
    along = jnp.concatenate(
        [
            jnp.concatenate([jnp.zeros((cases, cases), jnp.float32), total[:cases, :cases]], axis=1),
            total[:cases],
        ],
        axis=0,
    )
    conjugating = times(gram_inverse[...], along)
    taken = times(along.T, conjugating)
    gram00 = total[cases : 2 * cases, :cases]
    _, _, _, next0, next1 = solve_halves(
        gram00 - taken[:cases, :cases],
        total[cases : 2 * cases, cases:] - taken[:cases, cases:],
        total[2 * cases :, cases:] - taken[cases:, cases:],
        total[2 * cases :, :cases],
        scale * gram00,
    )
    next_steps = jnp.concatenate([next0, next1], axis=0)
    old_steps = -times(conjugating, next_steps).T
    next_steps = next_steps.T
    next_image1 = out1[...] + 0.5 * read_faces(place, (x0, x1, y0, y1))
    images = jnp.concatenate(
        [image0[...], image1[...], next_image0[...], next_image1], axis=0
    )
    resid = resid - times(jnp.concatenate([old_steps, next_steps], axis=1), images)
    fields = weighting * jnp.concatenate(
        [first_resid, scale * image0[...], state[:cases], scale * next_image0[...]], axis=0
    )
    answer = times(jnp.concatenate([steps + old_steps, next_steps], axis=1), fields)
    both = exact_pick(jnp.concatenate([answer, resid], axis=0), pick[...])
    solution_out[...] = both[:cases]
    resid_out[...] = both[cases:]


def call(kernel, name, outs, *operands, scratch=(), mebibytes=8, smem=1, flops=0):
    shapes = [
        jax.ShapeDtypeStruct(one[0], one[1]) if isinstance(one[0], tuple)
        else jax.ShapeDtypeStruct(one, jnp.float32)
        for one in outs
    ]
    touched = sum(one.size * one.dtype.itemsize for one in (*operands, *shapes))
    cost = pl.CostEstimate(flops=flops, bytes_accessed=touched, transcendentals=0)
    return pl.pallas_call(
        kernel,
        out_shape=shapes,
        in_specs=[SMEM] * smem + [VMEM] * (len(operands) - smem),
        out_specs=[VMEM] * len(shapes),
        scratch_shapes=list(scratch),
        compiler_params=pltpu.CompilerParams(vmem_limit_bytes=mebibytes * 2**20),
        cost_estimate=cost if flops else None,
        name=name,
    )(*operands)


def swap_pairs(rows, columns, along, parity):
    pairs = []
    for x in range(rows):
        for y in range(columns):
            index, count = (x, rows) if along == "gx" else (y, columns)
            other = index + 1 if index % 2 == parity else index - 1
            if 0 <= other < count:
                target = (other, y) if along == "gx" else (x, other)
            else:
                target = (x, y ^ 1) if along == "gx" else (x ^ 1, y)
                if not (target[0] < rows and target[1] < columns):
                    target = (x, y)
            pairs.append((x * columns + y, target[0] * columns + target[1]))
    return pairs


def swap_faces(sends, axes=("gx", "gy")):
    rows, columns = lax.axis_size("gx"), lax.axis_size("gy")
    order = [(along, parity) for along in axes for parity in (0, 1)]
    return [
        lax.ppermute(send, ("gx", "gy"), swap_pairs(rows, columns, along, parity))
        for send, (along, parity) in zip(sends, order)
    ]


def stage_masks(axis, first):
    count = lax.axis_size(axis)
    stages = []
    step = first
    while step < count:
        last = step * 2 >= count
        stages.append((axis, (step,) if last else (step, 2 * step, 3 * step)))
        step *= 4
    return stages


def from_mask(value, axis, mask):
    count = lax.axis_size(axis)
    return lax.ppermute(value, axis, [(source, source ^ mask) for source in range(count)])


def sum_over_devices(keep, send, add, work, inputs):
    value = add([keep, from_mask(send, "gy", 1)])
    stages = stage_masks("gy", 2) + stage_masks("gx", 1)
    done, sends, received = (), (), []
    for index, (axis, masks) in enumerate(stages):
        value, inputs, sends = lax.optimization_barrier((value, inputs, sends))
        parts = [value] + [from_mask(value, axis, mask) for mask in masks]
        if index == 0:
            done, sends = work(*inputs)
        if index == len(stages) - 1:
            received = swap_faces(sends)
        value = add(parts)
        value, done, sends = lax.optimization_barrier((value, done, sends))
    return value, from_mask(value, "gy", 1), received, done


def plain(parts):
    value = parts[0] + parts[1]
    return value + (parts[2] + parts[3]) if len(parts) == 4 else value


def rescaled(power, parts):
    cases = parts[0].shape[0] - PAD
    scales = [part[cases:] for part in parts]
    scale = functools.reduce(jnp.minimum, scales)
    ready = []
    for part, own in zip(parts, scales):
        ratio = (scale / own)[:1]
        factor = jnp.where(power == 0.0, 1.0, jnp.where(power == 1.0, ratio, ratio * ratio))
        ready.append(part[:cases] * factor)
    return jnp.concatenate([plain(ready), scale], axis=0)


def local(right_side, weights, signs, face_map, pattern, factor):
    cases, size = right_side.shape[1:]
    blocks = pattern.shape[1]
    place = jnp.stack(
        [
            lax.axis_index("gx"),
            lax.axis_index("gy"),
            jnp.int32(lax.axis_size("gx")),
            jnp.int32(lax.axis_size("gy")),
        ]
    )
    field, padded = (cases, size), (cases + PAD, size)
    face, padded_face = (cases, size // 4), (cases + PAD, size // 4)
    half_type = ((size, size), jnp.bfloat16)

    work = 6 * cases * size * size
    (pick,) = call(pick_kernel, "pick", [half_type], face_map, smem=0, flops=20 * work)
    small, *sends = call(
        start_kernel, "start_fields", [padded] + [padded_face] * 4,
        place, right_side[0], weights, signs, face_map, pick,
    )
    received = swap_faces(sends)
    high, low = call(
        functools.partial(factor_kernel, blocks), "masked_factor", [half_type] * 2,
        pattern[0], factor[0], face_map,
        scratch=[pltpu.VMEM((size, size), jnp.bfloat16)] * 2,
        smem=0,
    )
    ghosts, half0, out0, *sends = call(
        first_kernel, "first_operator", [padded, field, field] + [face] * 4,
        place, small, *received, high, low,
    )
    received = swap_faces(sends)
    image0, ghost_image0, second, keep, send, power = call(
        gram_kernel, "first_gram",
        [field, field, padded] + [(cases + PAD, 2 * cases)] * 2 + [(1, 2 * cases)],
        place, small, ghosts, half0, out0, *received, high, low,
    )

    def lift(second):
        out, *sends = call(
            lift_kernel, "second_operator", [field] + [padded_face] * 4,
            place, small, second, high, low,
        )
        return out, sends

    mine, other, faces, out1 = sum_over_devices(
        keep, send, functools.partial(rescaled, power), lift, (second,)
    )
    state, inverse, image1, next_half0, next_out0, *next_sends = call(
        step_kernel, "first_step",
        [(2 * cases, size), (2 * cases, 2 * cases), field, field, field] + [face] * 4,
        place, small, ghosts, mine, other, image0, ghost_image0, second, out1,
        *faces, high, low,
    )
    faces = swap_faces(next_sends)
    next_image0, next_half1, keep, send = call(
        next_gram_kernel, "second_gram", [field, field] + [(3 * cases // 2, 2 * cases)] * 2,
        place, small, ghosts, mine, second, state, next_half0, next_out0, *faces, high, low,
    )

    def prepare(inverse, half):
        pick, gram_inverse = call(
            functools.partial(prepare_kernel, cases), "prepare_last",
            [half_type, (2 * cases, 2 * cases)], small, inverse, smem=0,
        )
        out, *sends = call(
            next_lift_kernel, "last_operator", [field] + [face] * 4,
            place, small, half, high, low,
        )
        return (pick, gram_inverse, out), sends

    next_mine, next_other, faces, (pick, gram_inverse, next_out1) = sum_over_devices(
        keep, send, plain, prepare, (inverse, next_half1)
    )
    answer, resid = call(
        last_kernel, "last_step", [field, field],
        place, small, mine, next_mine, next_other, state, gram_inverse, image0, image1,
        next_image0, next_out1, *faces, pick,
    )
    return (answer[None], resid[None])


def solution(mesh):
    return jax.shard_map(
        local,
        mesh=mesh,
        in_specs=(
            P("gx", None, "gy"),
            P("gx", "gy"),
            P("gx", "gy"),
            P("gx", "gy"),
            P("gx", None, "gy"),
            P("gx", None, "gy"),
        ),
        out_specs=(P("gx", None, "gy"), P("gx", None, "gy")),
        check_vma=False,
    )
```

```python
import functools

import jax
import jax.numpy as jnp
from jax import lax
from jax.experimental import pallas as pl
from jax.experimental.pallas import tpu as pltpu
from jax.sharding import PartitionSpec as P

HIGH = lax.Precision.HIGHEST
VMEM = pl.BlockSpec(memory_space=pltpu.VMEM)
SMEM = pl.BlockSpec(memory_space=pltpu.SMEM)
PAD = 8
SMALL = 1e-6
LANES = 128


def halves(value):
    high = value.astype(jnp.bfloat16)
    low = (value - high.astype(jnp.float32)).astype(jnp.bfloat16)
    return high, low


def thirds(value):
    high = value.astype(jnp.bfloat16)
    rest = value - high.astype(jnp.float32)
    middle = rest.astype(jnp.bfloat16)
    low = (rest - middle.astype(jnp.float32)).astype(jnp.bfloat16)
    return jnp.concatenate([high, middle, low], axis=0)


def bf16_dot(left, right, right_dim):
    return lax.dot_general(
        left, right, (((1,), (right_dim,)), ((), ())), preferred_element_type=jnp.float32
    )


def exact_pick(value, pick):
    rows = value.shape[0]
    parts = bf16_dot(thirds(value), pick, 0)
    return parts[:rows] + (parts[rows : 2 * rows] + parts[2 * rows :])


def product(value, high, low, dim):
    rows = value.shape[0]
    value_high, value_low = halves(value)
    both = bf16_dot(jnp.concatenate([value_high, value_low], axis=0), high[...], dim)
    return both[:rows] + (both[rows:] + bf16_dot(value_high, low[...], dim))


def inner_prod(left, right):
    return lax.dot_general(
        left, right, (((1,), (1,)), ((), ())), precision=HIGH, preferred_element_type=jnp.float32
    )


def times(left, right):
    return jnp.dot(left, right, precision=HIGH, preferred_element_type=jnp.float32)


def row_to_square(row, size):
    return jnp.broadcast_to(row, (LANES, size)).T


def pick_columns(face_row):
    size = face_row.shape[1]
    unknown = lax.broadcasted_iota(jnp.int32, (size, size), 0)
    return jnp.where(unknown == face_row, 1.0, 0.0).astype(jnp.bfloat16)


def pick_rows(face_row):
    size = face_row.shape[1]
    face = row_to_square(face_row, size)
    lane = lax.broadcasted_iota(jnp.int32, (size, LANES), 1)
    return jnp.concatenate(
        [
            jnp.where(face == lane + start, 1.0, 0.0).astype(jnp.bfloat16)
            for start in range(0, size, LANES)
        ],
        axis=1,
    )


def faces_of(field):
    face_len = field.shape[1] // 4
    return [field[:, face * face_len : (face + 1) * face_len] for face in range(4)]


def write_faces(place, field, outs):
    north, south, west, east = faces_of(field)
    even_x, even_y = place[0] % 2 == 0, place[1] % 2 == 0
    outs[0][...] = jnp.where(even_x, south, north)
    outs[1][...] = jnp.where(even_x, north, south)
    outs[2][...] = jnp.where(even_y, east, west)
    outs[3][...] = jnp.where(even_y, west, east)


def read_faces(place, received):
    x_first, x_second, y_first, y_second = [one[...] for one in received]
    even_x, even_y = place[0] % 2 == 0, place[1] % 2 == 0
    north = jnp.where(place[0] > 0, jnp.where(even_x, x_second, x_first), 0.0)
    south = jnp.where(place[0] + 1 < place[2], jnp.where(even_x, x_first, x_second), 0.0)
    west = jnp.where(place[1] > 0, jnp.where(even_y, y_second, y_first), 0.0)
    east = jnp.where(place[1] + 1 < place[3], jnp.where(even_y, y_first, y_second), 0.0)
    return jnp.concatenate([north, south, west, east], axis=1)


def rows_of(small, cases):
    return small[:cases], small[cases : cases + 1], small[cases + 1 : cases + 2]


def images_of(out, signed_ghost, jump, ghost_jump):
    image = out + 0.5 * signed_ghost
    ghost = ghost_jump * signed_ghost + (0.5 * jump * jnp.abs(ghost_jump)) * out
    return image, ghost


def inverse_of(matrix):
    size = matrix.shape[0]
    eye = lax.broadcasted_iota(jnp.int32, matrix.shape, 0) == lax.broadcasted_iota(
        jnp.int32, matrix.shape, 1
    )
    diagonal = jnp.where(eye, matrix, 0.0)
    by_row = lax.rsqrt(jnp.sum(diagonal, axis=1, keepdims=True))
    by_column = lax.rsqrt(jnp.sum(diagonal, axis=0, keepdims=True))
    scaled = matrix * by_row * by_column
    bound = jnp.max(jnp.sum(jnp.abs(scaled), axis=0, keepdims=True), axis=1, keepdims=True)
    square = jnp.sum(jnp.sum(scaled * scaled, axis=0, keepdims=True), axis=1, keepdims=True)
    one = jnp.where(eye, 1.0, 0.0)

    def again(state):
        _, before, now, count = state
        return (now > SMALL) & ((now < before) | (now > 1.0)) & (count < 64)

    def better(state):
        x, _, now, count = state
        left = one - times(scaled, x)
        twice = times(left, left)
        nearer = x + times(x, left)
        return nearer + times(nearer, twice), now, jnp.sum(twice * twice), count + 1

    start = one * jnp.minimum(size / square, 1.9 / bound)
    large = jnp.float32(4 * size)
    x, _, _, _ = lax.while_loop(again, better, (start, large, large, jnp.int32(0)))
    return x * by_row * by_column


def solve_halves(a00, a01, a11, b0, b1):
    size = a00.shape[0]
    first = inverse_of(a00)
    both = times(first, jnp.concatenate([a01, b0], axis=1))
    along, part = both[:, :size], both[:, size:]
    taken = times(a01.T, both)
    second = inverse_of(a11 - taken[:, :size])
    x1 = times(second, b1 - taken[:, size:])
    return first, along, second, part - times(along, x1), x1


def pick_kernel(faces, pick):
    pick[...] = pick_columns(faces[...])


def start_kernel(place, loads, weights, signs, faces, pick, small, *sends):
    cases, size = loads.shape
    jump = (2 * signs[...] - 1).astype(jnp.float32)
    more = jnp.concatenate(
        [weights[...], jump, jnp.zeros((PAD - 2, size), jnp.float32)], axis=0
    )
    value = exact_pick(jnp.concatenate([loads[...], more], axis=0), pick[...])
    write_faces(place, value, sends)
    small[...] = value
    small[cases + 2 : cases + 3] = faces[...].astype(jnp.float32)


def face_row(small, cases):
    return small[cases + 2 : cases + 3].astype(jnp.int32)


def factor_kernel(blocks, pattern, factor, faces, high, low, masked_high, masked_low):
    size = factor.shape[0]
    length = size // blocks
    for i in range(blocks):
        for j in range(blocks):
            rows, columns = pl.ds(i * length, length), pl.ds(j * length, length)
            value = factor[rows, columns]
            if i != j:
                keep = jnp.broadcast_to(pattern[i : i + 1, j : j + 1], value.shape)
                value = jnp.where(keep == 1, value, 0.0)
            masked_high[rows, columns], masked_low[rows, columns] = halves(value)
    pick = pick_rows(faces[...])
    chunk = size // 4
    for masked, out in ((masked_high, high), (masked_low, low)):
        for start in range(0, size, chunk):
            out[start : start + chunk] = bf16_dot(
                pick[start : start + chunk], masked[...], 0
            ).astype(jnp.bfloat16)


def prepare_kernel(cases, small, inverse, pick, gram_inverse):
    pick[...] = pick_rows(face_row(small, cases))
    first, second = inverse[:cases], inverse[cases:]
    beside, lower = first[:, cases:], second[:, :cases]
    corner = -times(beside, lower)
    gram_inverse[:cases, :cases] = first[:, :cases] - times(corner, beside.T)
    gram_inverse[:cases, cases:] = corner
    gram_inverse[cases:, :cases] = corner.T
    gram_inverse[cases:, cases:] = lower


def split_sums(place, first, second, more, keep, send):
    even = place[1] % 2 == 0
    rows = first.shape[0]
    keep[:rows] = jnp.where(even, first, second)
    send[:rows] = jnp.where(even, second, first)
    if more is not None:
        keep[rows:] = more
        send[rows:] = more


def join_sums(place, mine, other):
    even = place[1] % 2 == 0
    mine, other = mine[...], other[...]
    return jnp.where(even, mine, other), jnp.where(even, other, mine)


def first_kernel(place, small, x0, x1, y0, y1, high, low, ghosts, half, out, *sends):
    value, ghost = small[...], read_faces(place, (x0, x1, y0, y1))
    ghosts[...] = ghost
    cases = half.shape[0]
    resid, weighting, jump = rows_of(value, cases)
    ghost_resid, ghost_weighting, _ = rows_of(ghost, cases)
    field = weighting * resid + (0.5 * jump) * (ghost_weighting * ghost_resid)
    halfway = product(field, high, low, 0)
    half[...] = halfway
    lifted = product(halfway, high, low, 1)
    out[...] = lifted
    write_faces(place, jump * lifted, sends)


def gram_kernel(
    place, small, ghosts, half, out, x0, x1, y0, y1, high, low, image, ghost_image, second, keep, send, power
):
    cases = half.shape[0]
    resid, weighting, jump = rows_of(small[...], cases)
    _, ghost_weighting, ghost_jump = rows_of(ghosts[...], cases)
    own, ghost = images_of(out[...], read_faces(place, (x0, x1, y0, y1)), jump, ghost_jump)
    image[...] = own
    ghost_image[...] = ghost
    field = weighting * own + (0.5 * jump) * (ghost_weighting * ghost)
    largest = jnp.max(jnp.max(jnp.abs(field), axis=1, keepdims=True), axis=0, keepdims=True)
    scale = 1.0 / jnp.maximum(largest, 1e-30)
    second_half = product(field * scale, high, low, 0)
    second[:cases] = second_half
    second[cases:] = jnp.broadcast_to(scale, (PAD, field.shape[1]))
    first_half = half[...]
    cross = inner_prod(second_half, jnp.concatenate([first_half, second_half], axis=0))
    split_sums(
        place,
        jnp.concatenate(
            [inner_prod(first_half, first_half), inner_prod(weighting * resid, resid)], axis=1
        ),
        jnp.concatenate([cross[:, :cases].T, cross[:, cases:]], axis=1),
        jnp.broadcast_to(scale, (PAD, 2 * cases)),
        keep,
        send,
    )
    lane = lax.broadcasted_iota(jnp.int32, (1, 2 * cases), 1)
    scaled = jnp.where(lane < cases, 1.0, 2.0)
    power[...] = jnp.where(place[1] % 2 == 0, jnp.zeros_like(scaled), scaled)


def lift_kernel(place, small, second, high, low, out, *sends):
    cases = out.shape[0]
    jump = small[cases + 1 : cases + 2]
    lifted = product(second[:cases], high, low, 1)
    out[...] = lifted
    write_faces(place, jnp.concatenate([jump * lifted, second[cases:]], axis=0), sends)


def solve_kernel(place, mine, other, steps, inverse):
    cases = steps.shape[0]
    scale = mine[cases : cases + 1, :1]
    top, bottom = join_sums(place, mine, other)
    gram00, gram01, gram11 = top[:cases, :cases], bottom[:cases, :cases], bottom[:cases, cases:]
    first, along, corner, steps0, steps1 = solve_halves(
        gram00, gram01, gram11, top[:cases, cases:], scale * gram00
    )
    inverse[:cases, :cases] = first
    inverse[:cases, cases:] = along
    inverse[cases:, :cases] = corner
    inverse[cases:, cases:] = corner
    steps[...] = jnp.concatenate([steps0, steps1], axis=0).T


def step_kernel(
    place, small, ghosts, mine, steps, image0, ghost_image0, second, out1, x0, x1, y0, y1,
    high, low, state, image1, half, out, *sends
):
    cases = half.shape[0]
    resid, weighting, jump = rows_of(small[...], cases)
    ghost_resid, ghost_weighting, ghost_jump = rows_of(ghosts[...], cases)
    scale = mine[cases : cases + 1, :1]
    received = read_faces(place, (x0, x1, y0, y1))
    own_ratio = scale / second[cases : cases + 1]
    there = received[cases : cases + 1]
    ghost_ratio = jnp.where(there > 0.0, scale / jnp.where(there > 0.0, there, 1.0), 0.0)
    own1, ghost1 = images_of(
        out1[...] * own_ratio, received[:cases] * ghost_ratio, jump, ghost_jump
    )
    image1[...] = own1
    resid = resid - times(steps[...], jnp.concatenate([image0[...], own1], axis=0))
    ghost_resid = ghost_resid - times(
        steps[...], jnp.concatenate([ghost_image0[...], ghost1], axis=0)
    )
    state[...] = resid
    field = weighting * resid + (0.5 * jump) * (ghost_weighting * ghost_resid)
    halfway = product(field, high, low, 0)
    half[...] = halfway
    lifted = product(halfway, high, low, 1)
    out[...] = lifted
    write_faces(place, jump * lifted, sends)


def next_gram_kernel(
    place, small, ghosts, mine, second, state, half, out, x0, x1, y0, y1, high, low,
    image, next_half, keep, send
):
    cases = half.shape[0]
    _, weighting, jump = rows_of(small[...], cases)
    _, ghost_weighting, ghost_jump = rows_of(ghosts[...], cases)
    scale = mine[cases : cases + 1, :1]
    own, ghost = images_of(out[...], read_faces(place, (x0, x1, y0, y1)), jump, ghost_jump)
    image[...] = own
    field = scale * (weighting * own + (0.5 * jump) * (ghost_weighting * ghost))
    halfway = product(field, high, low, 0)
    next_half[...] = halfway
    before = second[:cases] * (scale / second[cases : cases + 1])
    both = jnp.concatenate([half[...], halfway], axis=0)
    cross = inner_prod(jnp.concatenate([before, both], axis=0), both)
    resid = state[...]
    total = jnp.concatenate(
        [
            cross[: 2 * cases],
            jnp.concatenate(
                [inner_prod(weighting * resid, resid), cross[2 * cases :, cases:]], axis=1
            ),
        ],
        axis=0,
    )
    middle = total.shape[0] // 2
    split_sums(place, total[:middle], total[middle:], None, keep, send)


def next_lift_kernel(place, small, half, high, low, out, *sends):
    cases = out.shape[0]
    lifted = product(half[...], high, low, 1)
    out[...] = lifted
    write_faces(place, small[cases + 1 : cases + 2] * lifted, sends)


def last_solve_kernel(place, first_sums, mine, other, gram_inverse, steps, answer, change):
    cases = steps.shape[0]
    scale = first_sums[cases : cases + 1, :1]
    total = jnp.concatenate(join_sums(place, mine, other), axis=0)
    along = jnp.concatenate(
        [
            jnp.concatenate([jnp.zeros((cases, cases), jnp.float32), total[:cases, :cases]], axis=1),
            total[:cases],
        ],
        axis=0,
    )
    conjugating = times(gram_inverse[...], along)
    taken = times(along.T, conjugating)
    gram00 = total[cases : 2 * cases, :cases]
    _, _, _, next0, next1 = solve_halves(
        gram00 - taken[:cases, :cases],
        total[cases : 2 * cases, cases:] - taken[:cases, cases:],
        total[2 * cases :, cases:] - taken[cases:, cases:],
        total[2 * cases :, :cases],
        scale * gram00,
    )
    next_steps = jnp.concatenate([next0, next1], axis=0)
    old_steps = -times(conjugating, next_steps).T
    next_steps = next_steps.T
    answer[...] = jnp.concatenate([steps[...] + old_steps, next_steps], axis=1)
    change[...] = jnp.concatenate([old_steps, next_steps], axis=1)


def last_kernel(
    place, small, first_sums, answer, change, state, image0, image1, next_image0, out1,
    x0, x1, y0, y1, pick, solution_out, resid_out
):
    cases = image0.shape[0]
    first_resid, weighting, _ = rows_of(small[...], cases)
    scale = first_sums[cases : cases + 1, :1]
    next_image1 = out1[...] + 0.5 * read_faces(place, (x0, x1, y0, y1))
    images = jnp.concatenate(
        [image0[...], image1[...], next_image0[...], next_image1], axis=0
    )
    resid = state[...] - times(change[...], images)
    fields = weighting * jnp.concatenate(
        [first_resid, scale * image0[...], state[...], scale * next_image0[...]], axis=0
    )
    found = times(answer[...], fields)
    both = exact_pick(jnp.concatenate([found, resid], axis=0), pick[...])
    solution_out[...] = both[:cases]
    resid_out[...] = both[cases:]


def call(kernel, name, outs, *operands, scratch=(), mebibytes=8, smem=1, flops=0):
    shapes = [
        jax.ShapeDtypeStruct(one[0], one[1]) if isinstance(one[0], tuple)
        else jax.ShapeDtypeStruct(one, jnp.float32)
        for one in outs
    ]
    touched = sum(one.size * one.dtype.itemsize for one in (*operands, *shapes))
    cost = pl.CostEstimate(flops=flops, bytes_accessed=touched, transcendentals=0)
    return pl.pallas_call(
        kernel,
        out_shape=shapes,
        in_specs=[SMEM] * smem + [VMEM] * (len(operands) - smem),
        out_specs=[VMEM] * len(shapes),
        scratch_shapes=list(scratch),
        compiler_params=pltpu.CompilerParams(vmem_limit_bytes=mebibytes * 2**20),
        cost_estimate=cost if flops else None,
        name=name,
    )(*operands)


def swap_pairs(rows, columns, along, parity):
    pairs = []
    for x in range(rows):
        for y in range(columns):
            index, count = (x, rows) if along == "gx" else (y, columns)
            other = index + 1 if index % 2 == parity else index - 1
            if 0 <= other < count:
                target = (other, y) if along == "gx" else (x, other)
            else:
                target = (x, y ^ 1) if along == "gx" else (x ^ 1, y)
                if not (target[0] < rows and target[1] < columns):
                    target = (x, y)
            pairs.append((x * columns + y, target[0] * columns + target[1]))
    return pairs


def swap_faces(sends, axes=("gx", "gy")):
    rows, columns = lax.axis_size("gx"), lax.axis_size("gy")
    order = [(along, parity) for along in axes for parity in (0, 1)]
    return [
        lax.ppermute(send, ("gx", "gy"), swap_pairs(rows, columns, along, parity))
        for send, (along, parity) in zip(sends, order)
    ]


def stage_masks(axis, first):
    count = lax.axis_size(axis)
    stages = []
    step = first
    while step < count:
        last = step * 2 >= count
        stages.append((axis, (step,) if last else (step, 2 * step, 3 * step)))
        step *= 4
    return stages


def from_mask(value, axis, mask):
    count = lax.axis_size(axis)
    return lax.ppermute(value, axis, [(source, source ^ mask) for source in range(count)])


def sum_over_devices(keep, send, add, work, inputs):
    value = add([keep, from_mask(send, "gy", 1)])
    stages = stage_masks("gy", 2) + stage_masks("gx", 1)
    done, sends, received = (), (), []
    for index, (axis, masks) in enumerate(stages):
        value, inputs, sends = lax.optimization_barrier((value, inputs, sends))
        parts = [value] + [from_mask(value, axis, mask) for mask in masks]
        if index == 0:
            done, sends = work(*inputs)
        if index == len(stages) - 1:
            received = swap_faces(sends)
        value = add(parts)
        value, done, sends = lax.optimization_barrier((value, done, sends))
    return value, from_mask(value, "gy", 1), received, done


def plain(parts):
    value = parts[0] + parts[1]
    return value + (parts[2] + parts[3]) if len(parts) == 4 else value


def rescaled(power, parts):
    cases = parts[0].shape[0] - PAD
    scales = [part[cases:] for part in parts]
    scale = functools.reduce(jnp.minimum, scales)
    ready = []
    for part, own in zip(parts, scales):
        ratio = (scale / own)[:1]
        factor = jnp.where(power == 0.0, 1.0, jnp.where(power == 1.0, ratio, ratio * ratio))
        ready.append(part[:cases] * factor)
    return jnp.concatenate([plain(ready), scale], axis=0)


def local(right_side, weights, signs, face_map, pattern, factor):
    cases, size = right_side.shape[1:]
    blocks = pattern.shape[1]
    place = jnp.stack(
        [
            lax.axis_index("gx"),
            lax.axis_index("gy"),
            jnp.int32(lax.axis_size("gx")),
            jnp.int32(lax.axis_size("gy")),
        ]
    )
    field, padded = (cases, size), (cases + PAD, size)
    face, padded_face = (cases, size // 4), (cases + PAD, size // 4)
    half_type = ((size, size), jnp.bfloat16)

    work = 6 * cases * size * size
    (pick,) = call(pick_kernel, "pick", [half_type], face_map, smem=0, flops=20 * work)
    small, *sends = call(
        start_kernel, "start_fields", [padded] + [padded_face] * 4,
        place, right_side[0], weights, signs, face_map, pick,
    )
    received = swap_faces(sends)
    high, low = call(
        functools.partial(factor_kernel, blocks), "masked_factor", [half_type] * 2,
        pattern[0], factor[0], face_map,
        scratch=[pltpu.VMEM((size, size), jnp.bfloat16)] * 2,
        smem=0,
    )
    ghosts, half0, out0, *sends = call(
        first_kernel, "first_operator", [padded, field, field] + [face] * 4,
        place, small, *received, high, low,
    )
    received = swap_faces(sends)
    image0, ghost_image0, second, keep, send, power = call(
        gram_kernel, "first_gram",
        [field, field, padded] + [(cases + PAD, 2 * cases)] * 2 + [(1, 2 * cases)],
        place, small, ghosts, half0, out0, *received, high, low,
    )

    def lift(second):
        out, *sends = call(
            lift_kernel, "second_operator", [field] + [padded_face] * 4,
            place, small, second, high, low,
        )
        return out, sends

    mine, other, faces, out1 = sum_over_devices(
        keep, send, functools.partial(rescaled, power), lift, (second,)
    )
    steps, inverse = call(
        solve_kernel, "first_solve", [(cases, 2 * cases), (2 * cases, 2 * cases)],
        place, mine, other,
    )
    state, image1, next_half0, next_out0, *next_sends = call(
        step_kernel, "first_step", [field] * 4 + [face] * 4,
        place, small, ghosts, mine, steps, image0, ghost_image0, second, out1,
        *faces, high, low,
    )
    inverse, next_sends = lax.optimization_barrier((inverse, next_sends))
    faces = swap_faces(next_sends)
    pick, gram_inverse = call(
        functools.partial(prepare_kernel, cases), "prepare_last",
        [half_type, (2 * cases, 2 * cases)], small, inverse, smem=0,
    )
    faces, pick, gram_inverse = lax.optimization_barrier((faces, pick, gram_inverse))
    next_image0, next_half1, keep, send = call(
        next_gram_kernel, "second_gram", [field, field] + [(3 * cases // 2, 2 * cases)] * 2,
        place, small, ghosts, mine, second, state, next_half0, next_out0, *faces, high, low,
    )

    def last_lift(half):
        out, *sends = call(
            next_lift_kernel, "last_operator", [field] + [face] * 4,
            place, small, half, high, low,
        )
        return out, sends

    next_mine, next_other, faces, next_out1 = sum_over_devices(
        keep, send, plain, last_lift, (next_half1,)
    )
    wide = (cases, 4 * cases)
    found, change = call(
        last_solve_kernel, "last_solve", [wide, wide],
        place, mine, next_mine, next_other, gram_inverse, steps,
    )
    answer, resid = call(
        last_kernel, "last_step", [field, field],
        place, small, mine, found, change, state, image0, image1, next_image0, next_out1,
        *faces, pick,
    )
    return (answer[None], resid[None])


def solution(mesh):
    return jax.shard_map(
        local,
        mesh=mesh,
        in_specs=(
            P("gx", None, "gy"),
            P("gx", "gy"),
            P("gx", "gy"),
            P("gx", "gy"),
            P("gx", None, "gy"),
            P("gx", None, "gy"),
        ),
        out_specs=(P("gx", None, "gy"), P("gx", None, "gy")),
        check_vma=False,
    )
```

```python
import functools

import jax
import jax.numpy as jnp
from jax import lax
from jax.experimental import pallas as pl
from jax.experimental.pallas import tpu as pltpu
from jax.sharding import PartitionSpec as P

HIGH = lax.Precision.HIGHEST
VMEM = pl.BlockSpec(memory_space=pltpu.VMEM)
SMEM = pl.BlockSpec(memory_space=pltpu.SMEM)
PAD = 8
SMALL = 1e-6
LANES = 128


def halves(value):
    high = value.astype(jnp.bfloat16)
    low = (value - high.astype(jnp.float32)).astype(jnp.bfloat16)
    return high, low


def thirds(value):
    high = value.astype(jnp.bfloat16)
    rest = value - high.astype(jnp.float32)
    middle = rest.astype(jnp.bfloat16)
    low = (rest - middle.astype(jnp.float32)).astype(jnp.bfloat16)
    return jnp.concatenate([high, middle, low], axis=0)


def bf16_dot(left, right, right_dim):
    return lax.dot_general(
        left, right, (((1,), (right_dim,)), ((), ())), preferred_element_type=jnp.float32
    )


def exact_pick(value, pick):
    rows = value.shape[0]
    parts = bf16_dot(thirds(value), pick, 0)
    return parts[:rows] + (parts[rows : 2 * rows] + parts[2 * rows :])


def product(value, high, low, dim):
    rows = value.shape[0]
    value_high, value_low = halves(value)
    both = bf16_dot(jnp.concatenate([value_high, value_low], axis=0), high[...], dim)
    return both[:rows] + (both[rows:] + bf16_dot(value_high, low[...], dim))


def inner_prod(left, right):
    return lax.dot_general(
        left, right, (((1,), (1,)), ((), ())), precision=HIGH, preferred_element_type=jnp.float32
    )


def times(left, right):
    return jnp.dot(left, right, precision=HIGH, preferred_element_type=jnp.float32)


def row_to_square(row, size):
    return jnp.broadcast_to(row, (LANES, size)).T


def pick_columns(face_row):
    size = face_row.shape[1]
    unknown = lax.broadcasted_iota(jnp.int32, (size, size), 0)
    return jnp.where(unknown == face_row, 1.0, 0.0).astype(jnp.bfloat16)


def pick_rows(face_row):
    size = face_row.shape[1]
    face = row_to_square(face_row, size)
    lane = lax.broadcasted_iota(jnp.int32, (size, LANES), 1)
    return jnp.concatenate(
        [
            jnp.where(face == lane + start, 1.0, 0.0).astype(jnp.bfloat16)
            for start in range(0, size, LANES)
        ],
        axis=1,
    )


def faces_of(field):
    face_len = field.shape[1] // 4
    return [field[:, face * face_len : (face + 1) * face_len] for face in range(4)]


def write_packed(out, face):
    rows = face.shape[0]
    if out.shape == face.shape:
        out[...] = face
    else:
        for index in range(face.shape[1] // LANES):
            out[index * rows : (index + 1) * rows] = face[:, index * LANES : (index + 1) * LANES]


def read_packed(ref, shape):
    if ref.shape == shape:
        return ref[...]
    rows, count = shape[0], shape[1] // LANES
    first = ref.shape[0] - count * rows
    return jnp.concatenate(
        [ref[first + index * rows : first + (index + 1) * rows] for index in range(count)], axis=1
    )


def write_faces(place, field, outs):
    north, south, west, east = faces_of(field)
    even_x, even_y = place[0] % 2 == 0, place[1] % 2 == 0
    write_packed(outs[0], jnp.where(even_x, south, north))
    write_packed(outs[1], jnp.where(even_x, north, south))
    outs[2][...] = jnp.where(even_y, east, west)
    outs[3][...] = jnp.where(even_y, west, east)


def read_faces(place, received):
    shape = received[2].shape
    x_first, x_second, y_first, y_second = [read_packed(one, shape) for one in received]
    even_x, even_y = place[0] % 2 == 0, place[1] % 2 == 0
    north = jnp.where(place[0] > 0, jnp.where(even_x, x_second, x_first), 0.0)
    south = jnp.where(place[0] + 1 < place[2], jnp.where(even_x, x_first, x_second), 0.0)
    west = jnp.where(place[1] > 0, jnp.where(even_y, y_second, y_first), 0.0)
    east = jnp.where(place[1] + 1 < place[3], jnp.where(even_y, y_first, y_second), 0.0)
    return jnp.concatenate([north, south, west, east], axis=1)


def rows_of(small, cases):
    return small[:cases], small[cases : cases + 1], small[cases + 1 : cases + 2]


def images_of(out, signed_ghost, jump, ghost_jump):
    image = out + 0.5 * signed_ghost
    ghost = ghost_jump * signed_ghost + (0.5 * jump * jnp.abs(ghost_jump)) * out
    return image, ghost


def inverse_of(matrix):
    size = matrix.shape[0]
    eye = lax.broadcasted_iota(jnp.int32, matrix.shape, 0) == lax.broadcasted_iota(
        jnp.int32, matrix.shape, 1
    )
    diagonal = jnp.where(eye, matrix, 0.0)
    by_row = lax.rsqrt(jnp.sum(diagonal, axis=1, keepdims=True))
    by_column = lax.rsqrt(jnp.sum(diagonal, axis=0, keepdims=True))
    scaled = matrix * by_row * by_column
    bound = jnp.max(jnp.sum(jnp.abs(scaled), axis=0, keepdims=True), axis=1, keepdims=True)
    square = jnp.sum(jnp.sum(scaled * scaled, axis=0, keepdims=True), axis=1, keepdims=True)
    one = jnp.where(eye, 1.0, 0.0)

    def again(state):
        _, before, now, count = state
        return (now > SMALL) & ((now < before) | (now > 1.0)) & (count < 64)

    def better(state):
        x, _, now, count = state
        left = one - times(scaled, x)
        twice = times(left, left)
        nearer = x + times(x, left)
        return nearer + times(nearer, twice), now, jnp.sum(twice * twice), count + 1

    start = one * jnp.minimum(size / square, 1.9 / bound)
    large = jnp.float32(4 * size)
    state = better(better((start, large, large, jnp.int32(0))))
    x, _, _, _ = lax.while_loop(again, better, state)
    return x * by_row * by_column


def solve_halves(a00, a01, a11, b0, b1):
    size = a00.shape[0]
    first = inverse_of(a00)
    both = times(first, jnp.concatenate([a01, b0], axis=1))
    along, part = both[:, :size], both[:, size:]
    taken = times(a01.T, both)
    second = inverse_of(a11 - taken[:, :size])
    x1 = times(second, b1 - taken[:, size:])
    return first, along, second, part - times(along, x1), x1


def pick_kernel(faces, pick):
    pick[...] = pick_columns(faces[...])


def start_kernel(place, loads, weights, signs, faces, pick, small, *sends):
    cases, size = loads.shape
    jump = (2 * signs[...] - 1).astype(jnp.float32)
    more = jnp.concatenate(
        [weights[...], jump, jnp.zeros((PAD - 2, size), jnp.float32)], axis=0
    )
    value = exact_pick(jnp.concatenate([loads[...], more], axis=0), pick[...])
    write_faces(place, value, sends)
    small[...] = value
    small[cases + 2 : cases + 3] = faces[...].astype(jnp.float32)


def face_row(small, cases):
    return small[cases + 2 : cases + 3].astype(jnp.int32)


def factor_kernel(blocks, pattern, factor, faces, high, low, masked_high, masked_low):
    size = factor.shape[0]
    length = size // blocks
    for i in range(blocks):
        for j in range(blocks):
            rows, columns = pl.ds(i * length, length), pl.ds(j * length, length)
            value = factor[rows, columns]
            if i != j:
                keep = jnp.broadcast_to(pattern[i : i + 1, j : j + 1], value.shape)
                value = jnp.where(keep == 1, value, 0.0)
            masked_high[rows, columns], masked_low[rows, columns] = halves(value)
    pick = pick_rows(faces[...])
    chunk = size // 4
    for masked, out in ((masked_high, high), (masked_low, low)):
        for start in range(0, size, chunk):
            out[start : start + chunk] = bf16_dot(
                pick[start : start + chunk], masked[...], 0
            ).astype(jnp.bfloat16)


def prepare_kernel(cases, small, inverse, pick, gram_inverse):
    pick[...] = pick_rows(face_row(small, cases))
    first, second = inverse[:cases], inverse[cases:]
    beside, lower = first[:, cases:], second[:, :cases]
    corner = -times(beside, lower)
    gram_inverse[:cases, :cases] = first[:, :cases] - times(corner, beside.T)
    gram_inverse[:cases, cases:] = corner
    gram_inverse[cases:, :cases] = corner.T
    gram_inverse[cases:, cases:] = lower


def split_sums(place, first, second, more, keep, send):
    even = place[1] % 2 == 0
    rows = first.shape[0]
    keep[:rows] = jnp.where(even, first, second)
    send[:rows] = jnp.where(even, second, first)
    if more is not None:
        keep[rows:] = more
        send[rows:] = more


def join_sums(place, mine, other):
    even = place[1] % 2 == 0
    mine, other = mine[...], other[...]
    return jnp.where(even, mine, other), jnp.where(even, other, mine)


def first_kernel(place, small, x0, x1, y0, y1, high, low, ghosts, half, out, *sends):
    value, ghost = small[...], read_faces(place, (x0, x1, y0, y1))
    ghosts[...] = ghost
    cases = half.shape[0]
    resid, weighting, jump = rows_of(value, cases)
    ghost_resid, ghost_weighting, _ = rows_of(ghost, cases)
    field = weighting * resid + (0.5 * jump) * (ghost_weighting * ghost_resid)
    halfway = product(field, high, low, 0)
    half[...] = halfway
    lifted = product(halfway, high, low, 1)
    out[...] = lifted
    write_faces(place, jump * lifted, sends)


def gram_kernel(
    place, small, ghosts, half, out, x0, x1, y0, y1, high, low, image, ghost_image, second, keep, send, power
):
    cases = half.shape[0]
    resid, weighting, jump = rows_of(small[...], cases)
    _, ghost_weighting, ghost_jump = rows_of(ghosts[...], cases)
    own, ghost = images_of(out[...], read_faces(place, (x0, x1, y0, y1)), jump, ghost_jump)
    image[...] = own
    ghost_image[...] = ghost
    field = weighting * own + (0.5 * jump) * (ghost_weighting * ghost)
    largest = jnp.max(jnp.max(jnp.abs(field), axis=1, keepdims=True), axis=0, keepdims=True)
    scale = 1.0 / jnp.maximum(largest, 1e-30)
    second_half = product(field * scale, high, low, 0)
    second[:cases] = second_half
    second[cases:] = jnp.broadcast_to(scale, (PAD, field.shape[1]))
    first_half = half[...]
    cross = inner_prod(second_half, jnp.concatenate([first_half, second_half], axis=0))
    split_sums(
        place,
        jnp.concatenate(
            [inner_prod(first_half, first_half), inner_prod(weighting * resid, resid)], axis=1
        ),
        jnp.concatenate([cross[:, :cases].T, cross[:, cases:]], axis=1),
        jnp.broadcast_to(scale, (PAD, 2 * cases)),
        keep,
        send,
    )
    lane = lax.broadcasted_iota(jnp.int32, (1, 2 * cases), 1)
    scaled = jnp.where(lane < cases, 1.0, 2.0)
    power[...] = jnp.where(place[1] % 2 == 0, jnp.zeros_like(scaled), scaled)


def lift_kernel(place, small, second, high, low, out, *sends):
    cases = out.shape[0]
    jump = small[cases + 1 : cases + 2]
    lifted = product(second[:cases], high, low, 1)
    out[...] = lifted
    write_faces(place, jnp.concatenate([jump * lifted, second[cases:]], axis=0), sends)


def solve_kernel(place, mine, other, steps, inverse):
    cases = steps.shape[0]
    scale = mine[cases : cases + 1, :1]
    top, bottom = join_sums(place, mine, other)
    gram00, gram01, gram11 = top[:cases, :cases], bottom[:cases, :cases], bottom[:cases, cases:]
    first, along, corner, steps0, steps1 = solve_halves(
        gram00, gram01, gram11, top[:cases, cases:], scale * gram00
    )
    inverse[:cases, :cases] = first
    inverse[:cases, cases:] = along
    inverse[cases:, :cases] = corner
    inverse[cases:, cases:] = corner
    steps[...] = jnp.concatenate([steps0, steps1], axis=0).T


def step_kernel(
    place, small, ghosts, mine, steps, image0, ghost_image0, second, out1, x0, x1, y0, y1,
    high, low, state, image1, half, out, *sends
):
    cases = half.shape[0]
    resid, weighting, jump = rows_of(small[...], cases)
    ghost_resid, ghost_weighting, ghost_jump = rows_of(ghosts[...], cases)
    scale = mine[cases : cases + 1, :1]
    received = read_faces(place, (x0, x1, y0, y1))
    own_ratio = scale / second[cases : cases + 1]
    there = received[cases : cases + 1]
    ghost_ratio = jnp.where(there > 0.0, scale / jnp.where(there > 0.0, there, 1.0), 0.0)
    own1, ghost1 = images_of(
        out1[...] * own_ratio, received[:cases] * ghost_ratio, jump, ghost_jump
    )
    image1[...] = own1
    resid = resid - times(steps[...], jnp.concatenate([image0[...], own1], axis=0))
    ghost_resid = ghost_resid - times(
        steps[...], jnp.concatenate([ghost_image0[...], ghost1], axis=0)
    )
    state[...] = resid
    field = weighting * resid + (0.5 * jump) * (ghost_weighting * ghost_resid)
    halfway = product(field, high, low, 0)
    half[...] = halfway
    lifted = product(halfway, high, low, 1)
    out[...] = lifted
    write_faces(place, jump * lifted, sends)


def next_gram_kernel(
    place, small, ghosts, mine, second, state, half, out, x0, x1, y0, y1, high, low,
    image, next_half, keep, send
):
    cases = half.shape[0]
    _, weighting, jump = rows_of(small[...], cases)
    _, ghost_weighting, ghost_jump = rows_of(ghosts[...], cases)
    scale = mine[cases : cases + 1, :1]
    own, ghost = images_of(out[...], read_faces(place, (x0, x1, y0, y1)), jump, ghost_jump)
    image[...] = own
    field = scale * (weighting * own + (0.5 * jump) * (ghost_weighting * ghost))
    halfway = product(field, high, low, 0)
    next_half[...] = halfway
    before = second[:cases] * (scale / second[cases : cases + 1])
    both = jnp.concatenate([half[...], halfway], axis=0)
    cross = inner_prod(jnp.concatenate([before, both], axis=0), both)
    resid = state[...]
    total = jnp.concatenate(
        [
            cross[: 2 * cases],
            jnp.concatenate(
                [inner_prod(weighting * resid, resid), cross[2 * cases :, cases:]], axis=1
            ),
        ],
        axis=0,
    )
    middle = total.shape[0] // 2
    split_sums(place, total[:middle], total[middle:], None, keep, send)


def next_lift_kernel(place, small, half, high, low, out, *sends):
    cases = out.shape[0]
    lifted = product(half[...], high, low, 1)
    out[...] = lifted
    write_faces(place, small[cases + 1 : cases + 2] * lifted, sends)


def last_solve_kernel(place, first_sums, mine, other, gram_inverse, steps, answer, change):
    cases = steps.shape[0]
    scale = first_sums[cases : cases + 1, :1]
    total = jnp.concatenate(join_sums(place, mine, other), axis=0)
    along = jnp.concatenate(
        [
            jnp.concatenate([jnp.zeros((cases, cases), jnp.float32), total[:cases, :cases]], axis=1),
            total[:cases],
        ],
        axis=0,
    )
    conjugating = times(gram_inverse[...], along)
    taken = times(along.T, conjugating)
    gram00 = total[cases : 2 * cases, :cases]
    _, _, _, next0, next1 = solve_halves(
        gram00 - taken[:cases, :cases],
        total[cases : 2 * cases, cases:] - taken[:cases, cases:],
        total[2 * cases :, cases:] - taken[cases:, cases:],
        total[2 * cases :, :cases],
        scale * gram00,
    )
    next_steps = jnp.concatenate([next0, next1], axis=0)
    old_steps = -times(conjugating, next_steps).T
    next_steps = next_steps.T
    answer[...] = jnp.concatenate([steps[...] + old_steps, next_steps], axis=1)
    change[...] = jnp.concatenate([old_steps, next_steps], axis=1)


def last_kernel(
    place, small, first_sums, answer, change, state, image0, image1, next_image0, out1,
    x0, x1, y0, y1, pick, solution_out, resid_out
):
    cases = image0.shape[0]
    first_resid, weighting, _ = rows_of(small[...], cases)
    scale = first_sums[cases : cases + 1, :1]
    next_image1 = out1[...] + 0.5 * read_faces(place, (x0, x1, y0, y1))
    images = jnp.concatenate(
        [image0[...], image1[...], next_image0[...], next_image1], axis=0
    )
    resid = state[...] - times(change[...], images)
    fields = weighting * jnp.concatenate(
        [first_resid, scale * image0[...], state[...], scale * next_image0[...]], axis=0
    )
    found = times(answer[...], fields)
    both = exact_pick(jnp.concatenate([found, resid], axis=0), pick[...])
    solution_out[...] = both[:cases]
    resid_out[...] = both[cases:]


def call(kernel, name, outs, *operands, scratch=(), mebibytes=8, smem=1, flops=0):
    shapes = [
        jax.ShapeDtypeStruct(one[0], one[1]) if isinstance(one[0], tuple)
        else jax.ShapeDtypeStruct(one, jnp.float32)
        for one in outs
    ]
    touched = sum(one.size * one.dtype.itemsize for one in (*operands, *shapes))
    cost = pl.CostEstimate(flops=flops, bytes_accessed=touched, transcendentals=0)
    return pl.pallas_call(
        kernel,
        out_shape=shapes,
        in_specs=[SMEM] * smem + [VMEM] * (len(operands) - smem),
        out_specs=[VMEM] * len(shapes),
        scratch_shapes=list(scratch),
        compiler_params=pltpu.CompilerParams(vmem_limit_bytes=mebibytes * 2**20),
        cost_estimate=cost if flops else None,
        name=name,
    )(*operands)


def swap_pairs(rows, columns, along, parity):
    pairs = []
    for x in range(rows):
        for y in range(columns):
            index, count = (x, rows) if along == "gx" else (y, columns)
            other = index + 1 if index % 2 == parity else index - 1
            if 0 <= other < count:
                target = (other, y) if along == "gx" else (x, other)
            else:
                target = (x, y ^ 1) if along == "gx" else (x ^ 1, y)
                if not (target[0] < rows and target[1] < columns):
                    target = (x, y)
            pairs.append((x * columns + y, target[0] * columns + target[1]))
    return pairs


FACES = (("gx", 0), ("gx", 1), ("gy", 0), ("gy", 1))


def swap_face(send, along, parity):
    pairs = swap_pairs(lax.axis_size("gx"), lax.axis_size("gy"), along, parity)
    return lax.ppermute(send, ("gx", "gy"), pairs)


def swap_faces(sends):
    return [swap_face(send, *face) for send, face in zip(sends, FACES)]


def stage_masks(axis, first):
    count = lax.axis_size(axis)
    stages = []
    step = first
    while step < count:
        last = step * 2 >= count
        stages.append((axis, (step,) if last else (step, 2 * step, 3 * step)))
        step *= 4
    return stages


def from_mask(value, axis, mask):
    count = lax.axis_size(axis)
    return lax.ppermute(value, axis, [(source, source ^ mask) for source in range(count)])


def carriers(count, masks):
    found = {}
    for parity in (0, 1):
        for mask in masks:
            reaches = all(low ^ mask == low + 1 for low in range(parity, count - 1, 2))
            if reaches and mask not in found:
                found[mask] = parity
                break
    return found


def sum_over_devices(keep, send, add, work, inputs):
    value = add([keep, from_mask(send, "gy", 1)])
    stages = stage_masks("gy", 2) + stage_masks("gx", 1)
    done, sends, received = (), (), None
    for index, (axis, masks) in enumerate(stages):
        value, inputs, sends = lax.optimization_barrier((value, inputs, sends))
        carried = {}
        if axis == "gx" and received is None and index > 0:
            carried = carriers(lax.axis_size(axis), masks)
            received = {}
        parts = [value]
        for mask in masks:
            if mask in carried:
                parity = carried[mask]
                both = from_mask(jnp.concatenate([value, sends[parity]], axis=0), axis, mask)
                received[parity] = both
                parts.append(both[: value.shape[0]])
            else:
                parts.append(from_mask(value, axis, mask))
        if index == 0:
            done, sends = work(*inputs)
        if received is not None:
            for slot, (one, face) in enumerate(zip(sends, FACES)):
                if slot not in received:
                    received[slot] = swap_face(one, *face)
        value = add(parts)
        value, done, sends = lax.optimization_barrier((value, done, sends))
    if received is None:
        received = dict(enumerate(swap_faces(sends)))
    faces = [received[slot] for slot in range(len(FACES))]
    return value, from_mask(value, "gy", 1), faces, done


def plain(parts):
    value = parts[0] + parts[1]
    return value + (parts[2] + parts[3]) if len(parts) == 4 else value


def rescaled(power, parts):
    cases = parts[0].shape[0] - PAD
    scales = [part[cases:] for part in parts]
    scale = functools.reduce(jnp.minimum, scales)
    ready = []
    for part, own in zip(parts, scales):
        ratio = (scale / own)[:1]
        factor = jnp.where(power == 0.0, 1.0, jnp.where(power == 1.0, ratio, ratio * ratio))
        ready.append(part[:cases] * factor)
    return jnp.concatenate([plain(ready), scale], axis=0)


def local(right_side, weights, signs, face_map, pattern, factor):
    cases, size = right_side.shape[1:]
    blocks = pattern.shape[1]
    place = jnp.stack(
        [
            lax.axis_index("gx"),
            lax.axis_index("gy"),
            jnp.int32(lax.axis_size("gx")),
            jnp.int32(lax.axis_size("gy")),
        ]
    )
    field, padded = (cases, size), (cases + PAD, size)
    face, padded_face = (cases, size // 4), (cases + PAD, size // 4)
    half_type = ((size, size), jnp.bfloat16)
    narrow = lambda shape: (shape[0] * shape[1] // LANES, LANES)

    work = 6 * cases * size * size
    (pick,) = call(pick_kernel, "pick", [half_type], face_map, smem=0, flops=20 * work)
    small, *sends = call(
        start_kernel, "start_fields", [padded] + [padded_face] * 4,
        place, right_side[0], weights, signs, face_map, pick,
    )
    received = swap_faces(sends)
    high, low = call(
        functools.partial(factor_kernel, blocks), "masked_factor", [half_type] * 2,
        pattern[0], factor[0], face_map,
        scratch=[pltpu.VMEM((size, size), jnp.bfloat16)] * 2,
        smem=0,
    )
    ghosts, half0, out0, *sends = call(
        first_kernel, "first_operator", [padded, field, field] + [face] * 4,
        place, small, *received, high, low,
    )
    received = swap_faces(sends)
    image0, ghost_image0, second, keep, send, power = call(
        gram_kernel, "first_gram",
        [field, field, padded] + [(cases + PAD, 2 * cases)] * 2 + [(1, 2 * cases)],
        place, small, ghosts, half0, out0, *received, high, low,
    )

    def lift(second):
        out, *sends = call(
            lift_kernel, "second_operator",
            [field] + [narrow(padded_face)] * 2 + [padded_face] * 2,
            place, small, second, high, low,
        )
        return out, sends

    mine, other, faces, out1 = sum_over_devices(
        keep, send, functools.partial(rescaled, power), lift, (second,)
    )
    steps, inverse = call(
        solve_kernel, "first_solve", [(cases, 2 * cases), (2 * cases, 2 * cases)],
        place, mine, other,
    )
    state, image1, next_half0, next_out0, *next_sends = call(
        step_kernel, "first_step", [field] * 4 + [face] * 4,
        place, small, ghosts, mine, steps, image0, ghost_image0, second, out1,
        *faces, high, low,
    )
    inverse, next_sends = lax.optimization_barrier((inverse, next_sends))
    faces = swap_faces(next_sends)
    pick, gram_inverse = call(
        functools.partial(prepare_kernel, cases), "prepare_last",
        [half_type, (2 * cases, 2 * cases)], small, inverse, smem=0,
    )
    faces, pick, gram_inverse = lax.optimization_barrier((faces, pick, gram_inverse))
    next_image0, next_half1, keep, send = call(
        next_gram_kernel, "second_gram", [field, field] + [(3 * cases // 2, 2 * cases)] * 2,
        place, small, ghosts, mine, second, state, next_half0, next_out0, *faces, high, low,
    )

    def last_lift(half):
        out, *sends = call(
            next_lift_kernel, "last_operator", [field] + [narrow(face)] * 2 + [face] * 2,
            place, small, half, high, low,
        )
        return out, sends

    next_mine, next_other, faces, next_out1 = sum_over_devices(
        keep, send, plain, last_lift, (next_half1,)
    )
    wide = (cases, 4 * cases)
    found, change = call(
        last_solve_kernel, "last_solve", [wide, wide],
        place, mine, next_mine, next_other, gram_inverse, steps,
    )
    answer, resid = call(
        last_kernel, "last_step", [field, field],
        place, small, mine, found, change, state, image0, image1, next_image0, next_out1,
        *faces, pick,
    )
    return (answer[None], resid[None])


def solution(mesh):
    return jax.shard_map(
        local,
        mesh=mesh,
        in_specs=(
            P("gx", None, "gy"),
            P("gx", "gy"),
            P("gx", "gy"),
            P("gx", "gy"),
            P("gx", None, "gy"),
            P("gx", None, "gy"),
        ),
        out_specs=(P("gx", None, "gy"), P("gx", None, "gy")),
        check_vma=False,
    )
```

```python
import functools

import jax
import jax.numpy as jnp
from jax import lax
from jax.experimental import pallas as pl
from jax.experimental.pallas import tpu as pltpu
from jax.sharding import PartitionSpec as P

HIGH = lax.Precision.HIGHEST
VMEM = pl.BlockSpec(memory_space=pltpu.VMEM)
SMEM = pl.BlockSpec(memory_space=pltpu.SMEM)
PAD = 8
SMALL = 1e-6
LANES = 128


def halves(value):
    high = value.astype(jnp.bfloat16)
    low = (value - high.astype(jnp.float32)).astype(jnp.bfloat16)
    return high, low


def thirds(value):
    high = value.astype(jnp.bfloat16)
    rest = value - high.astype(jnp.float32)
    middle = rest.astype(jnp.bfloat16)
    low = (rest - middle.astype(jnp.float32)).astype(jnp.bfloat16)
    return jnp.concatenate([high, middle, low], axis=0)


def bf16_dot(left, right, right_dim):
    return lax.dot_general(
        left, right, (((1,), (right_dim,)), ((), ())), preferred_element_type=jnp.float32
    )


def exact_pick(value, pick):
    rows = value.shape[0]
    parts = bf16_dot(thirds(value), pick, 0)
    return parts[:rows] + (parts[rows : 2 * rows] + parts[2 * rows :])


def product(value, high, low, dim):
    rows = value.shape[0]
    value_high, value_low = halves(value)
    both = bf16_dot(jnp.concatenate([value_high, value_low], axis=0), high[...], dim)
    return both[:rows] + (both[rows:] + bf16_dot(value_high, low[...], dim))


def inner_prod(left, right):
    return lax.dot_general(
        left, right, (((1,), (1,)), ((), ())), precision=HIGH, preferred_element_type=jnp.float32
    )


def times(left, right):
    return jnp.dot(left, right, precision=HIGH, preferred_element_type=jnp.float32)


def row_to_square(row, size):
    return jnp.broadcast_to(row, (LANES, size)).T


def pick_columns(face_row):
    size = face_row.shape[1]
    unknown = lax.broadcasted_iota(jnp.int32, (size, size), 0)
    return jnp.where(unknown == face_row, 1.0, 0.0).astype(jnp.bfloat16)


def pick_rows(face_row):
    size = face_row.shape[1]
    face = row_to_square(face_row, size)
    lane = lax.broadcasted_iota(jnp.int32, (size, LANES), 1)
    return jnp.concatenate(
        [
            jnp.where(face == lane + start, 1.0, 0.0).astype(jnp.bfloat16)
            for start in range(0, size, LANES)
        ],
        axis=1,
    )


def faces_of(field):
    face_len = field.shape[1] // 4
    return [field[:, face * face_len : (face + 1) * face_len] for face in range(4)]


def write_faces(place, field, outs):
    north, south, west, east = faces_of(field)
    even_x, even_y = place[0] % 2 == 0, place[1] % 2 == 0
    outs[0][...] = jnp.where(even_x, south, north)
    outs[1][...] = jnp.where(even_x, north, south)
    outs[2][...] = jnp.where(even_y, east, west)
    outs[3][...] = jnp.where(even_y, west, east)


def read_faces(place, received):
    x_first, x_second, y_first, y_second = [one[...] for one in received]
    even_x, even_y = place[0] % 2 == 0, place[1] % 2 == 0
    north = jnp.where(place[0] > 0, jnp.where(even_x, x_second, x_first), 0.0)
    south = jnp.where(place[0] + 1 < place[2], jnp.where(even_x, x_first, x_second), 0.0)
    west = jnp.where(place[1] > 0, jnp.where(even_y, y_second, y_first), 0.0)
    east = jnp.where(place[1] + 1 < place[3], jnp.where(even_y, y_first, y_second), 0.0)
    return jnp.concatenate([north, south, west, east], axis=1)


def rows_of(small, cases):
    return small[:cases], small[cases : cases + 1], small[cases + 1 : cases + 2]


def images_of(out, signed_ghost, jump, ghost_jump):
    image = out + 0.5 * signed_ghost
    ghost = ghost_jump * signed_ghost + (0.5 * jump * jnp.abs(ghost_jump)) * out
    return image, ghost


def inverse_of(matrix):
    size = matrix.shape[0]
    eye = lax.broadcasted_iota(jnp.int32, matrix.shape, 0) == lax.broadcasted_iota(
        jnp.int32, matrix.shape, 1
    )
    diagonal = jnp.where(eye, matrix, 0.0)
    by_row = lax.rsqrt(jnp.sum(diagonal, axis=1, keepdims=True))
    by_column = lax.rsqrt(jnp.sum(diagonal, axis=0, keepdims=True))
    scaled = matrix * by_row * by_column
    bound = jnp.max(jnp.sum(jnp.abs(scaled), axis=0, keepdims=True), axis=1, keepdims=True)
    square = jnp.sum(jnp.sum(scaled * scaled, axis=0, keepdims=True), axis=1, keepdims=True)
    one = jnp.where(eye, 1.0, 0.0)

    def again(state):
        _, before, now, count = state
        return (now > SMALL) & ((now < before) | (now > 1.0)) & (count < 64)

    def better(state):
        x, _, now, count = state
        left = one - times(scaled, x)
        twice = times(left, left)
        nearer = x + times(x, left)
        return nearer + times(nearer, twice), now, jnp.sum(twice * twice), count + 1

    start = jnp.minimum(size / square, 1.9 / bound)
    left = one - start * scaled
    twice = times(left, left)
    nearer = one + left
    x = start * (nearer + times(nearer, twice))
    large = jnp.float32(4 * size)
    state = better((x, large, large, jnp.int32(1)))
    x, _, _, _ = lax.while_loop(again, better, state)
    return x * by_row * by_column


def solve_halves(a00, a01, a11, b0, b1):
    size = a00.shape[0]
    first = inverse_of(a00)
    both = times(first, jnp.concatenate([a01, b0], axis=1))
    along, part = both[:, :size], both[:, size:]
    taken = times(a01.T, both)
    second = inverse_of(a11 - taken[:, :size])
    x1 = times(second, b1 - taken[:, size:])
    return first, along, second, part - times(along, x1), x1


def pick_kernel(faces, pick):
    pick[...] = pick_columns(faces[...])


def start_kernel(place, loads, weights, signs, faces, pick, small, *sends):
    cases, size = loads.shape
    jump = (2 * signs[...] - 1).astype(jnp.float32)
    more = jnp.concatenate(
        [weights[...], jump, jnp.zeros((PAD - 2, size), jnp.float32)], axis=0
    )
    value = exact_pick(jnp.concatenate([loads[...], more], axis=0), pick[...])
    write_faces(place, value, sends)
    small[...] = value
    small[cases + 2 : cases + 3] = faces[...].astype(jnp.float32)


def face_row(small, cases):
    return small[cases + 2 : cases + 3].astype(jnp.int32)


def factor_kernel(blocks, pattern, factor, faces, high, low, masked_high, masked_low):
    size = factor.shape[0]
    length = size // blocks
    for i in range(blocks):
        for j in range(blocks):
            rows, columns = pl.ds(i * length, length), pl.ds(j * length, length)
            value = factor[rows, columns]
            if i != j:
                keep = jnp.broadcast_to(pattern[i : i + 1, j : j + 1], value.shape)
                value = jnp.where(keep == 1, value, 0.0)
            masked_high[rows, columns], masked_low[rows, columns] = halves(value)
    pick = pick_rows(faces[...])
    chunk = size // 4
    for masked, out in ((masked_high, high), (masked_low, low)):
        for start in range(0, size, chunk):
            out[start : start + chunk] = bf16_dot(
                pick[start : start + chunk], masked[...], 0
            ).astype(jnp.bfloat16)


def prepare_kernel(cases, small, inverse, pick, gram_inverse):
    pick[...] = pick_rows(face_row(small, cases))
    first, second = inverse[:cases], inverse[cases:]
    beside, lower = first[:, cases:], second[:, :cases]
    corner = -times(beside, lower)
    gram_inverse[:cases, :cases] = first[:, :cases] - times(corner, beside.T)
    gram_inverse[:cases, cases:] = corner
    gram_inverse[cases:, :cases] = corner.T
    gram_inverse[cases:, cases:] = lower


def split_sums(place, first, second, more, keep, send):
    even = place[1] % 2 == 0
    rows = first.shape[0]
    keep[:rows] = jnp.where(even, first, second)
    send[:rows] = jnp.where(even, second, first)
    if more is not None:
        keep[rows:] = more
        send[rows:] = more


def join_sums(place, mine, other):
    even = place[1] % 2 == 0
    mine, other = mine[...], other[...]
    return jnp.where(even, mine, other), jnp.where(even, other, mine)


def first_kernel(place, small, x0, x1, y0, y1, high, low, ghosts, half, out, *sends):
    value, ghost = small[...], read_faces(place, (x0, x1, y0, y1))
    ghosts[...] = ghost
    cases = half.shape[0]
    resid, weighting, jump = rows_of(value, cases)
    ghost_resid, ghost_weighting, _ = rows_of(ghost, cases)
    field = weighting * resid + (0.5 * jump) * (ghost_weighting * ghost_resid)
    halfway = product(field, high, low, 0)
    half[...] = halfway
    lifted = product(halfway, high, low, 1)
    out[...] = lifted
    write_faces(place, jump * lifted, sends)


def early_gram_kernel(small, half, top):
    cases = half.shape[0]
    resid, weighting, _ = rows_of(small[...], cases)
    top[:, :cases] = inner_prod(half[...], half[...])
    top[:, cases:] = inner_prod(weighting * resid, resid)


def gram_kernel(
    place, small, ghosts, half, top, out, x0, x1, y0, y1, high, low, image, ghost_image, second, keep, send, power
):
    cases = half.shape[0]
    _, weighting, jump = rows_of(small[...], cases)
    _, ghost_weighting, ghost_jump = rows_of(ghosts[...], cases)
    own, ghost = images_of(out[...], read_faces(place, (x0, x1, y0, y1)), jump, ghost_jump)
    image[...] = own
    ghost_image[...] = ghost
    field = weighting * own + (0.5 * jump) * (ghost_weighting * ghost)
    largest = jnp.max(jnp.max(jnp.abs(field), axis=1, keepdims=True), axis=0, keepdims=True)
    scale = 1.0 / jnp.maximum(largest, 1e-30)
    second_half = product(field * scale, high, low, 0)
    second[:cases] = second_half
    second[cases:] = jnp.broadcast_to(scale, (PAD, field.shape[1]))
    first_half = half[...]
    cross = inner_prod(second_half, jnp.concatenate([first_half, second_half], axis=0))
    split_sums(
        place,
        top[...],
        jnp.concatenate([cross[:, :cases].T, cross[:, cases:]], axis=1),
        jnp.broadcast_to(scale, (PAD, 2 * cases)),
        keep,
        send,
    )
    lane = lax.broadcasted_iota(jnp.int32, (1, 2 * cases), 1)
    scaled = jnp.where(lane < cases, 1.0, 2.0)
    power[...] = jnp.where(place[1] % 2 == 0, jnp.zeros_like(scaled), scaled)


def lift_kernel(place, small, second, high, low, out, *sends):
    cases = out.shape[0]
    jump = small[cases + 1 : cases + 2]
    lifted = product(second[:cases], high, low, 1)
    out[...] = lifted
    write_faces(place, jnp.concatenate([jump * lifted, second[cases:]], axis=0), sends)


def solve_kernel(place, mine, other, steps, inverse):
    cases = steps.shape[0]
    scale = mine[cases : cases + 1, :1]
    top, bottom = join_sums(place, mine, other)
    gram00, gram01, gram11 = top[:cases, :cases], bottom[:cases, :cases], bottom[:cases, cases:]
    first, along, corner, steps0, steps1 = solve_halves(
        gram00, gram01, gram11, top[:cases, cases:], scale * gram00
    )
    inverse[:cases, :cases] = first
    inverse[:cases, cases:] = along
    inverse[cases:, :cases] = corner
    inverse[cases:, cases:] = corner
    steps[...] = jnp.concatenate([steps0, steps1], axis=0).T


def step_kernel(
    place, small, ghosts, mine, steps, image0, ghost_image0, second, out1, x0, x1, y0, y1,
    high, low, state, image1, half, out, *sends
):
    cases = half.shape[0]
    resid, weighting, jump = rows_of(small[...], cases)
    ghost_resid, ghost_weighting, ghost_jump = rows_of(ghosts[...], cases)
    scale = mine[cases : cases + 1, :1]
    received = read_faces(place, (x0, x1, y0, y1))
    own_ratio = scale / second[cases : cases + 1]
    there = received[cases : cases + 1]
    ghost_ratio = jnp.where(there > 0.0, scale / jnp.where(there > 0.0, there, 1.0), 0.0)
    own1, ghost1 = images_of(
        out1[...] * own_ratio, received[:cases] * ghost_ratio, jump, ghost_jump
    )
    image1[...] = own1
    resid = resid - times(steps[...], jnp.concatenate([image0[...], own1], axis=0))
    ghost_resid = ghost_resid - times(
        steps[...], jnp.concatenate([ghost_image0[...], ghost1], axis=0)
    )
    state[...] = resid
    field = weighting * resid + (0.5 * jump) * (ghost_weighting * ghost_resid)
    halfway = product(field, high, low, 0)
    half[...] = halfway
    lifted = product(halfway, high, low, 1)
    out[...] = lifted
    write_faces(place, jump * lifted, sends)


def next_early_gram_kernel(small, mine, second, state, half, left, before):
    cases = half.shape[0]
    _, weighting, _ = rows_of(small[...], cases)
    scale = mine[cases : cases + 1, :1]
    before[...] = second[:cases] * (scale / second[cases : cases + 1])
    left[: 2 * cases] = inner_prod(jnp.concatenate([before[...], half[...]], axis=0), half[...])
    left[2 * cases :] = inner_prod(weighting * state[...], state[...])


def next_gram_kernel(
    place, small, ghosts, mine, before, half, left, out, x0, x1, y0, y1, high, low,
    image, next_half, keep, send
):
    cases = half.shape[0]
    _, weighting, jump = rows_of(small[...], cases)
    _, ghost_weighting, ghost_jump = rows_of(ghosts[...], cases)
    scale = mine[cases : cases + 1, :1]
    own, ghost = images_of(out[...], read_faces(place, (x0, x1, y0, y1)), jump, ghost_jump)
    image[...] = own
    field = scale * (weighting * own + (0.5 * jump) * (ghost_weighting * ghost))
    halfway = product(field, high, low, 0)
    next_half[...] = halfway
    cross = inner_prod(jnp.concatenate([before[...], half[...], halfway], axis=0), halfway)
    total = jnp.concatenate([left[...], cross], axis=1)
    middle = total.shape[0] // 2
    split_sums(place, total[:middle], total[middle:], None, keep, send)


def next_lift_kernel(place, small, half, high, low, out, *sends):
    cases = out.shape[0]
    lifted = product(half[...], high, low, 1)
    out[...] = lifted
    write_faces(place, small[cases + 1 : cases + 2] * lifted, sends)


def last_solve_kernel(place, first_sums, mine, other, gram_inverse, steps, answer, change):
    cases = steps.shape[0]
    scale = first_sums[cases : cases + 1, :1]
    total = jnp.concatenate(join_sums(place, mine, other), axis=0)
    along = jnp.concatenate(
        [
            jnp.concatenate([jnp.zeros((cases, cases), jnp.float32), total[:cases, :cases]], axis=1),
            total[:cases],
        ],
        axis=0,
    )
    conjugating = times(gram_inverse[...], along)
    taken = times(along.T, conjugating)
    gram00 = total[cases : 2 * cases, :cases]
    _, _, _, next0, next1 = solve_halves(
        gram00 - taken[:cases, :cases],
        total[cases : 2 * cases, cases:] - taken[:cases, cases:],
        total[2 * cases :, cases:] - taken[cases:, cases:],
        total[2 * cases :, :cases],
        scale * gram00,
    )
    next_steps = jnp.concatenate([next0, next1], axis=0)
    old_steps = -times(conjugating, next_steps).T
    next_steps = next_steps.T
    answer[...] = jnp.concatenate([steps[...] + old_steps, next_steps], axis=1)
    change[...] = jnp.concatenate([old_steps, next_steps], axis=1)


def last_kernel(
    place, small, first_sums, answer, change, state, image0, image1, next_image0, out1,
    x0, x1, y0, y1, pick, solution_out, resid_out
):
    cases = image0.shape[0]
    first_resid, weighting, _ = rows_of(small[...], cases)
    scale = first_sums[cases : cases + 1, :1]
    next_image1 = out1[...] + 0.5 * read_faces(place, (x0, x1, y0, y1))
    images = jnp.concatenate(
        [image0[...], image1[...], next_image0[...], next_image1], axis=0
    )
    resid = state[...] - times(change[...], images)
    fields = weighting * jnp.concatenate(
        [first_resid, scale * image0[...], state[...], scale * next_image0[...]], axis=0
    )
    found = times(answer[...], fields)
    both = exact_pick(jnp.concatenate([found, resid], axis=0), pick[...])
    solution_out[...] = both[:cases]
    resid_out[...] = both[cases:]


def call(kernel, name, outs, *operands, scratch=(), mebibytes=8, smem=1, flops=0):
    shapes = [
        jax.ShapeDtypeStruct(one[0], one[1]) if isinstance(one[0], tuple)
        else jax.ShapeDtypeStruct(one, jnp.float32)
        for one in outs
    ]
    touched = sum(one.size * one.dtype.itemsize for one in (*operands, *shapes))
    cost = pl.CostEstimate(flops=flops, bytes_accessed=touched, transcendentals=0)
    return pl.pallas_call(
        kernel,
        out_shape=shapes,
        in_specs=[SMEM] * smem + [VMEM] * (len(operands) - smem),
        out_specs=[VMEM] * len(shapes),
        scratch_shapes=list(scratch),
        compiler_params=pltpu.CompilerParams(vmem_limit_bytes=mebibytes * 2**20),
        cost_estimate=cost if flops else None,
        name=name,
    )(*operands)


def swap_pairs(rows, columns, along, parity):
    pairs = []
    for x in range(rows):
        for y in range(columns):
            index, count = (x, rows) if along == "gx" else (y, columns)
            other = index + 1 if index % 2 == parity else index - 1
            if 0 <= other < count:
                target = (other, y) if along == "gx" else (x, other)
            else:
                target = (x, y ^ 1) if along == "gx" else (x ^ 1, y)
                if not (target[0] < rows and target[1] < columns):
                    target = (x, y)
            pairs.append((x * columns + y, target[0] * columns + target[1]))
    return pairs


def swap_faces(sends, axes=("gx", "gy")):
    rows, columns = lax.axis_size("gx"), lax.axis_size("gy")
    order = [(along, parity) for along in axes for parity in (0, 1)]
    return [
        lax.ppermute(send, ("gx", "gy"), swap_pairs(rows, columns, along, parity))
        for send, (along, parity) in zip(sends, order)
    ]


def stage_masks(axis, first):
    count = lax.axis_size(axis)
    stages = []
    step = first
    while step < count:
        last = step * 2 >= count
        stages.append((axis, (step,) if last else (step, 2 * step, 3 * step)))
        step *= 4
    return stages


def from_mask(value, axis, mask):
    count = lax.axis_size(axis)
    return lax.ppermute(value, axis, [(source, source ^ mask) for source in range(count)])


def sum_over_devices(keep, send, add, work, inputs):
    value = add([keep, from_mask(send, "gy", 1)])
    stages = stage_masks("gy", 2) + stage_masks("gx", 1)
    done, sends, received = (), (), []
    for index, (axis, masks) in enumerate(stages):
        value, inputs, sends = lax.optimization_barrier((value, inputs, sends))
        parts = [value] + [from_mask(value, axis, mask) for mask in masks]
        if index == 0:
            done, sends = work(*inputs)
        if index == len(stages) - 1:
            received = swap_faces(sends)
        value = add(parts)
        value, done, sends = lax.optimization_barrier((value, done, sends))
    return value, from_mask(value, "gy", 1), received, done


def plain(parts):
    value = parts[0] + parts[1]
    return value + (parts[2] + parts[3]) if len(parts) == 4 else value


def rescaled(power, parts):
    cases = parts[0].shape[0] - PAD
    scales = [part[cases:] for part in parts]
    scale = functools.reduce(jnp.minimum, scales)
    ready = []
    for part, own in zip(parts, scales):
        ratio = (scale / own)[:1]
        factor = jnp.where(power == 0.0, 1.0, jnp.where(power == 1.0, ratio, ratio * ratio))
        ready.append(part[:cases] * factor)
    return jnp.concatenate([plain(ready), scale], axis=0)


def local(right_side, weights, signs, face_map, pattern, factor):
    cases, size = right_side.shape[1:]
    blocks = pattern.shape[1]
    place = jnp.stack(
        [
            lax.axis_index("gx"),
            lax.axis_index("gy"),
            jnp.int32(lax.axis_size("gx")),
            jnp.int32(lax.axis_size("gy")),
        ]
    )
    field, padded = (cases, size), (cases + PAD, size)
    face, padded_face = (cases, size // 4), (cases + PAD, size // 4)
    half_type = ((size, size), jnp.bfloat16)

    work = 6 * cases * size * size
    (pick,) = call(pick_kernel, "pick", [half_type], face_map, smem=0, flops=20 * work)
    small, *sends = call(
        start_kernel, "start_fields", [padded] + [padded_face] * 4,
        place, right_side[0], weights, signs, face_map, pick,
    )
    received = swap_faces(sends)
    high, low = call(
        functools.partial(factor_kernel, blocks), "masked_factor", [half_type] * 2,
        pattern[0], factor[0], face_map,
        scratch=[pltpu.VMEM((size, size), jnp.bfloat16)] * 2,
        smem=0,
    )
    ghosts, half0, out0, *sends = call(
        first_kernel, "first_operator", [padded, field, field] + [face] * 4,
        place, small, *received, high, low,
    )
    received = swap_faces(sends)
    (top,) = call(
        early_gram_kernel, "early_gram", [(cases, 2 * cases)], small, half0, smem=0
    )
    received, top = lax.optimization_barrier((received, top))
    image0, ghost_image0, second, keep, send, power = call(
        gram_kernel, "first_gram",
        [field, field, padded] + [(cases + PAD, 2 * cases)] * 2 + [(1, 2 * cases)],
        place, small, ghosts, half0, top, out0, *received, high, low,
    )

    def lift(second):
        out, *sends = call(
            lift_kernel, "second_operator", [field] + [padded_face] * 4,
            place, small, second, high, low,
        )
        return out, sends

    mine, other, faces, out1 = sum_over_devices(
        keep, send, functools.partial(rescaled, power), lift, (second,)
    )
    steps, inverse = call(
        solve_kernel, "first_solve", [(cases, 2 * cases), (2 * cases, 2 * cases)],
        place, mine, other,
    )
    state, image1, next_half0, next_out0, *next_sends = call(
        step_kernel, "first_step", [field] * 4 + [face] * 4,
        place, small, ghosts, mine, steps, image0, ghost_image0, second, out1,
        *faces, high, low,
    )
    inverse, next_sends = lax.optimization_barrier((inverse, next_sends))
    faces = swap_faces(next_sends)
    pick, gram_inverse = call(
        functools.partial(prepare_kernel, cases), "prepare_last",
        [half_type, (2 * cases, 2 * cases)], small, inverse, smem=0,
    )
    left, before = call(
        next_early_gram_kernel, "next_early_gram", [(3 * cases, cases), field],
        small, mine, second, state, next_half0, smem=0,
    )
    faces, pick, gram_inverse, left, before = lax.optimization_barrier(
        (faces, pick, gram_inverse, left, before)
    )
    next_image0, next_half1, keep, send = call(
        next_gram_kernel, "second_gram", [field, field] + [(3 * cases // 2, 2 * cases)] * 2,
        place, small, ghosts, mine, before, next_half0, left, next_out0, *faces, high, low,
    )

    def last_lift(half):
        out, *sends = call(
            next_lift_kernel, "last_operator", [field] + [face] * 4,
            place, small, half, high, low,
        )
        return out, sends

    next_mine, next_other, faces, next_out1 = sum_over_devices(
        keep, send, plain, last_lift, (next_half1,)
    )
    wide = (cases, 4 * cases)
    found, change = call(
        last_solve_kernel, "last_solve", [wide, wide],
        place, mine, next_mine, next_other, gram_inverse, steps,
    )
    answer, resid = call(
        last_kernel, "last_step", [field, field],
        place, small, mine, found, change, state, image0, image1, next_image0, next_out1,
        *faces, pick,
    )
    return (answer[None], resid[None])


def solution(mesh):
    return jax.shard_map(
        local,
        mesh=mesh,
        in_specs=(
            P("gx", None, "gy"),
            P("gx", "gy"),
            P("gx", "gy"),
            P("gx", "gy"),
            P("gx", None, "gy"),
            P("gx", None, "gy"),
        ),
        out_specs=(P("gx", None, "gy"), P("gx", None, "gy")),
        check_vma=False,
    )
```

```python
import functools

import jax
import jax.numpy as jnp
from jax import lax
from jax.experimental import pallas as pl
from jax.experimental.pallas import tpu as pltpu
from jax.sharding import PartitionSpec as P

HIGH = lax.Precision.HIGHEST
VMEM = pl.BlockSpec(memory_space=pltpu.VMEM)
SMEM = pl.BlockSpec(memory_space=pltpu.SMEM)
PAD = 8
SMALL = 1e-6
LANES = 128


def halves(value):
    high = value.astype(jnp.bfloat16)
    low = (value - high.astype(jnp.float32)).astype(jnp.bfloat16)
    return high, low


def thirds(value):
    high = value.astype(jnp.bfloat16)
    rest = value - high.astype(jnp.float32)
    middle = rest.astype(jnp.bfloat16)
    low = (rest - middle.astype(jnp.float32)).astype(jnp.bfloat16)
    return jnp.concatenate([high, middle, low], axis=0)


def bf16_dot(left, right, right_dim):
    return lax.dot_general(
        left, right, (((1,), (right_dim,)), ((), ())), preferred_element_type=jnp.float32
    )


def exact_pick(value, pick):
    rows = value.shape[0]
    parts = bf16_dot(thirds(value), pick, 0)
    return parts[:rows] + (parts[rows : 2 * rows] + parts[2 * rows :])


def product(value, high, low, dim):
    rows = value.shape[0]
    value_high, value_low = halves(value)
    both = bf16_dot(jnp.concatenate([value_high, value_low], axis=0), high[...], dim)
    return both[:rows] + (both[rows:] + bf16_dot(value_high, low[...], dim))


def inner_prod(left, right):
    return lax.dot_general(
        left, right, (((1,), (1,)), ((), ())), precision=HIGH, preferred_element_type=jnp.float32
    )


def times(left, right):
    return jnp.dot(left, right, precision=HIGH, preferred_element_type=jnp.float32)


def row_to_square(row, size):
    return jnp.broadcast_to(row, (LANES, size)).T


def pick_columns(face_row):
    size = face_row.shape[1]
    unknown = lax.broadcasted_iota(jnp.int32, (size, size), 0)
    return jnp.where(unknown == face_row, 1.0, 0.0).astype(jnp.bfloat16)


def pick_rows(face_row):
    size = face_row.shape[1]
    face = row_to_square(face_row, size)
    lane = lax.broadcasted_iota(jnp.int32, (size, LANES), 1)
    return jnp.concatenate(
        [
            jnp.where(face == lane + start, 1.0, 0.0).astype(jnp.bfloat16)
            for start in range(0, size, LANES)
        ],
        axis=1,
    )


def faces_of(field):
    face_len = field.shape[1] // 4
    return [field[:, face * face_len : (face + 1) * face_len] for face in range(4)]


def write_faces(place, field, outs):
    north, south, west, east = faces_of(field)
    even_x, even_y = place[0] % 2 == 0, place[1] % 2 == 0
    outs[0][...] = jnp.where(even_x, south, north)
    outs[1][...] = jnp.where(even_x, north, south)
    outs[2][...] = jnp.where(even_y, east, west)
    outs[3][...] = jnp.where(even_y, west, east)


def read_faces(place, received):
    x_first, x_second, y_first, y_second = [one[...] for one in received]
    even_x, even_y = place[0] % 2 == 0, place[1] % 2 == 0
    north = jnp.where(place[0] > 0, jnp.where(even_x, x_second, x_first), 0.0)
    south = jnp.where(place[0] + 1 < place[2], jnp.where(even_x, x_first, x_second), 0.0)
    west = jnp.where(place[1] > 0, jnp.where(even_y, y_second, y_first), 0.0)
    east = jnp.where(place[1] + 1 < place[3], jnp.where(even_y, y_first, y_second), 0.0)
    return jnp.concatenate([north, south, west, east], axis=1)


def rows_of(small, cases):
    return small[:cases], small[cases : cases + 1], small[cases + 1 : cases + 2]


def images_of(out, signed_ghost, jump, ghost_jump):
    image = out + 0.5 * signed_ghost
    ghost = ghost_jump * signed_ghost + (0.5 * jump * jnp.abs(ghost_jump)) * out
    return image, ghost


def inverse_of(matrix):
    size = matrix.shape[0]
    eye = lax.broadcasted_iota(jnp.int32, matrix.shape, 0) == lax.broadcasted_iota(
        jnp.int32, matrix.shape, 1
    )
    diagonal = jnp.where(eye, matrix, 0.0)
    by_row = lax.rsqrt(jnp.sum(diagonal, axis=1, keepdims=True))
    by_column = lax.rsqrt(jnp.sum(diagonal, axis=0, keepdims=True))
    scaled = matrix * by_row * by_column
    bound = jnp.max(jnp.sum(jnp.abs(scaled), axis=0, keepdims=True), axis=1, keepdims=True)
    square = jnp.sum(jnp.sum(scaled * scaled, axis=0, keepdims=True), axis=1, keepdims=True)
    one = jnp.where(eye, 1.0, 0.0)

    def again(state):
        _, before, now, count = state
        return (now > SMALL) & ((now < before) | (now > 1.0)) & (count < 64)

    def better(state):
        x, _, now, count = state
        left = one - times(scaled, x)
        twice = times(left, left)
        x = x + times(x, left)
        fourth = times(twice, twice)
        x = x + times(x, twice)
        return x + times(x, fourth), now, jnp.sum(fourth * fourth), count + 1

    start = jnp.minimum(size / square, 1.9 / bound)
    left = one - start * scaled
    twice = times(left, left)
    fourth = times(twice, twice)
    x = one + left + twice + times(left, twice)
    x = start * (x + times(x, fourth))
    large = jnp.float32(4 * size)
    state = (x, large, jnp.sum(fourth * fourth), jnp.int32(1))
    x, _, _, _ = lax.while_loop(again, better, state)
    return x * by_row * by_column


def solve_halves(a00, a01, a11, b0, b1):
    size = a00.shape[0]
    first = inverse_of(a00)
    both = times(first, jnp.concatenate([a01, b0], axis=1))
    along, part = both[:, :size], both[:, size:]
    taken = times(a01.T, both)
    second = inverse_of(a11 - taken[:, :size])
    x1 = times(second, b1 - taken[:, size:])
    return first, along, second, part - times(along, x1), x1


def pick_kernel(faces, pick):
    pick[...] = pick_columns(faces[...])


def start_kernel(place, loads, weights, signs, faces, pick, small, *sends):
    cases, size = loads.shape
    jump = (2 * signs[...] - 1).astype(jnp.float32)
    more = jnp.concatenate(
        [weights[...], jump, jnp.zeros((PAD - 2, size), jnp.float32)], axis=0
    )
    value = exact_pick(jnp.concatenate([loads[...], more], axis=0), pick[...])
    write_faces(place, value, sends)
    small[...] = value
    small[cases + 2 : cases + 3] = faces[...].astype(jnp.float32)


def face_row(small, cases):
    return small[cases + 2 : cases + 3].astype(jnp.int32)


def factor_kernel(blocks, pattern, factor, faces, high, low, masked_high, masked_low):
    size = factor.shape[0]
    length = size // blocks
    for i in range(blocks):
        for j in range(blocks):
            rows, columns = pl.ds(i * length, length), pl.ds(j * length, length)
            value = factor[rows, columns]
            if i != j:
                keep = jnp.broadcast_to(pattern[i : i + 1, j : j + 1], value.shape)
                value = jnp.where(keep == 1, value, 0.0)
            masked_high[rows, columns], masked_low[rows, columns] = halves(value)
    pick = pick_rows(faces[...])
    chunk = size // 4
    for masked, out in ((masked_high, high), (masked_low, low)):
        for start in range(0, size, chunk):
            out[start : start + chunk] = bf16_dot(
                pick[start : start + chunk], masked[...], 0
            ).astype(jnp.bfloat16)


def prepare_kernel(cases, small, inverse, pick, gram_inverse):
    pick[...] = pick_rows(face_row(small, cases))
    first, second = inverse[:cases], inverse[cases:]
    beside, lower = first[:, cases:], second[:, :cases]
    corner = -times(beside, lower)
    gram_inverse[:cases, :cases] = first[:, :cases] - times(corner, beside.T)
    gram_inverse[:cases, cases:] = corner
    gram_inverse[cases:, :cases] = corner.T
    gram_inverse[cases:, cases:] = lower


def split_sums(place, first, second, more, keep, send):
    even = place[1] % 2 == 0
    rows = first.shape[0]
    keep[:rows] = jnp.where(even, first, second)
    send[:rows] = jnp.where(even, second, first)
    if more is not None:
        keep[rows:] = more
        send[rows:] = more


def join_sums(place, mine, other):
    even = place[1] % 2 == 0
    mine, other = mine[...], other[...]
    return jnp.where(even, mine, other), jnp.where(even, other, mine)


def first_kernel(place, small, x0, x1, y0, y1, high, low, ghosts, half, out, *sends):
    value, ghost = small[...], read_faces(place, (x0, x1, y0, y1))
    ghosts[...] = ghost
    cases = half.shape[0]
    resid, weighting, jump = rows_of(value, cases)
    ghost_resid, ghost_weighting, _ = rows_of(ghost, cases)
    field = weighting * resid + (0.5 * jump) * (ghost_weighting * ghost_resid)
    halfway = product(field, high, low, 0)
    half[...] = halfway
    lifted = product(halfway, high, low, 1)
    out[...] = lifted
    write_faces(place, jump * lifted, sends)


def early_gram_kernel(small, half, top):
    cases = half.shape[0]
    resid, weighting, _ = rows_of(small[...], cases)
    top[:, :cases] = inner_prod(half[...], half[...])
    top[:, cases:] = inner_prod(weighting * resid, resid)


def gram_kernel(
    place, small, ghosts, half, top, out, x0, x1, y0, y1, high, low, image, ghost_image, second, keep, send, power
):
    cases = half.shape[0]
    _, weighting, jump = rows_of(small[...], cases)
    _, ghost_weighting, ghost_jump = rows_of(ghosts[...], cases)
    own, ghost = images_of(out[...], read_faces(place, (x0, x1, y0, y1)), jump, ghost_jump)
    image[...] = own
    ghost_image[...] = ghost
    field = weighting * own + (0.5 * jump) * (ghost_weighting * ghost)
    largest = jnp.max(jnp.max(jnp.abs(field), axis=1, keepdims=True), axis=0, keepdims=True)
    scale = 1.0 / jnp.maximum(largest, 1e-30)
    second_half = product(field * scale, high, low, 0)
    second[:cases] = second_half
    second[cases:] = jnp.broadcast_to(scale, (PAD, field.shape[1]))
    first_half = half[...]
    cross = inner_prod(second_half, jnp.concatenate([first_half, second_half], axis=0))
    split_sums(
        place,
        top[...],
        jnp.concatenate([cross[:, :cases].T, cross[:, cases:]], axis=1),
        jnp.broadcast_to(scale, (PAD, 2 * cases)),
        keep,
        send,
    )
    lane = lax.broadcasted_iota(jnp.int32, (1, 2 * cases), 1)
    scaled = jnp.where(lane < cases, 1.0, 2.0)
    power[...] = jnp.where(place[1] % 2 == 0, jnp.zeros_like(scaled), scaled)


def lift_kernel(place, small, second, high, low, out, *sends):
    cases = out.shape[0]
    jump = small[cases + 1 : cases + 2]
    lifted = product(second[:cases], high, low, 1)
    out[...] = lifted
    write_faces(place, jnp.concatenate([jump * lifted, second[cases:]], axis=0), sends)


def solve_kernel(place, mine, other, steps, inverse):
    cases = steps.shape[0]
    scale = mine[cases : cases + 1, :1]
    top, bottom = join_sums(place, mine, other)
    gram00, gram01, gram11 = top[:cases, :cases], bottom[:cases, :cases], bottom[:cases, cases:]
    first, along, corner, steps0, steps1 = solve_halves(
        gram00, gram01, gram11, top[:cases, cases:], scale * gram00
    )
    inverse[:cases, :cases] = first
    inverse[:cases, cases:] = along
    inverse[cases:, :cases] = corner
    inverse[cases:, cases:] = corner
    steps[...] = jnp.concatenate([steps0, steps1], axis=0).T


def step_kernel(
    place, small, ghosts, mine, steps, image0, ghost_image0, second, out1, x0, x1, y0, y1,
    high, low, state, image1, half, out, *sends
):
    cases = half.shape[0]
    resid, weighting, jump = rows_of(small[...], cases)
    ghost_resid, ghost_weighting, ghost_jump = rows_of(ghosts[...], cases)
    scale = mine[cases : cases + 1, :1]
    received = read_faces(place, (x0, x1, y0, y1))
    own_ratio = scale / second[cases : cases + 1]
    there = received[cases : cases + 1]
    ghost_ratio = jnp.where(there > 0.0, scale / jnp.where(there > 0.0, there, 1.0), 0.0)
    own1, ghost1 = images_of(
        out1[...] * own_ratio, received[:cases] * ghost_ratio, jump, ghost_jump
    )
    image1[...] = own1
    resid = resid - times(steps[...], jnp.concatenate([image0[...], own1], axis=0))
    ghost_resid = ghost_resid - times(
        steps[...], jnp.concatenate([ghost_image0[...], ghost1], axis=0)
    )
    state[...] = resid
    field = weighting * resid + (0.5 * jump) * (ghost_weighting * ghost_resid)
    halfway = product(field, high, low, 0)
    half[...] = halfway
    lifted = product(halfway, high, low, 1)
    out[...] = lifted
    write_faces(place, jump * lifted, sends)


def next_early_gram_kernel(small, mine, second, state, half, left, before):
    cases = half.shape[0]
    _, weighting, _ = rows_of(small[...], cases)
    scale = mine[cases : cases + 1, :1]
    before[...] = second[:cases] * (scale / second[cases : cases + 1])
    left[: 2 * cases] = inner_prod(jnp.concatenate([before[...], half[...]], axis=0), half[...])
    left[2 * cases :] = inner_prod(weighting * state[...], state[...])


def next_gram_kernel(
    place, small, ghosts, mine, before, half, left, out, x0, x1, y0, y1, high, low,
    image, next_half, keep, send
):
    cases = half.shape[0]
    _, weighting, jump = rows_of(small[...], cases)
    _, ghost_weighting, ghost_jump = rows_of(ghosts[...], cases)
    scale = mine[cases : cases + 1, :1]
    own, ghost = images_of(out[...], read_faces(place, (x0, x1, y0, y1)), jump, ghost_jump)
    image[...] = own
    field = scale * (weighting * own + (0.5 * jump) * (ghost_weighting * ghost))
    halfway = product(field, high, low, 0)
    next_half[...] = halfway
    cross = inner_prod(jnp.concatenate([before[...], half[...], halfway], axis=0), halfway)
    total = jnp.concatenate([left[...], cross], axis=1)
    middle = total.shape[0] // 2
    split_sums(place, total[:middle], total[middle:], None, keep, send)


def next_lift_kernel(place, small, half, high, low, out, *sends):
    cases = out.shape[0]
    lifted = product(half[...], high, low, 1)
    out[...] = lifted
    write_faces(place, small[cases + 1 : cases + 2] * lifted, sends)


def last_solve_kernel(place, first_sums, mine, other, gram_inverse, steps, answer, change):
    cases = steps.shape[0]
    scale = first_sums[cases : cases + 1, :1]
    total = jnp.concatenate(join_sums(place, mine, other), axis=0)
    along = jnp.concatenate(
        [
            jnp.concatenate([jnp.zeros((cases, cases), jnp.float32), total[:cases, :cases]], axis=1),
            total[:cases],
        ],
        axis=0,
    )
    conjugating = times(gram_inverse[...], along)
    taken = times(along.T, conjugating)
    gram00 = total[cases : 2 * cases, :cases]
    _, _, _, next0, next1 = solve_halves(
        gram00 - taken[:cases, :cases],
        total[cases : 2 * cases, cases:] - taken[:cases, cases:],
        total[2 * cases :, cases:] - taken[cases:, cases:],
        total[2 * cases :, :cases],
        scale * gram00,
    )
    next_steps = jnp.concatenate([next0, next1], axis=0)
    old_steps = -times(conjugating, next_steps).T
    next_steps = next_steps.T
    answer[...] = jnp.concatenate([steps[...] + old_steps, next_steps], axis=1)
    change[...] = jnp.concatenate([old_steps, next_steps], axis=1)


def last_kernel(
    place, small, first_sums, answer, change, state, image0, image1, next_image0, out1,
    x0, x1, y0, y1, pick, solution_out, resid_out
):
    cases = image0.shape[0]
    first_resid, weighting, _ = rows_of(small[...], cases)
    scale = first_sums[cases : cases + 1, :1]
    next_image1 = out1[...] + 0.5 * read_faces(place, (x0, x1, y0, y1))
    images = jnp.concatenate(
        [image0[...], image1[...], next_image0[...], next_image1], axis=0
    )
    resid = state[...] - times(change[...], images)
    fields = weighting * jnp.concatenate(
        [first_resid, scale * image0[...], state[...], scale * next_image0[...]], axis=0
    )
    found = times(answer[...], fields)
    both = exact_pick(jnp.concatenate([found, resid], axis=0), pick[...])
    solution_out[...] = both[:cases]
    resid_out[...] = both[cases:]


def call(kernel, name, outs, *operands, scratch=(), mebibytes=8, smem=1, flops=0):
    shapes = [
        jax.ShapeDtypeStruct(one[0], one[1]) if isinstance(one[0], tuple)
        else jax.ShapeDtypeStruct(one, jnp.float32)
        for one in outs
    ]
    touched = sum(one.size * one.dtype.itemsize for one in (*operands, *shapes))
    cost = pl.CostEstimate(flops=flops, bytes_accessed=touched, transcendentals=0)
    return pl.pallas_call(
        kernel,
        out_shape=shapes,
        in_specs=[SMEM] * smem + [VMEM] * (len(operands) - smem),
        out_specs=[VMEM] * len(shapes),
        scratch_shapes=list(scratch),
        compiler_params=pltpu.CompilerParams(vmem_limit_bytes=mebibytes * 2**20),
        cost_estimate=cost if flops else None,
        name=name,
    )(*operands)


def swap_pairs(rows, columns, along, parity):
    pairs = []
    for x in range(rows):
        for y in range(columns):
            index, count = (x, rows) if along == "gx" else (y, columns)
            other = index + 1 if index % 2 == parity else index - 1
            if 0 <= other < count:
                target = (other, y) if along == "gx" else (x, other)
            else:
                target = (x, y ^ 1) if along == "gx" else (x ^ 1, y)
                if not (target[0] < rows and target[1] < columns):
                    target = (x, y)
            pairs.append((x * columns + y, target[0] * columns + target[1]))
    return pairs


def swap_faces(sends, axes=("gx", "gy")):
    rows, columns = lax.axis_size("gx"), lax.axis_size("gy")
    order = [(along, parity) for along in axes for parity in (0, 1)]
    return [
        lax.ppermute(send, ("gx", "gy"), swap_pairs(rows, columns, along, parity))
        for send, (along, parity) in zip(sends, order)
    ]


def stage_masks(axis, first):
    count = lax.axis_size(axis)
    stages = []
    step = first
    while step < count:
        last = step * 2 >= count
        stages.append((axis, (step,) if last else (step, 2 * step, 3 * step)))
        step *= 4
    return stages


def from_mask(value, axis, mask):
    count = lax.axis_size(axis)
    return lax.ppermute(value, axis, [(source, source ^ mask) for source in range(count)])


def sum_over_devices(keep, send, add, work, inputs):
    value = add([keep, from_mask(send, "gy", 1)])
    stages = stage_masks("gy", 2) + stage_masks("gx", 1)
    done, sends, received = (), (), []
    for index, (axis, masks) in enumerate(stages):
        value, inputs, sends = lax.optimization_barrier((value, inputs, sends))
        parts = [value] + [from_mask(value, axis, mask) for mask in masks]
        if index == 0:
            done, sends = work(*inputs)
        if index == len(stages) - 1:
            received = swap_faces(sends)
        value = add(parts)
        value, done, sends = lax.optimization_barrier((value, done, sends))
    return value, from_mask(value, "gy", 1), received, done


def plain(parts):
    value = parts[0] + parts[1]
    return value + (parts[2] + parts[3]) if len(parts) == 4 else value


def rescaled(power, parts):
    cases = parts[0].shape[0] - PAD
    scales = [part[cases:] for part in parts]
    scale = functools.reduce(jnp.minimum, scales)
    ready = []
    for part, own in zip(parts, scales):
        ratio = (scale / own)[:1]
        factor = jnp.where(power == 0.0, 1.0, jnp.where(power == 1.0, ratio, ratio * ratio))
        ready.append(part[:cases] * factor)
    return jnp.concatenate([plain(ready), scale], axis=0)


def local(right_side, weights, signs, face_map, pattern, factor):
    cases, size = right_side.shape[1:]
    blocks = pattern.shape[1]
    place = jnp.stack(
        [
            lax.axis_index("gx"),
            lax.axis_index("gy"),
            jnp.int32(lax.axis_size("gx")),
            jnp.int32(lax.axis_size("gy")),
        ]
    )
    field, padded = (cases, size), (cases + PAD, size)
    face, padded_face = (cases, size // 4), (cases + PAD, size // 4)
    half_type = ((size, size), jnp.bfloat16)

    work = 6 * cases * size * size
    (pick,) = call(pick_kernel, "pick", [half_type], face_map, smem=0, flops=20 * work)
    small, *sends = call(
        start_kernel, "start_fields", [padded] + [padded_face] * 4,
        place, right_side[0], weights, signs, face_map, pick,
    )
    received = swap_faces(sends)
    high, low = call(
        functools.partial(factor_kernel, blocks), "masked_factor", [half_type] * 2,
        pattern[0], factor[0], face_map,
        scratch=[pltpu.VMEM((size, size), jnp.bfloat16)] * 2,
        smem=0,
    )
    ghosts, half0, out0, *sends = call(
        first_kernel, "first_operator", [padded, field, field] + [face] * 4,
        place, small, *received, high, low,
    )
    received = swap_faces(sends)
    (top,) = call(
        early_gram_kernel, "early_gram", [(cases, 2 * cases)], small, half0, smem=0
    )
    received, top = lax.optimization_barrier((received, top))
    image0, ghost_image0, second, keep, send, power = call(
        gram_kernel, "first_gram",
        [field, field, padded] + [(cases + PAD, 2 * cases)] * 2 + [(1, 2 * cases)],
        place, small, ghosts, half0, top, out0, *received, high, low,
    )

    def lift(second):
        out, *sends = call(
            lift_kernel, "second_operator", [field] + [padded_face] * 4,
            place, small, second, high, low,
        )
        return out, sends

    mine, other, faces, out1 = sum_over_devices(
        keep, send, functools.partial(rescaled, power), lift, (second,)
    )
    steps, inverse = call(
        solve_kernel, "first_solve", [(cases, 2 * cases), (2 * cases, 2 * cases)],
        place, mine, other,
    )
    state, image1, next_half0, next_out0, *next_sends = call(
        step_kernel, "first_step", [field] * 4 + [face] * 4,
        place, small, ghosts, mine, steps, image0, ghost_image0, second, out1,
        *faces, high, low,
    )
    inverse, next_sends = lax.optimization_barrier((inverse, next_sends))
    faces = swap_faces(next_sends)
    pick, gram_inverse = call(
        functools.partial(prepare_kernel, cases), "prepare_last",
        [half_type, (2 * cases, 2 * cases)], small, inverse, smem=0,
    )
    left, before = call(
        next_early_gram_kernel, "next_early_gram", [(3 * cases, cases), field],
        small, mine, second, state, next_half0, smem=0,
    )
    faces, pick, gram_inverse, left, before = lax.optimization_barrier(
        (faces, pick, gram_inverse, left, before)
    )
    next_image0, next_half1, keep, send = call(
        next_gram_kernel, "second_gram", [field, field] + [(3 * cases // 2, 2 * cases)] * 2,
        place, small, ghosts, mine, before, next_half0, left, next_out0, *faces, high, low,
    )

    def last_lift(half):
        out, *sends = call(
            next_lift_kernel, "last_operator", [field] + [face] * 4,
            place, small, half, high, low,
        )
        return out, sends

    next_mine, next_other, faces, next_out1 = sum_over_devices(
        keep, send, plain, last_lift, (next_half1,)
    )
    wide = (cases, 4 * cases)
    found, change = call(
        last_solve_kernel, "last_solve", [wide, wide],
        place, mine, next_mine, next_other, gram_inverse, steps,
    )
    answer, resid = call(
        last_kernel, "last_step", [field, field],
        place, small, mine, found, change, state, image0, image1, next_image0, next_out1,
        *faces, pick,
    )
    return (answer[None], resid[None])


def solution(mesh):
    return jax.shard_map(
        local,
        mesh=mesh,
        in_specs=(
            P("gx", None, "gy"),
            P("gx", "gy"),
            P("gx", "gy"),
            P("gx", "gy"),
            P("gx", None, "gy"),
            P("gx", None, "gy"),
        ),
        out_specs=(P("gx", None, "gy"), P("gx", None, "gy")),
        check_vma=False,
    )
```

```python
import functools

import jax
import jax.numpy as jnp
from jax import lax
from jax.experimental import pallas as pl
from jax.experimental.pallas import tpu as pltpu
from jax.sharding import PartitionSpec as P

HIGH = lax.Precision.HIGHEST
VMEM = pl.BlockSpec(memory_space=pltpu.VMEM)
SMEM = pl.BlockSpec(memory_space=pltpu.SMEM)
PAD = 8
SMALL = 1e-6
LANES = 128


def halves(value):
    high = value.astype(jnp.bfloat16)
    low = (value - high.astype(jnp.float32)).astype(jnp.bfloat16)
    return high, low


def thirds(value):
    high = value.astype(jnp.bfloat16)
    rest = value - high.astype(jnp.float32)
    middle = rest.astype(jnp.bfloat16)
    low = (rest - middle.astype(jnp.float32)).astype(jnp.bfloat16)
    return jnp.concatenate([high, middle, low], axis=0)


def bf16_dot(left, right, right_dim):
    return lax.dot_general(
        left, right, (((1,), (right_dim,)), ((), ())), preferred_element_type=jnp.float32
    )


def exact_pick(value, pick):
    rows = value.shape[0]
    parts = bf16_dot(thirds(value), pick, 0)
    return parts[:rows] + (parts[rows : 2 * rows] + parts[2 * rows :])


def product(value, high, low, dim):
    rows = value.shape[0]
    value_high, value_low = halves(value)
    both = bf16_dot(jnp.concatenate([value_high, value_low], axis=0), high[...], dim)
    return both[:rows] + (both[rows:] + bf16_dot(value_high, low[...], dim))


def inner_prod(left, right):
    return lax.dot_general(
        left, right, (((1,), (1,)), ((), ())), precision=HIGH, preferred_element_type=jnp.float32
    )


def times(left, right):
    return jnp.dot(left, right, precision=HIGH, preferred_element_type=jnp.float32)


def row_to_square(row, size):
    return jnp.broadcast_to(row, (LANES, size)).T


def pick_columns(face_row):
    size = face_row.shape[1]
    unknown = lax.broadcasted_iota(jnp.int32, (size, size), 0)
    return jnp.where(unknown == face_row, 1.0, 0.0).astype(jnp.bfloat16)


def pick_rows(face_row):
    size = face_row.shape[1]
    face = row_to_square(face_row, size)
    lane = lax.broadcasted_iota(jnp.int32, (size, LANES), 1)
    return jnp.concatenate(
        [
            jnp.where(face == lane + start, 1.0, 0.0).astype(jnp.bfloat16)
            for start in range(0, size, LANES)
        ],
        axis=1,
    )


def faces_of(field):
    face_len = field.shape[1] // 4
    return [field[:, face * face_len : (face + 1) * face_len] for face in range(4)]


def write_faces(place, field, outs):
    north, south, west, east = faces_of(field)
    even_x, even_y = place[0] % 2 == 0, place[1] % 2 == 0
    outs[0][...] = jnp.where(even_x, south, north)
    outs[1][...] = jnp.where(even_x, north, south)
    outs[2][...] = jnp.where(even_y, east, west)
    outs[3][...] = jnp.where(even_y, west, east)


def read_faces(place, received):
    x_first, x_second, y_first, y_second = [one[...] for one in received]
    even_x, even_y = place[0] % 2 == 0, place[1] % 2 == 0
    north = jnp.where(place[0] > 0, jnp.where(even_x, x_second, x_first), 0.0)
    south = jnp.where(place[0] + 1 < place[2], jnp.where(even_x, x_first, x_second), 0.0)
    west = jnp.where(place[1] > 0, jnp.where(even_y, y_second, y_first), 0.0)
    east = jnp.where(place[1] + 1 < place[3], jnp.where(even_y, y_first, y_second), 0.0)
    return jnp.concatenate([north, south, west, east], axis=1)


def rows_of(small, cases):
    return small[:cases], small[cases : cases + 1], small[cases + 1 : cases + 2]


def images_of(out, signed_ghost, jump, ghost_jump):
    image = out + 0.5 * signed_ghost
    ghost = ghost_jump * signed_ghost + (0.5 * jump * jnp.abs(ghost_jump)) * out
    return image, ghost


def inverse_of(matrix):
    size = matrix.shape[0]
    eye = lax.broadcasted_iota(jnp.int32, matrix.shape, 0) == lax.broadcasted_iota(
        jnp.int32, matrix.shape, 1
    )
    diagonal = jnp.where(eye, matrix, 0.0)
    by_row = lax.rsqrt(jnp.sum(diagonal, axis=1, keepdims=True))
    by_column = lax.rsqrt(jnp.sum(diagonal, axis=0, keepdims=True))
    scaled = matrix * by_row * by_column
    bound = jnp.max(jnp.sum(jnp.abs(scaled), axis=0, keepdims=True), axis=1, keepdims=True)
    square = jnp.sum(jnp.sum(scaled * scaled, axis=0, keepdims=True), axis=1, keepdims=True)
    one = jnp.where(eye, 1.0, 0.0)

    def again(state):
        _, before, now, count = state
        return (now > SMALL) & ((now < before) | (now > 1.0)) & (count < 64)

    def better(state):
        x, _, now, count = state
        left = one - times(scaled, x)
        twice = times(left, left)
        nearer = x + times(x, left)
        return nearer + times(nearer, twice), now, jnp.sum(twice * twice), count + 1

    start = jnp.minimum(size / square, 1.9 / bound)
    left = one - start * scaled
    twice = times(left, left)
    nearer = one + left
    x = start * (nearer + times(nearer, twice))
    large = jnp.float32(4 * size)
    state = better((x, large, large, jnp.int32(1)))
    x, _, _, _ = lax.while_loop(again, better, state)
    return x * by_row * by_column


def solve_halves(a00, a01, a11, b0, b1):
    size = a00.shape[0]
    first = inverse_of(a00)
    both = times(first, jnp.concatenate([a01, b0], axis=1))
    along, part = both[:, :size], both[:, size:]
    taken = times(a01.T, both)
    second = inverse_of(a11 - taken[:, :size])
    x1 = times(second, b1 - taken[:, size:])
    return first, along, second, part - times(along, x1), x1


def pick_kernel(faces, pick):
    pick[...] = pick_columns(faces[...])


def start_kernel(place, loads, weights, signs, faces, pick, small, *sends):
    cases, size = loads.shape
    jump = (2 * signs[...] - 1).astype(jnp.float32)
    more = jnp.concatenate(
        [weights[...], jump, jnp.zeros((PAD - 2, size), jnp.float32)], axis=0
    )
    value = exact_pick(jnp.concatenate([loads[...], more], axis=0), pick[...])
    write_faces(place, value, sends)
    small[...] = value
    small[cases + 2 : cases + 3] = faces[...].astype(jnp.float32)


def face_row(small, cases):
    return small[cases + 2 : cases + 3].astype(jnp.int32)


def factor_kernel(blocks, pattern, factor, faces, high, low, masked_high, masked_low):
    size = factor.shape[0]
    length = size // blocks
    for i in range(blocks):
        for j in range(blocks):
            rows, columns = pl.ds(i * length, length), pl.ds(j * length, length)
            value = factor[rows, columns]
            if i != j:
                keep = jnp.broadcast_to(pattern[i : i + 1, j : j + 1], value.shape)
                value = jnp.where(keep == 1, value, 0.0)
            masked_high[rows, columns], masked_low[rows, columns] = halves(value)
    pick = pick_rows(faces[...])
    chunk = size // 4
    for masked, out in ((masked_high, high), (masked_low, low)):
        for start in range(0, size, chunk):
            out[start : start + chunk] = bf16_dot(
                pick[start : start + chunk], masked[...], 0
            ).astype(jnp.bfloat16)


def prepare_kernel(cases, small, inverse, pick, gram_inverse):
    pick[...] = pick_rows(face_row(small, cases))
    first, second = inverse[:cases], inverse[cases:]
    beside, lower = first[:, cases:], second[:, :cases]
    corner = -times(beside, lower)
    gram_inverse[:cases, :cases] = first[:, :cases] - times(corner, beside.T)
    gram_inverse[:cases, cases:] = corner
    gram_inverse[cases:, :cases] = corner.T
    gram_inverse[cases:, cases:] = lower


def split_sums(place, first, second, more, keep, send):
    even = place[1] % 2 == 0
    rows = first.shape[0]
    keep[:rows] = jnp.where(even, first, second)
    send[:rows] = jnp.where(even, second, first)
    if more is not None:
        keep[rows:] = more
        send[rows:] = more


def join_sums(place, mine, other):
    even = place[1] % 2 == 0
    mine, other = mine[...], other[...]
    return jnp.where(even, mine, other), jnp.where(even, other, mine)


def first_kernel(place, small, x0, x1, y0, y1, high, low, ghosts, half, out, *sends):
    value, ghost = small[...], read_faces(place, (x0, x1, y0, y1))
    ghosts[...] = ghost
    cases = half.shape[0]
    resid, weighting, jump = rows_of(value, cases)
    ghost_resid, ghost_weighting, _ = rows_of(ghost, cases)
    field = weighting * resid + (0.5 * jump) * (ghost_weighting * ghost_resid)
    halfway = product(field, high, low, 0)
    half[...] = halfway
    lifted = product(halfway, high, low, 1)
    out[...] = lifted
    write_faces(place, jump * lifted, sends)


def early_gram_kernel(small, half, top):
    cases = half.shape[0]
    resid, weighting, _ = rows_of(small[...], cases)
    top[:, :cases] = inner_prod(half[...], half[...])
    top[:, cases:] = inner_prod(weighting * resid, resid)


def gram_kernel(
    place, small, ghosts, half, top, out, x0, x1, y0, y1, high, low, image, ghost_image, second, keep, send, power
):
    cases = half.shape[0]
    _, weighting, jump = rows_of(small[...], cases)
    _, ghost_weighting, ghost_jump = rows_of(ghosts[...], cases)
    own, ghost = images_of(out[...], read_faces(place, (x0, x1, y0, y1)), jump, ghost_jump)
    image[...] = own
    ghost_image[...] = ghost
    field = weighting * own + (0.5 * jump) * (ghost_weighting * ghost)
    largest = jnp.max(jnp.max(jnp.abs(field), axis=1, keepdims=True), axis=0, keepdims=True)
    scale = 1.0 / jnp.maximum(largest, 1e-30)
    second_half = product(field * scale, high, low, 0)
    second[:cases] = second_half
    second[cases:] = jnp.broadcast_to(scale, (PAD, field.shape[1]))
    first_half = half[...]
    cross = inner_prod(second_half, jnp.concatenate([first_half, second_half], axis=0))
    split_sums(
        place,
        top[...],
        jnp.concatenate([cross[:, :cases].T, cross[:, cases:]], axis=1),
        jnp.broadcast_to(scale, (PAD, 2 * cases)),
        keep,
        send,
    )
    lane = lax.broadcasted_iota(jnp.int32, (1, 2 * cases), 1)
    scaled = jnp.where(lane < cases, 1.0, 2.0)
    power[...] = jnp.where(place[1] % 2 == 0, jnp.zeros_like(scaled), scaled)


def lift_kernel(place, small, second, high, low, out, *sends):
    cases = out.shape[0]
    jump = small[cases + 1 : cases + 2]
    lifted = product(second[:cases], high, low, 1)
    out[...] = lifted
    write_faces(place, jnp.concatenate([jump * lifted, second[cases:]], axis=0), sends)


def solve_kernel(place, mine, other, steps, inverse):
    cases = steps.shape[0]
    scale = mine[cases : cases + 1, :1]
    top, bottom = join_sums(place, mine, other)
    gram00, gram01, gram11 = top[:cases, :cases], bottom[:cases, :cases], bottom[:cases, cases:]
    first, along, corner, steps0, steps1 = solve_halves(
        gram00, gram01, gram11, top[:cases, cases:], scale * gram00
    )
    inverse[:cases, :cases] = first
    inverse[:cases, cases:] = along
    inverse[cases:, :cases] = corner
    inverse[cases:, cases:] = corner
    steps[...] = jnp.concatenate([steps0, steps1], axis=0).T


def step_kernel(
    place, small, ghosts, mine, steps, image0, ghost_image0, second, out1, x0, x1, y0, y1,
    high, low, state, image1, half, out, *sends
):
    cases = half.shape[0]
    resid, weighting, jump = rows_of(small[...], cases)
    ghost_resid, ghost_weighting, ghost_jump = rows_of(ghosts[...], cases)
    scale = mine[cases : cases + 1, :1]
    received = read_faces(place, (x0, x1, y0, y1))
    own_ratio = scale / second[cases : cases + 1]
    there = received[cases : cases + 1]
    ghost_ratio = jnp.where(there > 0.0, scale / jnp.where(there > 0.0, there, 1.0), 0.0)
    own1, ghost1 = images_of(
        out1[...] * own_ratio, received[:cases] * ghost_ratio, jump, ghost_jump
    )
    image1[...] = own1
    resid = resid - times(steps[...], jnp.concatenate([image0[...], own1], axis=0))
    ghost_resid = ghost_resid - times(
        steps[...], jnp.concatenate([ghost_image0[...], ghost1], axis=0)
    )
    state[...] = resid
    field = weighting * resid + (0.5 * jump) * (ghost_weighting * ghost_resid)
    halfway = product(field, high, low, 0)
    half[...] = halfway
    lifted = product(halfway, high, low, 1)
    out[...] = lifted
    write_faces(place, jump * lifted, sends)


def next_early_gram_kernel(small, mine, second, state, half, left, before):
    cases = half.shape[0]
    _, weighting, _ = rows_of(small[...], cases)
    scale = mine[cases : cases + 1, :1]
    before[...] = second[:cases] * (scale / second[cases : cases + 1])
    left[: 2 * cases] = inner_prod(jnp.concatenate([before[...], half[...]], axis=0), half[...])
    left[2 * cases :] = inner_prod(weighting * state[...], state[...])


def next_gram_kernel(
    place, small, ghosts, mine, before, half, left, out, x0, x1, y0, y1, high, low,
    image, next_half, keep, send
):
    cases = half.shape[0]
    _, weighting, jump = rows_of(small[...], cases)
    _, ghost_weighting, ghost_jump = rows_of(ghosts[...], cases)
    scale = mine[cases : cases + 1, :1]
    own, ghost = images_of(out[...], read_faces(place, (x0, x1, y0, y1)), jump, ghost_jump)
    image[...] = own
    field = scale * (weighting * own + (0.5 * jump) * (ghost_weighting * ghost))
    halfway = product(field, high, low, 0)
    next_half[...] = halfway
    cross = inner_prod(jnp.concatenate([before[...], half[...], halfway], axis=0), halfway)
    total = jnp.concatenate([left[...], cross], axis=1)
    middle = total.shape[0] // 2
    split_sums(place, total[:middle], total[middle:], None, keep, send)


def next_lift_kernel(place, small, half, high, low, out, *sends):
    cases = out.shape[0]
    lifted = product(half[...], high, low, 1)
    out[...] = lifted
    write_faces(place, small[cases + 1 : cases + 2] * lifted, sends)


def last_solve_kernel(place, first_sums, mine, other, gram_inverse, steps, answer, change):
    cases = steps.shape[0]
    scale = first_sums[cases : cases + 1, :1]
    total = jnp.concatenate(join_sums(place, mine, other), axis=0)
    along = jnp.concatenate(
        [
            jnp.concatenate([jnp.zeros((cases, cases), jnp.float32), total[:cases, :cases]], axis=1),
            total[:cases],
        ],
        axis=0,
    )
    conjugating = times(gram_inverse[...], along)
    taken = times(along.T, conjugating)
    gram00 = total[cases : 2 * cases, :cases]
    _, _, _, next0, next1 = solve_halves(
        gram00 - taken[:cases, :cases],
        total[cases : 2 * cases, cases:] - taken[:cases, cases:],
        total[2 * cases :, cases:] - taken[cases:, cases:],
        total[2 * cases :, :cases],
        scale * gram00,
    )
    next_steps = jnp.concatenate([next0, next1], axis=0)
    old_steps = -times(conjugating, next_steps).T
    next_steps = next_steps.T
    answer[...] = jnp.concatenate([steps[...] + old_steps, next_steps], axis=1)
    change[...] = jnp.concatenate([old_steps, next_steps], axis=1)


def last_kernel(
    place, small, first_sums, answer, change, state, image0, image1, next_image0, out1,
    x0, x1, y0, y1, pick, solution_out, resid_out
):
    cases = image0.shape[0]
    first_resid, weighting, _ = rows_of(small[...], cases)
    scale = first_sums[cases : cases + 1, :1]
    next_image1 = out1[...] + 0.5 * read_faces(place, (x0, x1, y0, y1))
    images = jnp.concatenate(
        [image0[...], image1[...], next_image0[...], next_image1], axis=0
    )
    resid = state[...] - times(change[...], images)
    fields = weighting * jnp.concatenate(
        [first_resid, scale * image0[...], state[...], scale * next_image0[...]], axis=0
    )
    found = times(answer[...], fields)
    both = exact_pick(jnp.concatenate([found, resid], axis=0), pick[...])
    solution_out[...] = both[:cases]
    resid_out[...] = both[cases:]


def call(kernel, name, outs, *operands, scratch=(), mebibytes=8, smem=1, flops=0):
    shapes = [
        jax.ShapeDtypeStruct(one[0], one[1]) if isinstance(one[0], tuple)
        else jax.ShapeDtypeStruct(one, jnp.float32)
        for one in outs
    ]
    touched = sum(one.size * one.dtype.itemsize for one in (*operands, *shapes))
    cost = pl.CostEstimate(flops=flops, bytes_accessed=touched, transcendentals=0)
    return pl.pallas_call(
        kernel,
        out_shape=shapes,
        in_specs=[SMEM] * smem + [VMEM] * (len(operands) - smem),
        out_specs=[VMEM] * len(shapes),
        scratch_shapes=list(scratch),
        compiler_params=pltpu.CompilerParams(vmem_limit_bytes=mebibytes * 2**20),
        cost_estimate=cost if flops else None,
        name=name,
    )(*operands)


def swap_pairs(rows, columns, along, parity):
    pairs = []
    for x in range(rows):
        for y in range(columns):
            index, count = (x, rows) if along == "gx" else (y, columns)
            other = index + 1 if index % 2 == parity else index - 1
            if 0 <= other < count:
                target = (other, y) if along == "gx" else (x, other)
            else:
                target = (x, y ^ 1) if along == "gx" else (x ^ 1, y)
                if not (target[0] < rows and target[1] < columns):
                    target = (x, y)
            pairs.append((x * columns + y, target[0] * columns + target[1]))
    return pairs


def swap_faces(sends, axes=("gx", "gy")):
    rows, columns = lax.axis_size("gx"), lax.axis_size("gy")
    order = [(along, parity) for along in axes for parity in (0, 1)]
    return [
        lax.ppermute(send, ("gx", "gy"), swap_pairs(rows, columns, along, parity))
        for send, (along, parity) in zip(sends, order)
    ]


def stage_masks(axis, first):
    count = lax.axis_size(axis)
    stages = []
    step = first
    while step < count:
        last = step * 2 >= count
        stages.append((axis, (step,) if last else (3 * step, 2 * step, step)))
        step *= 4
    return stages


def from_mask(value, axis, mask):
    count = lax.axis_size(axis)
    return lax.ppermute(value, axis, [(source, source ^ mask) for source in range(count)])


def sum_over_devices(keep, send, add, work, inputs):
    value = add([keep, from_mask(send, "gy", 1)])
    stages = stage_masks("gy", 2) + stage_masks("gx", 1)
    done, sends, received = (), (), []
    for index, (axis, masks) in enumerate(stages):
        value, inputs, sends = lax.optimization_barrier((value, inputs, sends))
        parts = [value] + [from_mask(value, axis, mask) for mask in masks]
        if index == 0:
            done, sends = work(*inputs)
        if index == len(stages) - 1:
            received = swap_faces(sends)
        value = add(parts)
        value, done, sends = lax.optimization_barrier((value, done, sends))
    return value, from_mask(value, "gy", 1), received, done


def plain(parts):
    value = parts[0] + parts[1]
    return value + (parts[2] + parts[3]) if len(parts) == 4 else value


def rescaled(power, parts):
    cases = parts[0].shape[0] - PAD
    scales = [part[cases:] for part in parts]
    scale = functools.reduce(jnp.minimum, scales)
    ready = []
    for part, own in zip(parts, scales):
        ratio = (scale / own)[:1]
        factor = jnp.where(power == 0.0, 1.0, jnp.where(power == 1.0, ratio, ratio * ratio))
        ready.append(part[:cases] * factor)
    return jnp.concatenate([plain(ready), scale], axis=0)


def local(right_side, weights, signs, face_map, pattern, factor):
    cases, size = right_side.shape[1:]
    blocks = pattern.shape[1]
    place = jnp.stack(
        [
            lax.axis_index("gx"),
            lax.axis_index("gy"),
            jnp.int32(lax.axis_size("gx")),
            jnp.int32(lax.axis_size("gy")),
        ]
    )
    field, padded = (cases, size), (cases + PAD, size)
    face, padded_face = (cases, size // 4), (cases + PAD, size // 4)
    half_type = ((size, size), jnp.bfloat16)

    work = 6 * cases * size * size
    (pick,) = call(pick_kernel, "pick", [half_type], face_map, smem=0, flops=20 * work)
    small, *sends = call(
        start_kernel, "start_fields", [padded] + [padded_face] * 4,
        place, right_side[0], weights, signs, face_map, pick,
    )
    received = swap_faces(sends)
    high, low = call(
        functools.partial(factor_kernel, blocks), "masked_factor", [half_type] * 2,
        pattern[0], factor[0], face_map,
        scratch=[pltpu.VMEM((size, size), jnp.bfloat16)] * 2,
        smem=0,
    )
    ghosts, half0, out0, *sends = call(
        first_kernel, "first_operator", [padded, field, field] + [face] * 4,
        place, small, *received, high, low,
    )
    received = swap_faces(sends)
    (top,) = call(
        early_gram_kernel, "early_gram", [(cases, 2 * cases)], small, half0, smem=0
    )
    received, top = lax.optimization_barrier((received, top))
    image0, ghost_image0, second, keep, send, power = call(
        gram_kernel, "first_gram",
        [field, field, padded] + [(cases + PAD, 2 * cases)] * 2 + [(1, 2 * cases)],
        place, small, ghosts, half0, top, out0, *received, high, low,
    )

    def lift(second):
        out, *sends = call(
            lift_kernel, "second_operator", [field] + [padded_face] * 4,
            place, small, second, high, low,
        )
        return out, sends

    mine, other, faces, out1 = sum_over_devices(
        keep, send, functools.partial(rescaled, power), lift, (second,)
    )
    steps, inverse = call(
        solve_kernel, "first_solve", [(cases, 2 * cases), (2 * cases, 2 * cases)],
        place, mine, other,
    )
    state, image1, next_half0, next_out0, *next_sends = call(
        step_kernel, "first_step", [field] * 4 + [face] * 4,
        place, small, ghosts, mine, steps, image0, ghost_image0, second, out1,
        *faces, high, low,
    )
    inverse, next_sends = lax.optimization_barrier((inverse, next_sends))
    faces = swap_faces(next_sends)
    pick, gram_inverse = call(
        functools.partial(prepare_kernel, cases), "prepare_last",
        [half_type, (2 * cases, 2 * cases)], small, inverse, smem=0,
    )
    left, before = call(
        next_early_gram_kernel, "next_early_gram", [(3 * cases, cases), field],
        small, mine, second, state, next_half0, smem=0,
    )
    faces, pick, gram_inverse, left, before = lax.optimization_barrier(
        (faces, pick, gram_inverse, left, before)
    )
    next_image0, next_half1, keep, send = call(
        next_gram_kernel, "second_gram", [field, field] + [(3 * cases // 2, 2 * cases)] * 2,
        place, small, ghosts, mine, before, next_half0, left, next_out0, *faces, high, low,
    )

    def last_lift(half):
        out, *sends = call(
            next_lift_kernel, "last_operator", [field] + [face] * 4,
            place, small, half, high, low,
        )
        return out, sends

    next_mine, next_other, faces, next_out1 = sum_over_devices(
        keep, send, plain, last_lift, (next_half1,)
    )
    wide = (cases, 4 * cases)
    found, change = call(
        last_solve_kernel, "last_solve", [wide, wide],
        place, mine, next_mine, next_other, gram_inverse, steps,
    )
    answer, resid = call(
        last_kernel, "last_step", [field, field],
        place, small, mine, found, change, state, image0, image1, next_image0, next_out1,
        *faces, pick,
    )
    return (answer[None], resid[None])


def solution(mesh):
    return jax.shard_map(
        local,
        mesh=mesh,
        in_specs=(
            P("gx", None, "gy"),
            P("gx", "gy"),
            P("gx", "gy"),
            P("gx", "gy"),
            P("gx", None, "gy"),
            P("gx", None, "gy"),
        ),
        out_specs=(P("gx", None, "gy"), P("gx", None, "gy")),
        check_vma=False,
    )
```

```python
import functools

import jax
import jax.numpy as jnp
from jax import lax
from jax.experimental import pallas as pl
from jax.experimental.pallas import tpu as pltpu
from jax.sharding import PartitionSpec as P

HIGH = lax.Precision.HIGHEST
VMEM = pl.BlockSpec(memory_space=pltpu.VMEM)
SMEM = pl.BlockSpec(memory_space=pltpu.SMEM)
PAD = 8
SMALL = 1e-6
LANES = 128


def halves(value):
    high = value.astype(jnp.bfloat16)
    low = (value - high.astype(jnp.float32)).astype(jnp.bfloat16)
    return high, low


def thirds(value):
    high = value.astype(jnp.bfloat16)
    rest = value - high.astype(jnp.float32)
    middle = rest.astype(jnp.bfloat16)
    low = (rest - middle.astype(jnp.float32)).astype(jnp.bfloat16)
    return jnp.concatenate([high, middle, low], axis=0)


def bf16_dot(left, right, right_dim):
    return lax.dot_general(
        left, right, (((1,), (right_dim,)), ((), ())), preferred_element_type=jnp.float32
    )


def exact_pick(value, pick):
    rows = value.shape[0]
    parts = bf16_dot(thirds(value), pick, 0)
    return parts[:rows] + (parts[rows : 2 * rows] + parts[2 * rows :])


def product(value, high, low, dim):
    rows = value.shape[0]
    value_high, value_low = halves(value)
    both = bf16_dot(jnp.concatenate([value_high, value_low], axis=0), high[...], dim)
    return both[:rows] + (both[rows:] + bf16_dot(value_high, low[...], dim))


def inner_prod(left, right):
    return lax.dot_general(
        left, right, (((1,), (1,)), ((), ())), precision=HIGH, preferred_element_type=jnp.float32
    )


def times(left, right):
    return jnp.dot(left, right, precision=HIGH, preferred_element_type=jnp.float32)


def row_to_square(row, size):
    return jnp.broadcast_to(row, (LANES, size)).T


def pick_columns(face_row):
    size = face_row.shape[1]
    unknown = lax.broadcasted_iota(jnp.int32, (size, size), 0)
    return jnp.where(unknown == face_row, 1.0, 0.0).astype(jnp.bfloat16)


def pick_rows(face_row):
    size = face_row.shape[1]
    face = row_to_square(face_row, size)
    lane = lax.broadcasted_iota(jnp.int32, (size, LANES), 1)
    return jnp.concatenate(
        [
            jnp.where(face == lane + start, 1.0, 0.0).astype(jnp.bfloat16)
            for start in range(0, size, LANES)
        ],
        axis=1,
    )


def faces_of(field):
    face_len = field.shape[1] // 4
    return [field[:, face * face_len : (face + 1) * face_len] for face in range(4)]


def write_faces(place, field, outs):
    north, south, west, east = faces_of(field)
    even_x, even_y = place[0] % 2 == 0, place[1] % 2 == 0
    outs[0][...] = jnp.where(even_x, south, north)
    outs[1][...] = jnp.where(even_x, north, south)
    outs[2][...] = jnp.where(even_y, east, west)
    outs[3][...] = jnp.where(even_y, west, east)


def read_faces(place, received):
    x_first, x_second, y_first, y_second = [one[...] for one in received]
    even_x, even_y = place[0] % 2 == 0, place[1] % 2 == 0
    north = jnp.where(place[0] > 0, jnp.where(even_x, x_second, x_first), 0.0)
    south = jnp.where(place[0] + 1 < place[2], jnp.where(even_x, x_first, x_second), 0.0)
    west = jnp.where(place[1] > 0, jnp.where(even_y, y_second, y_first), 0.0)
    east = jnp.where(place[1] + 1 < place[3], jnp.where(even_y, y_first, y_second), 0.0)
    return jnp.concatenate([north, south, west, east], axis=1)


def rows_of(small, cases):
    return small[:cases], small[cases : cases + 1], small[cases + 1 : cases + 2]


def images_of(out, signed_ghost, jump, ghost_jump):
    image = out + 0.5 * signed_ghost
    ghost = ghost_jump * signed_ghost + (0.5 * jump * jnp.abs(ghost_jump)) * out
    return image, ghost


def inverse_of(matrix):
    size = matrix.shape[0]
    eye = lax.broadcasted_iota(jnp.int32, matrix.shape, 0) == lax.broadcasted_iota(
        jnp.int32, matrix.shape, 1
    )
    diagonal = jnp.where(eye, matrix, 0.0)
    by_row = lax.rsqrt(jnp.sum(diagonal, axis=1, keepdims=True))
    by_column = lax.rsqrt(jnp.sum(diagonal, axis=0, keepdims=True))
    scaled = matrix * by_row * by_column
    bound = jnp.max(jnp.sum(jnp.abs(scaled), axis=0, keepdims=True), axis=1, keepdims=True)
    square = jnp.sum(jnp.sum(scaled * scaled, axis=0, keepdims=True), axis=1, keepdims=True)
    one = jnp.where(eye, 1.0, 0.0)

    def again(state):
        _, before, now, count = state
        return (now > SMALL) & ((now < before) | (now > 1.0)) & (count < 64)

    def better(state):
        x, _, now, count = state
        left = one - times(scaled, x)
        twice = times(left, left)
        nearer = x + times(x, left)
        return nearer + times(nearer, twice), now, jnp.sum(twice * twice), count + 1

    start = jnp.minimum(size / square, 1.9 / bound)
    left = one - start * scaled
    twice = times(left, left)
    nearer = one + left
    x = start * (nearer + times(nearer, twice))
    large = jnp.float32(4 * size)
    state = better((x, large, large, jnp.int32(1)))
    x, _, _, _ = lax.while_loop(again, better, state)
    return x * by_row * by_column


def solve_halves(a00, a01, a11, b0, b1):
    size = a00.shape[0]
    first = inverse_of(a00)
    both = times(first, jnp.concatenate([a01, b0], axis=1))
    along, part = both[:, :size], both[:, size:]
    taken = times(a01.T, both)
    second = inverse_of(a11 - taken[:, :size])
    x1 = times(second, b1 - taken[:, size:])
    return first, along, second, part - times(along, x1), x1


def pick_kernel(faces, pick):
    pick[...] = pick_columns(faces[...])


def start_kernel(place, loads, weights, signs, faces, pick, small, *sends):
    cases, size = loads.shape
    jump = (2 * signs[...] - 1).astype(jnp.float32)
    more = jnp.concatenate(
        [weights[...], jump, jnp.zeros((PAD - 2, size), jnp.float32)], axis=0
    )
    value = exact_pick(jnp.concatenate([loads[...], more], axis=0), pick[...])
    write_faces(place, value, sends)
    small[...] = value
    small[cases + 2 : cases + 3] = faces[...].astype(jnp.float32)


def face_row(small, cases):
    return small[cases + 2 : cases + 3].astype(jnp.int32)


def factor_kernel(blocks, pattern, factor, faces, high, low, masked_high, masked_low):
    size = factor.shape[0]
    length = size // blocks
    for i in range(blocks):
        for j in range(blocks):
            rows, columns = pl.ds(i * length, length), pl.ds(j * length, length)
            value = factor[rows, columns]
            if i != j:
                keep = jnp.broadcast_to(pattern[i : i + 1, j : j + 1], value.shape)
                value = jnp.where(keep == 1, value, 0.0)
            masked_high[rows, columns], masked_low[rows, columns] = halves(value)
    pick = pick_rows(faces[...])
    chunk = size // 4
    for masked, out in ((masked_high, high), (masked_low, low)):
        for start in range(0, size, chunk):
            out[start : start + chunk] = bf16_dot(
                pick[start : start + chunk], masked[...], 0
            ).astype(jnp.bfloat16)


def prepare_kernel(cases, small, inverse, pick, gram_inverse):
    pick[...] = pick_rows(face_row(small, cases))
    first, second = inverse[:cases], inverse[cases:]
    beside, lower = first[:, cases:], second[:, :cases]
    corner = -times(beside, lower)
    gram_inverse[:cases, :cases] = first[:, :cases] - times(corner, beside.T)
    gram_inverse[:cases, cases:] = corner
    gram_inverse[cases:, :cases] = corner.T
    gram_inverse[cases:, cases:] = lower


def split_sums(place, first, second, more, keep, send):
    even = place[1] % 2 == 0
    rows = first.shape[0]
    keep[:rows] = jnp.where(even, first, second)
    send[:rows] = jnp.where(even, second, first)
    if more is not None:
        keep[rows:] = more
        send[rows:] = more


def join_sums(place, mine, other):
    even = place[1] % 2 == 0
    mine, other = mine[...], other[...]
    return jnp.where(even, mine, other), jnp.where(even, other, mine)


def lift_pair(place, axis, halfway, jump, high, low, out, sends):
    count = high.shape[0] // 2
    slots = slice(axis * count, (axis + 1) * count)
    lifted = product(halfway, high[slots], low[slots], 1)
    out[...] = lifted
    signed = jump[:, slots] * lifted
    lower, upper = signed[:, : count // 2], signed[:, count // 2 :]
    even = place[axis] % 2 == 0
    sends[0][...] = jnp.where(even, upper, lower)
    sends[1][...] = jnp.where(even, lower, upper)


def other_faces_kernel(place, small, half, high, low, out, *sends):
    cases = half.shape[0]
    lift_pair(place, 1, half[...], small[cases + 1 : cases + 2], high, low, out, sends)


def first_kernel(place, small, x0, x1, y0, y1, high, low, ghosts, half, out, *sends):
    value, ghost = small[...], read_faces(place, (x0, x1, y0, y1))
    ghosts[...] = ghost
    cases = half.shape[0]
    resid, weighting, jump = rows_of(value, cases)
    ghost_resid, ghost_weighting, _ = rows_of(ghost, cases)
    field = weighting * resid + (0.5 * jump) * (ghost_weighting * ghost_resid)
    halfway = product(field, high, low, 0)
    half[...] = halfway
    lift_pair(place, 0, halfway, jump, high, low, out, sends)


def early_gram_kernel(small, half, top):
    cases = half.shape[0]
    resid, weighting, _ = rows_of(small[...], cases)
    top[:, :cases] = inner_prod(half[...], half[...])
    top[:, cases:] = inner_prod(weighting * resid, resid)


def gram_kernel(
    place, small, ghosts, half, top, out_x, out_y, x0, x1, y0, y1, high, low, image, ghost_image, second, keep, send, power
):
    cases = half.shape[0]
    _, weighting, jump = rows_of(small[...], cases)
    _, ghost_weighting, ghost_jump = rows_of(ghosts[...], cases)
    out = jnp.concatenate([out_x[...], out_y[...]], axis=1)
    own, ghost = images_of(out, read_faces(place, (x0, x1, y0, y1)), jump, ghost_jump)
    image[...] = own
    ghost_image[...] = ghost
    field = weighting * own + (0.5 * jump) * (ghost_weighting * ghost)
    largest = jnp.max(jnp.max(jnp.abs(field), axis=1, keepdims=True), axis=0, keepdims=True)
    scale = 1.0 / jnp.maximum(largest, 1e-30)
    second_half = product(field * scale, high, low, 0)
    second[:cases] = second_half
    second[cases:] = jnp.broadcast_to(scale, (PAD, field.shape[1]))
    first_half = half[...]
    cross = inner_prod(second_half, jnp.concatenate([first_half, second_half], axis=0))
    split_sums(
        place,
        top[...],
        jnp.concatenate([cross[:, :cases].T, cross[:, cases:]], axis=1),
        jnp.broadcast_to(scale, (PAD, 2 * cases)),
        keep,
        send,
    )
    lane = lax.broadcasted_iota(jnp.int32, (1, 2 * cases), 1)
    scaled = jnp.where(lane < cases, 1.0, 2.0)
    power[...] = jnp.where(place[1] % 2 == 0, jnp.zeros_like(scaled), scaled)


def lift_kernel(place, small, second, high, low, out, *sends):
    cases = out.shape[0]
    jump = small[cases + 1 : cases + 2]
    lifted = product(second[:cases], high, low, 1)
    out[...] = lifted
    write_faces(place, jnp.concatenate([jump * lifted, second[cases:]], axis=0), sends)


def solve_kernel(place, mine, other, steps, inverse):
    cases = steps.shape[0]
    scale = mine[cases : cases + 1, :1]
    top, bottom = join_sums(place, mine, other)
    gram00, gram01, gram11 = top[:cases, :cases], bottom[:cases, :cases], bottom[:cases, cases:]
    first, along, corner, steps0, steps1 = solve_halves(
        gram00, gram01, gram11, top[:cases, cases:], scale * gram00
    )
    inverse[:cases, :cases] = first
    inverse[:cases, cases:] = along
    inverse[cases:, :cases] = corner
    inverse[cases:, cases:] = corner
    steps[...] = jnp.concatenate([steps0, steps1], axis=0).T


def step_kernel(
    place, small, ghosts, mine, steps, image0, ghost_image0, second, out1, x0, x1, y0, y1,
    high, low, state, image1, half, out, *sends
):
    cases = half.shape[0]
    resid, weighting, jump = rows_of(small[...], cases)
    ghost_resid, ghost_weighting, ghost_jump = rows_of(ghosts[...], cases)
    scale = mine[cases : cases + 1, :1]
    received = read_faces(place, (x0, x1, y0, y1))
    own_ratio = scale / second[cases : cases + 1]
    there = received[cases : cases + 1]
    ghost_ratio = jnp.where(there > 0.0, scale / jnp.where(there > 0.0, there, 1.0), 0.0)
    own1, ghost1 = images_of(
        out1[...] * own_ratio, received[:cases] * ghost_ratio, jump, ghost_jump
    )
    image1[...] = own1
    resid = resid - times(steps[...], jnp.concatenate([image0[...], own1], axis=0))
    ghost_resid = ghost_resid - times(
        steps[...], jnp.concatenate([ghost_image0[...], ghost1], axis=0)
    )
    state[...] = resid
    field = weighting * resid + (0.5 * jump) * (ghost_weighting * ghost_resid)
    halfway = product(field, high, low, 0)
    half[...] = halfway
    lift_pair(place, 0, halfway, jump, high, low, out, sends)


def next_early_gram_kernel(small, mine, second, state, half, left, before):
    cases = half.shape[0]
    _, weighting, _ = rows_of(small[...], cases)
    scale = mine[cases : cases + 1, :1]
    before[...] = second[:cases] * (scale / second[cases : cases + 1])
    left[: 2 * cases] = inner_prod(jnp.concatenate([before[...], half[...]], axis=0), half[...])
    left[2 * cases :] = inner_prod(weighting * state[...], state[...])


def next_gram_kernel(
    place, small, ghosts, mine, before, half, left, out_x, out_y, x0, x1, y0, y1, high, low,
    image, next_half, keep, send
):
    cases = half.shape[0]
    _, weighting, jump = rows_of(small[...], cases)
    _, ghost_weighting, ghost_jump = rows_of(ghosts[...], cases)
    scale = mine[cases : cases + 1, :1]
    out = jnp.concatenate([out_x[...], out_y[...]], axis=1)
    own, ghost = images_of(out, read_faces(place, (x0, x1, y0, y1)), jump, ghost_jump)
    image[...] = own
    field = scale * (weighting * own + (0.5 * jump) * (ghost_weighting * ghost))
    halfway = product(field, high, low, 0)
    next_half[...] = halfway
    cross = inner_prod(jnp.concatenate([before[...], half[...], halfway], axis=0), halfway)
    total = jnp.concatenate([left[...], cross], axis=1)
    middle = total.shape[0] // 2
    split_sums(place, total[:middle], total[middle:], None, keep, send)


def next_lift_kernel(place, small, half, high, low, out, *sends):
    cases = out.shape[0]
    lifted = product(half[...], high, low, 1)
    out[...] = lifted
    write_faces(place, small[cases + 1 : cases + 2] * lifted, sends)


def last_solve_kernel(place, first_sums, mine, other, gram_inverse, steps, answer, change):
    cases = steps.shape[0]
    scale = first_sums[cases : cases + 1, :1]
    total = jnp.concatenate(join_sums(place, mine, other), axis=0)
    along = jnp.concatenate(
        [
            jnp.concatenate([jnp.zeros((cases, cases), jnp.float32), total[:cases, :cases]], axis=1),
            total[:cases],
        ],
        axis=0,
    )
    conjugating = times(gram_inverse[...], along)
    taken = times(along.T, conjugating)
    gram00 = total[cases : 2 * cases, :cases]
    _, _, _, next0, next1 = solve_halves(
        gram00 - taken[:cases, :cases],
        total[cases : 2 * cases, cases:] - taken[:cases, cases:],
        total[2 * cases :, cases:] - taken[cases:, cases:],
        total[2 * cases :, :cases],
        scale * gram00,
    )
    next_steps = jnp.concatenate([next0, next1], axis=0)
    old_steps = -times(conjugating, next_steps).T
    next_steps = next_steps.T
    answer[...] = jnp.concatenate([steps[...] + old_steps, next_steps], axis=1)
    change[...] = jnp.concatenate([old_steps, next_steps], axis=1)


def last_kernel(
    place, small, first_sums, answer, change, state, image0, image1, next_image0, out1,
    x0, x1, y0, y1, pick, solution_out, resid_out
):
    cases = image0.shape[0]
    first_resid, weighting, _ = rows_of(small[...], cases)
    scale = first_sums[cases : cases + 1, :1]
    next_image1 = out1[...] + 0.5 * read_faces(place, (x0, x1, y0, y1))
    images = jnp.concatenate(
        [image0[...], image1[...], next_image0[...], next_image1], axis=0
    )
    resid = state[...] - times(change[...], images)
    fields = weighting * jnp.concatenate(
        [first_resid, scale * image0[...], state[...], scale * next_image0[...]], axis=0
    )
    found = times(answer[...], fields)
    both = exact_pick(jnp.concatenate([found, resid], axis=0), pick[...])
    solution_out[...] = both[:cases]
    resid_out[...] = both[cases:]


def call(kernel, name, outs, *operands, scratch=(), mebibytes=8, smem=1, flops=0):
    shapes = [
        jax.ShapeDtypeStruct(one[0], one[1]) if isinstance(one[0], tuple)
        else jax.ShapeDtypeStruct(one, jnp.float32)
        for one in outs
    ]
    touched = sum(one.size * one.dtype.itemsize for one in (*operands, *shapes))
    cost = pl.CostEstimate(flops=flops, bytes_accessed=touched, transcendentals=0)
    return pl.pallas_call(
        kernel,
        out_shape=shapes,
        in_specs=[SMEM] * smem + [VMEM] * (len(operands) - smem),
        out_specs=[VMEM] * len(shapes),
        scratch_shapes=list(scratch),
        compiler_params=pltpu.CompilerParams(vmem_limit_bytes=mebibytes * 2**20),
        cost_estimate=cost if flops else None,
        name=name,
    )(*operands)


def swap_pairs(rows, columns, along, parity):
    pairs = []
    for x in range(rows):
        for y in range(columns):
            index, count = (x, rows) if along == "gx" else (y, columns)
            other = index + 1 if index % 2 == parity else index - 1
            if 0 <= other < count:
                target = (other, y) if along == "gx" else (x, other)
            else:
                target = (x, y ^ 1) if along == "gx" else (x ^ 1, y)
                if not (target[0] < rows and target[1] < columns):
                    target = (x, y)
            pairs.append((x * columns + y, target[0] * columns + target[1]))
    return pairs


def swap_faces(sends, axes=("gx", "gy")):
    rows, columns = lax.axis_size("gx"), lax.axis_size("gy")
    order = [(along, parity) for along in axes for parity in (0, 1)]
    return [
        lax.ppermute(send, ("gx", "gy"), swap_pairs(rows, columns, along, parity))
        for send, (along, parity) in zip(sends, order)
    ]


def stage_masks(axis, first):
    count = lax.axis_size(axis)
    stages = []
    step = first
    while step < count:
        last = step * 2 >= count
        stages.append((axis, (step,) if last else (step, 2 * step, 3 * step)))
        step *= 4
    return stages


def from_mask(value, axis, mask):
    count = lax.axis_size(axis)
    return lax.ppermute(value, axis, [(source, source ^ mask) for source in range(count)])


def sum_over_devices(keep, send, add, work, inputs):
    value = add([keep, from_mask(send, "gy", 1)])
    stages = stage_masks("gy", 2) + stage_masks("gx", 1)
    done, sends, received = (), (), []
    for index, (axis, masks) in enumerate(stages):
        value, inputs, sends = lax.optimization_barrier((value, inputs, sends))
        parts = [value] + [from_mask(value, axis, mask) for mask in masks]
        if index == 0:
            done, sends = work(*inputs)
        if index == len(stages) - 1:
            received = swap_faces(sends)
        value = add(parts)
        value, done, sends = lax.optimization_barrier((value, done, sends))
    return value, from_mask(value, "gy", 1), received, done


def plain(parts):
    value = parts[0] + parts[1]
    return value + (parts[2] + parts[3]) if len(parts) == 4 else value


def rescaled(power, parts):
    cases = parts[0].shape[0] - PAD
    scales = [part[cases:] for part in parts]
    scale = functools.reduce(jnp.minimum, scales)
    ready = []
    for part, own in zip(parts, scales):
        ratio = (scale / own)[:1]
        factor = jnp.where(power == 0.0, 1.0, jnp.where(power == 1.0, ratio, ratio * ratio))
        ready.append(part[:cases] * factor)
    return jnp.concatenate([plain(ready), scale], axis=0)


def local(right_side, weights, signs, face_map, pattern, factor):
    cases, size = right_side.shape[1:]
    blocks = pattern.shape[1]
    place = jnp.stack(
        [
            lax.axis_index("gx"),
            lax.axis_index("gy"),
            jnp.int32(lax.axis_size("gx")),
            jnp.int32(lax.axis_size("gy")),
        ]
    )
    field, padded = (cases, size), (cases + PAD, size)
    face, padded_face = (cases, size // 4), (cases + PAD, size // 4)
    half_type = ((size, size), jnp.bfloat16)
    part = (cases, size // 2)

    work = 6 * cases * size * size
    (pick,) = call(pick_kernel, "pick", [half_type], face_map, smem=0, flops=20 * work)
    small, *sends = call(
        start_kernel, "start_fields", [padded] + [padded_face] * 4,
        place, right_side[0], weights, signs, face_map, pick,
    )
    received = swap_faces(sends)
    high, low = call(
        functools.partial(factor_kernel, blocks), "masked_factor", [half_type] * 2,
        pattern[0], factor[0], face_map,
        scratch=[pltpu.VMEM((size, size), jnp.bfloat16)] * 2,
        smem=0,
    )
    ghosts, half0, out0, *sends = call(
        first_kernel, "first_operator", [padded, field, part] + [face] * 2,
        place, small, *received, high, low,
    )
    out0_y, *more = call(
        other_faces_kernel, "first_other_faces", [part] + [face] * 2,
        place, small, half0, high, low,
    )
    received = swap_faces(sends + more)
    (top,) = call(
        early_gram_kernel, "early_gram", [(cases, 2 * cases)], small, half0, smem=0
    )
    received, top = lax.optimization_barrier((received, top))
    image0, ghost_image0, second, keep, send, power = call(
        gram_kernel, "first_gram",
        [field, field, padded] + [(cases + PAD, 2 * cases)] * 2 + [(1, 2 * cases)],
        place, small, ghosts, half0, top, out0, out0_y, *received, high, low,
    )

    def lift(second):
        out, *sends = call(
            lift_kernel, "second_operator", [field] + [padded_face] * 4,
            place, small, second, high, low,
        )
        return out, sends

    mine, other, faces, out1 = sum_over_devices(
        keep, send, functools.partial(rescaled, power), lift, (second,)
    )
    steps, inverse = call(
        solve_kernel, "first_solve", [(cases, 2 * cases), (2 * cases, 2 * cases)],
        place, mine, other,
    )
    state, image1, next_half0, next_out0, *next_sends = call(
        step_kernel, "first_step", [field] * 3 + [part] + [face] * 2,
        place, small, ghosts, mine, steps, image0, ghost_image0, second, out1,
        *faces, high, low,
    )
    next_out0_y, *more = call(
        other_faces_kernel, "step_other_faces", [part] + [face] * 2,
        place, small, next_half0, high, low,
    )
    inverse, more = lax.optimization_barrier((inverse, more))
    faces = swap_faces(next_sends + more)
    pick, gram_inverse = call(
        functools.partial(prepare_kernel, cases), "prepare_last",
        [half_type, (2 * cases, 2 * cases)], small, inverse, smem=0,
    )
    left, before = call(
        next_early_gram_kernel, "next_early_gram", [(3 * cases, cases), field],
        small, mine, second, state, next_half0, smem=0,
    )
    faces, pick, gram_inverse, left, before = lax.optimization_barrier(
        (faces, pick, gram_inverse, left, before)
    )
    next_image0, next_half1, keep, send = call(
        next_gram_kernel, "second_gram", [field, field] + [(3 * cases // 2, 2 * cases)] * 2,
        place, small, ghosts, mine, before, next_half0, left, next_out0, next_out0_y, *faces, high, low,
    )

    def last_lift(half):
        out, *sends = call(
            next_lift_kernel, "last_operator", [field] + [face] * 4,
            place, small, half, high, low,
        )
        return out, sends

    next_mine, next_other, faces, next_out1 = sum_over_devices(
        keep, send, plain, last_lift, (next_half1,)
    )
    wide = (cases, 4 * cases)
    found, change = call(
        last_solve_kernel, "last_solve", [wide, wide],
        place, mine, next_mine, next_other, gram_inverse, steps,
    )
    answer, resid = call(
        last_kernel, "last_step", [field, field],
        place, small, mine, found, change, state, image0, image1, next_image0, next_out1,
        *faces, pick,
    )
    return (answer[None], resid[None])


def solution(mesh):
    return jax.shard_map(
        local,
        mesh=mesh,
        in_specs=(
            P("gx", None, "gy"),
            P("gx", "gy"),
            P("gx", "gy"),
            P("gx", "gy"),
            P("gx", None, "gy"),
            P("gx", None, "gy"),
        ),
        out_specs=(P("gx", None, "gy"), P("gx", None, "gy")),
        check_vma=False,
    )
```
